32 devices in a mesh: gx: 2 (over x), gy: 4 (over y, core), gz: 4 (over z).
Axes of the slice: x: 2, y: 2, z: 4, core: 2. Of those that a mesh axis runs over, the one named last changes fastest.
Arguments:
- start_block: float32 [16, 8, 64, 512], P(None, 'gx', 'gy', 'gz')
- basis: bfloat16 [256, 8, 64, 512], P(None, 'gx', 'gy', 'gz')
- trans_x: float32 [8, 64, 512], P('gx', 'gy', 'gz'), may hold values from 0.05 to 1
- trans_y: float32 [8, 64, 512], P('gx', 'gy', 'gz'), may hold values from 0.05 to 1
- trans_z: float32 [8, 64, 512], P('gx', 'gy', 'gz'), may hold values from 0.05 to 1
- pore_volume: float32 [8, 64, 512], P('gx', 'gy', 'gz'), may hold values from 0.5 to 2
- shift_table: float32 [16], replicated, may hold values from 0.5 to 4
- shift_index: int32 [1], replicated, may hold values from 0 to 15
- fault_send: int32 [32, 32, 32], P(('gx', 'gy', 'gz')), may hold values from 0 to 8191
- fault_recv: int32 [32, 32, 32], P(('gx', 'gy', 'gz')), may hold values from 0 to 8191
- fault_trans: float32 [32, 32, 32], P(('gx', 'gy', 'gz')), may hold values from 0.05 to 0.5
- well_cells: int32 [64], replicated, may hold values from 0 to 262143
Outputs:
- new_block: float32 [16, 8, 64, 512], P(None, 'gx', 'gy', 'gz')
- first_coeffs: float32 [256, 16], replicated
- coeffs: float32 [256, 16], replicated
- well_resp: float32 [64, 16], replicated
The draws below stay inside these ranges and needn't reach their ends.
Inputs may be any that keep to these rules, and one draw needn't show every extreme that they name: fault_send[d, p, s] is a local cell number on device d; the value of that cell feeds a connection into device p. fault_recv[d, p, s] is a local cell number on device d. `well_cells`: flat cell index, last dimension fastest.
All inputs are finite; a program needn't handle non-finite values.
Results may differ from the reference program's by a relative error of at most 0.0065.
Values sent between devices are 32-bit elements; how exact they have to be, the bound alone decides.
No kernel may reach another device: no remote copies, remote signals or barrier semaphores. Data moves between devices by JAX's collectives and lax.ppermute only.
A program may use at most 128 MiB of HBM per device.

```python
import math
import jax
import jax.numpy as jnp
from jax import lax

CX = 4
CY = 16
CZ = 128
SLOTS = 32
COLS = 16
BASIS = 256
WELLS = 64
TERMS = 8
SHIFTS = 16
NX = 8
NY = 64
NZ = 512
N_GX = 2
N_GY = 4
N_GZ = 4
DEVICES = 32


def mode_field(index):
    freq_x = (index % 4).astype(jnp.float32)
    freq_y = (index // 4 % 4).astype(jnp.float32)
    freq_z = (index // 16).astype(jnp.float32)
    pos_x = lax.broadcasted_iota(jnp.int32, (1, NX, 1, 1), 1).astype(jnp.float32)
    pos_y = lax.broadcasted_iota(jnp.int32, (1, 1, NY, 1), 2).astype(jnp.float32)
    pos_z = lax.broadcasted_iota(jnp.int32, (1, 1, 1, NZ), 3).astype(jnp.float32)
    root_two = math.sqrt(2.0)
    along_x = jnp.cos(math.pi * (pos_x + 0.5) * freq_x / NX) * jnp.where(freq_x > 0.0, root_two, 1.0)
    along_y = jnp.cos(math.pi * (pos_y + 0.5) * freq_y / NY) * jnp.where(freq_y > 0.0, root_two, 1.0)
    along_z = jnp.cos(math.pi * (pos_z + 0.5) * freq_z / NZ) * jnp.where(freq_z > 0.0, root_two, 1.0)
    return along_x * along_y * along_z


def draw_basis(key, part):
    column_index = lax.broadcasted_iota(jnp.int32, (BASIS, 1, 1, 1), 0)
    values = jax.random.normal(key, (BASIS, NX, NY, NZ), jnp.float32)
    gains = jax.random.uniform(jax.random.fold_in(key, 11), (BASIS, 1, 1, 1), jnp.float32, 0.8, 1.2)
    mixed = 0.6 * values + 0.8 * mode_field(column_index)
    return (mixed * gains * (1.0 / math.sqrt(NX * NY * NZ))).astype(jnp.bfloat16)


def draw_start_block(key, part):
    column_scale = jnp.exp(jax.random.uniform(jax.random.fold_in(key, 21), (COLS, 1, 1, 1), jnp.float32, 0.0, math.log(10.0)))
    pos_x = lax.broadcasted_iota(jnp.int32, (1, NX, 1, 1), 1).astype(jnp.float32)
    ramp = 1.0 + 2.0 * pos_x / max(NX - 1, 1)
    values = jax.random.normal(key, (COLS, NX, NY, NZ), jnp.float32)
    lead_index = lax.broadcasted_iota(jnp.int32, (COLS, 1, 1, 1), 0)
    repeats = BASIS // COLS
    smooth = jnp.zeros((COLS, NX, NY, NZ), jnp.float32)
    for turn in range(repeats):
        weights = jax.random.normal(jax.random.fold_in(key, 41 + turn), (COLS, 1, 1, 1), jnp.float32)
        smooth = smooth + weights * mode_field(lead_index + COLS * turn)
    smooth = smooth * (1.0 / math.sqrt(repeats))
    return column_scale * (values * ramp + smooth)


def plant(drawn, own_key, least, largest):
    shape = drawn.shape
    spot = [jax.random.randint(jax.random.fold_in(own_key, axis), (), 0, shape[axis]) for axis in range(len(shape))]
    drawn = drawn.at[tuple(spot)].set(least)
    longest = shape.index(max(shape))
    spot[longest] = (spot[longest] + 1) % shape[longest]
    return drawn.at[tuple(spot)].set(largest)


def steps_of(rng, extent, pieces, low, largest):
    def one(position, blocks):
        draws = jax.random.uniform(jax.random.fold_in(jax.random.fold_in(rng, 6), position), (blocks,), jnp.float32, low / len(pieces), largest / len(pieces))
        return jnp.repeat(jnp.exp(draws), extent[position] // blocks).reshape((-1,) + (1,) * (len(extent) - position - 1))

    loudness = one(*pieces[0])
    for cut in pieces[1:]:
        loudness = loudness * one(*cut)
    return loudness


def setup_inputs(seed: int = 0) -> dict:
    arg_keys = jax.random.split(jax.random.key(seed), 13)
    return {
        "start_block": draw_start_block(jax.random.fold_in(arg_keys[12], 71), 0),
        "basis": draw_basis(jax.random.fold_in(arg_keys[12], 71), 0),
        "trans_x": jnp.clip(jnp.exp(math.log(1.0) - 2.9957323 * jax.random.uniform(arg_keys[2], (NX, NY, NZ), jnp.float32) ** steps_of(arg_keys[2], (NX, NY, NZ), ((0, 2), (1, 4), (2, 4)), -0.2, 0.2)), 0.05, 1.0),
        "trans_y": jnp.clip(jnp.exp(math.log(1.0) - 2.9957323 * jax.random.uniform(arg_keys[3], (NX, NY, NZ), jnp.float32) ** steps_of(arg_keys[3], (NX, NY, NZ), ((0, 2), (1, 4), (2, 4)), -0.2, 0.2)), 0.05, 1.0),
        "trans_z": jnp.clip(jnp.exp(math.log(1.0) - 2.9957323 * jax.random.uniform(arg_keys[4], (NX, NY, NZ), jnp.float32) ** steps_of(arg_keys[4], (NX, NY, NZ), ((0, 2), (1, 4), (2, 4)), -0.2, 0.2)), 0.05, 1.0),
        "pore_volume": jnp.clip(jnp.exp(math.log(2.0) - 1.3862944 * jax.random.uniform(arg_keys[5], (NX, NY, NZ), jnp.float32) ** steps_of(arg_keys[5], (NX, NY, NZ), ((0, 2), (1, 4), (2, 4)), -0.2, 0.2)), 0.5, 2.0),
        "shift_table": jnp.clip(jnp.exp(jax.random.uniform(arg_keys[6], (SHIFTS,), jnp.float32, math.log(0.5), math.log(4.0))), 0.5, 4.0),
        "shift_index": jax.random.randint(arg_keys[7], (1,), 0, SHIFTS).astype(jnp.int32),
        "fault_send": plant(jax.random.randint(arg_keys[8], (DEVICES, DEVICES, SLOTS), 0, CX * CY * CZ), jax.random.fold_in(arg_keys[8], 1), 0, (CX * CY * CZ) - 1).astype(jnp.int32),
        "fault_recv": plant(jax.random.randint(arg_keys[9], (DEVICES, DEVICES, SLOTS), 0, CX * CY * CZ), jax.random.fold_in(arg_keys[9], 1), 0, (CX * CY * CZ) - 1).astype(jnp.int32),
        "fault_trans": jnp.clip(jnp.exp(math.log(0.5) - 2.3025851 * jax.random.uniform(arg_keys[10], (DEVICES, DEVICES, SLOTS), jnp.float32) ** steps_of(arg_keys[10], (DEVICES, DEVICES, SLOTS), ((0, 32),), -0.2, 0.2)), 0.05, 0.5),
        "well_cells": plant(jax.random.randint(arg_keys[11], (WELLS,), 0, NX * NY * NZ), jax.random.fold_in(arg_keys[11], 1), 0, (NX * NY * NZ) - 1).astype(jnp.int32),
    }


def to_blocks(field, lead):
    shaped = field.reshape(lead, N_GX, CX, N_GY, CY, N_GZ, CZ)
    shaped = shaped.transpose(1, 3, 5, 0, 2, 4, 6)
    return shaped.reshape(N_GX * N_GY * N_GZ, lead, CX * CY * CZ)

def from_blocks(blocked, lead):
    shaped = blocked.reshape(N_GX, N_GY, N_GZ, lead, CX, CY, CZ)
    shaped = shaped.transpose(3, 0, 4, 1, 5, 2, 6)
    return shaped.reshape(lead, NX, NY, NZ)

def land_values(weights, targets, values):
    total = jnp.zeros((COLS, CX * CY * CZ), jnp.float32)
    return total.at[:, targets.reshape(-1)].add((weights[None] * values).reshape(COLS, -1))

def land_weights(weights, targets):
    total = jnp.zeros((1, CX * CY * CZ), jnp.float32)
    return total.at[0, targets.reshape(-1)].add(weights.reshape(-1))

def pick_cells(block_values, sources):
    return block_values[:, sources]

def reference(start_block, basis, trans_x, trans_y, trans_z, pore_volume, shift_table, shift_index, fault_send, fault_recv, fault_trans, well_cells):
    pos_x = lax.broadcasted_iota(jnp.int32, (NX, NY, NZ), 0)
    pos_y = lax.broadcasted_iota(jnp.int32, (NX, NY, NZ), 1)
    pos_z = lax.broadcasted_iota(jnp.int32, (NX, NY, NZ), 2)
    upper_x = jnp.where(pos_x < NX - 1, trans_x, 0.0)
    upper_y = jnp.where(pos_y < NY - 1, trans_y, 0.0)
    upper_z = jnp.where(pos_z < NZ - 1, trans_z, 0.0)
    lower_x = jnp.pad(upper_x, ((1, 0), (0, 0), (0, 0)))[:-1]
    lower_y = jnp.pad(upper_y, ((0, 0), (1, 0), (0, 0)))[:, :-1]
    lower_z = jnp.pad(upper_z, ((0, 0), (0, 0), (1, 0)))[:, :, :-1]
    shift = jnp.sum(jnp.where(jnp.arange(SHIFTS, dtype=jnp.int32) == shift_index[0], shift_table, 0.0))
    fault_diag = from_blocks(jax.vmap(land_weights)(fault_trans, fault_recv), 1)[0]
    diagonal = upper_x + lower_x + upper_y + lower_y + upper_z + lower_z + shift * pore_volume + fault_diag

    def operate(field):
        padded = jnp.pad(field, ((0, 0), (1, 1), (1, 1), (1, 1)))
        beside = upper_x * padded[:, 2:, 1:-1, 1:-1] + lower_x * padded[:, :-2, 1:-1, 1:-1]
        beside = beside + upper_y * padded[:, 1:-1, 2:, 1:-1] + lower_y * padded[:, 1:-1, :-2, 1:-1]
        beside = beside + upper_z * padded[:, 1:-1, 1:-1, 2:] + lower_z * padded[:, 1:-1, 1:-1, :-2]
        blocked = to_blocks(field, COLS)
        sent = jax.vmap(pick_cells)(blocked, fault_send)
        arrived = jnp.transpose(sent, (2, 1, 0, 3))
        remote = from_blocks(jax.vmap(land_values)(fault_trans, fault_recv, arrived), COLS)
        return diagonal * field - beside - remote
    sigma = 1.0 / 0.9
    weight_now = 1.0 / sigma
    solution = jnp.zeros_like(start_block)
    residual = start_block
    direction = residual / diagonal
    for number in range(TERMS):
        solution = solution + direction
        if number < TERMS - 1:
            residual = residual - operate(direction)
            weight_new = 1.0 / (2.0 * sigma - weight_now)
            direction = weight_new * weight_now * direction + 2.0 * weight_new / 0.9 * (residual / diagonal)
            weight_now = weight_new
    cells = NX * NY * NZ
    flat_basis = basis.reshape(BASIS, cells)
    flat_x = solution.reshape(COLS, cells)
    first_coeffs = jnp.dot(flat_basis.astype(jnp.float32), flat_x.astype(jnp.bfloat16).T.astype(jnp.float32), preferred_element_type=jnp.float32)
    first_rest = flat_x - jnp.dot(first_coeffs.astype(jnp.bfloat16).T.astype(jnp.float32), flat_basis.astype(jnp.float32), preferred_element_type=jnp.float32)
    second_coeffs = jnp.dot(flat_basis.astype(jnp.float32), first_rest.astype(jnp.bfloat16).T.astype(jnp.float32), preferred_element_type=jnp.float32)
    rest = first_rest - jnp.dot(second_coeffs.astype(jnp.bfloat16).T.astype(jnp.float32), flat_basis.astype(jnp.float32), preferred_element_type=jnp.float32)
    gram = jnp.dot(rest, rest.T, precision=lax.Precision.HIGHEST)
    lower = jnp.linalg.cholesky(gram)
    scale = math.sqrt(cells)
    new_flat = lax.linalg.triangular_solve(lower, rest, left_side=True, lower=True) * scale
    well_resp = new_flat[:, well_cells].T
    return (new_flat.reshape(COLS, NX, NY, NZ), first_coeffs, first_coeffs + second_coeffs, well_resp)
```

```python
import functools
import math

import jax
import jax.numpy as jnp
from jax import lax
from jax.experimental import pallas as pl
from jax.experimental.pallas import tpu as pltpu
from jax.sharding import PartitionSpec as P

TERMS = 8
AXES = ("gx", "gy", "gz")
LANES = 128
VMEM_LIMIT = 48 * 1024 * 1024
BF16 = jnp.bfloat16
F32 = jnp.float32


def swap_pairs(size, odd):
    pairs = []
    for low in range(1 if odd else 0, size - 1, 2):
        pairs += [(low, low + 1), (low + 1, low)]
    return pairs


def swap(value, axis, odd):
    pairs = swap_pairs(lax.axis_size(axis), odd)
    return lax.ppermute(value, axis, pairs) if pairs else value


def from_behind(value, axis):
    size = lax.axis_size(axis)
    return lax.ppermute(value, axis, [(i, i + 1) for i in range(size - 1)])


def exchange(value):
    return lax.all_to_all(value, AXES, split_axis=0, concat_axis=0, tiled=True)


def regroup(tile, rows, slots):
    groups = LANES // slots
    columns = tile.shape[0]
    row_group = lax.broadcasted_iota(jnp.int32, tile.shape, 0) // rows
    lane_group = lax.broadcasted_iota(jnp.int32, tile.shape, 1) // slots
    ahead = lax.rem(lane_group - row_group + groups, groups)
    result = tile
    for k in range(1, groups):
        moved = pltpu.roll(tile, k * slots, 1)
        moved = pltpu.roll(moved, columns - k * rows, 0)
        result = jnp.where(ahead == k, moved, result)
    return result


def split_two(value):
    high = value.astype(BF16)
    low = (value - high.astype(F32)).astype(BF16)
    return high, low


def nt_dot(left, right):
    return lax.dot_general(left, right, (((1,), (1,)), ((), ())), preferred_element_type=F32)


def emit(direction_ref, par_ref, send_ref, faults_out, faces_out, dims):
    columns, size_x, size_y, size_z, slots = dims
    lines = size_x * size_y
    rows = columns * slots // LANES
    x_a, x_b, y_a, y_b, z_ab = faces_out
    even = [par_ref[i] == 0 for i in range(3)]
    field = direction_ref[...]
    first_x, last_x = field[:, :size_y, :], field[:, lines - size_y :, :]
    x_a[...] = jnp.where(even[0], last_x, first_x)
    if x_b is not None:
        x_b[...] = jnp.where(even[0], first_x, last_x)
    for i in range(size_x):
        first_y = direction_ref[:, i * size_y, :]
        last_y = direction_ref[:, (i + 1) * size_y - 1, :]
        y_a[i] = jnp.where(even[1], last_y, first_y)
        if y_b is not None:
            y_b[i] = jnp.where(even[1], first_y, last_y)
    both = jnp.concatenate(split_two(field.reshape(columns * lines, size_z)), axis=1)
    row = lax.broadcasted_iota(jnp.int32, (8, size_z), 0)
    lane = lax.broadcasted_iota(jnp.int32, (8, size_z), 1)
    pick = ((row == 0) & (lane == size_z - 1)) | ((row == 1) & (lane == 0))
    pick = jnp.where(pick, 1.0, 0.0).astype(BF16)
    ends = nt_dot(jnp.concatenate([pick, pick], axis=1), both)
    last_z, first_z = ends[0:1, :], ends[1:2, :]
    z_ab[0:1, :] = jnp.where(even[2], last_z, first_z)
    z_ab[1:2, :] = jnp.where(even[2], first_z, last_z)
    total = send_ref.shape[1]
    width = min(256, total)
    for start in range(0, total, width):
        cell = send_ref[:, start : start + width]
        lane_of = jnp.broadcast_to(cell % size_z, (size_z, width))
        hot = lane_of == lax.broadcasted_iota(jnp.int32, (size_z, width), 0)
        hot = jnp.where(hot, 1.0, 0.0).astype(BF16)
        found = jnp.dot(both, jnp.concatenate([hot, hot], axis=0), preferred_element_type=F32)
        line_of = jnp.broadcast_to(cell // size_z, (lines, width))
        mask = line_of == lax.broadcasted_iota(jnp.int32, (lines, width), 0)
        found = jnp.where(mask[None], found.reshape(columns, lines, width), 0.0)
        values = jnp.sum(found, axis=1)
        for j in range(0, width, LANES):
            at = (start + j) // LANES * columns
            faults_out[at : at + columns, :] = regroup(values[:, j : j + LANES], rows, slots)


def setup_kernel(dims, has_b, *refs):
    (par_ref, table_ref, which_ref, start_ref, tx_ref, ty_ref, tz_ref, pore_ref, ex_ref, ey_ref, ez_ref) = refs[:11]
    send_ref, recv_ref, weight_ref = refs[11:14]
    ops_ref, direction_ref, faults_out = refs[14:17]
    faces_out = unpack_faces(refs[17:], has_b)
    columns, size_x, size_y, size_z, slots = dims
    lines = size_x * size_y
    line = lax.broadcasted_iota(jnp.int32, (lines, size_z), 0)
    lane = lax.broadcasted_iota(jnp.int32, (lines, size_z), 1)
    last = [par_ref[3 + i] == 1 for i in range(3)]
    in_y = line % size_y
    upper_x = jnp.where((line >= lines - size_y) & last[0], 0.0, tx_ref[...])
    upper_y = jnp.where((in_y == size_y - 1) & last[1], 0.0, ty_ref[...])
    upper_z = jnp.where((lane == size_z - 1) & last[2], 0.0, tz_ref[...])
    lower_x = jnp.concatenate([ex_ref[...], upper_x[: lines - size_y]], axis=0)
    edge_y = jnp.concatenate(
        [jnp.broadcast_to(ey_ref[i : i + 1, :], (size_y, size_z)) for i in range(size_x)], axis=0
    )
    lower_y = jnp.where(in_y == 0, edge_y, pltpu.roll(upper_y, 1, 0))
    lower_z = jnp.where(lane == 0, ez_ref[...], pltpu.roll(upper_z, 1, 1))
    total = recv_ref.shape[1]
    cell = recv_ref[...]
    hot_line = jnp.broadcast_to(cell // size_z, (lines, total)) == lax.broadcasted_iota(
        jnp.int32, (lines, total), 0
    )
    hot_lane = jnp.broadcast_to(cell % size_z, (size_z, total)) == lax.broadcasted_iota(
        jnp.int32, (size_z, total), 0
    )
    weight = weight_ref[...]
    high = weight.astype(BF16).astype(F32)
    middle = (weight - high).astype(BF16).astype(F32)
    low = weight - high - middle
    parts = [jnp.where(hot_line, part, 0.0).astype(BF16) for part in (high, middle, low)]
    summed = nt_dot(jnp.concatenate(parts, axis=0), jnp.where(hot_lane, 1.0, 0.0).astype(BF16))
    fault_diag = summed[:lines] + summed[lines : 2 * lines] + summed[2 * lines :]
    shift = table_ref[which_ref[0]]
    diagonal = (
        upper_x + lower_x + upper_y + lower_y + upper_z + lower_z + shift * pore_ref[...] + fault_diag
    )
    inverse = 1.0 / diagonal
    for i, value in enumerate((upper_x, lower_x, upper_y, lower_y, upper_z, lower_z, diagonal, inverse)):
        ops_ref[i] = value
    for c in range(columns):
        direction_ref[c] = start_ref[c] * inverse
    emit(direction_ref, par_ref, send_ref, faults_out, faces_out, dims)


def unpack_faces(refs, has_b):
    refs = list(refs)
    x_a = refs.pop(0)
    x_b = refs.pop(0) if has_b[0] else None
    y_a = refs.pop(0)
    y_b = refs.pop(0) if has_b[1] else None
    return x_a, x_b, y_a, y_b, refs.pop(0)


def round_kernel(dims, has_b, keep, gain, last_round, *refs):
    refs = list(refs)
    par_ref, ops_ref, solution_ref, residual_ref, direction_ref = refs[:5]
    recv_ref, weight_ref, arrived_ref = refs[5:8]
    refs = refs[8:]
    xa_ref = refs.pop(0)
    xb_ref = refs.pop(0) if has_b[0] else xa_ref
    ya_ref = refs.pop(0)
    yb_ref = refs.pop(0) if has_b[1] else ya_ref
    za_ref = refs.pop(0)
    zb_ref = refs.pop(0) if has_b[2] else za_ref
    send_ref = None if last_round else refs.pop(0)
    solution_out = refs.pop(0)
    if not last_round:
        residual_out, direction_out, faults_out = refs[:3]
        refs = refs[3:]
        faces_out = unpack_faces(refs[: 3 + has_b[0] + has_b[1]], has_b)
        refs = refs[3 + has_b[0] + has_b[1] :]
    landed_ref = refs.pop(0)
    columns, size_x, size_y, size_z, slots = dims
    lines = size_x * size_y
    rows = columns * slots // LANES
    total = recv_ref.shape[1]
    cell = recv_ref[...]
    hot_line = jnp.broadcast_to(cell // size_z, (lines, total)) == lax.broadcasted_iota(
        jnp.int32, (lines, total), 0
    )
    hot_lane = jnp.broadcast_to(cell % size_z, (size_z, total)) == lax.broadcasted_iota(
        jnp.int32, (size_z, total), 0
    )
    hot_line = jnp.where(hot_line, 1.0, 0.0).astype(BF16)
    hot_lane = jnp.where(hot_lane, 1.0, 0.0).astype(BF16)
    tiles = [
        regroup(arrived_ref[j * columns : (j + 1) * columns, :], rows, slots)
        for j in range(total // LANES)
    ]
    weighted = (jnp.concatenate(tiles, axis=1) * weight_ref[...]).astype(BF16)
    spread = weighted[:, None, :] * hot_line[None, :, :]
    landed_ref[...] = nt_dot(spread.reshape(columns * lines, total), hot_lane)

    even = [par_ref[i] == 0 for i in range(3)]
    z_rows = jnp.concatenate(
        [
            jnp.where(even[2], zb_ref[...], za_ref[...]),
            jnp.where(even[2], za_ref[...], zb_ref[...]),
            jnp.zeros((6, columns * lines), F32),
        ],
        axis=0,
    )
    z_cols = z_rows.T
    in_y = lax.broadcasted_iota(jnp.int32, (lines, size_z), 0) % size_y
    lane = lax.broadcasted_iota(jnp.int32, (lines, size_z), 1)

    def rows_of(ref, c):
        return jnp.concatenate(
            [jnp.broadcast_to(ref[i, c : c + 1, :], (size_y, size_z)) for i in range(size_x)], axis=0
        )

    for c in range(columns):
        value = direction_ref[c]
        x_low = jnp.where(even[0], xb_ref[c], xa_ref[c])
        x_high = jnp.where(even[0], xa_ref[c], xb_ref[c])
        y_a, y_b = rows_of(ya_ref, c), rows_of(yb_ref, c)
        y_low = jnp.where(even[1], y_b, y_a)
        y_high = jnp.where(even[1], y_a, y_b)
        z_low = z_cols[c * lines : (c + 1) * lines, 0:1]
        z_high = z_cols[c * lines : (c + 1) * lines, 1:2]
        beside = ops_ref[0] * jnp.concatenate([value[size_y:], x_high], axis=0)
        beside += ops_ref[1] * jnp.concatenate([x_low, value[: lines - size_y]], axis=0)
        beside += ops_ref[2] * jnp.where(in_y == size_y - 1, y_high, pltpu.roll(value, lines - 1, 0))
        beside += ops_ref[3] * jnp.where(in_y == 0, y_low, pltpu.roll(value, 1, 0))
        beside += ops_ref[4] * jnp.where(lane == size_z - 1, z_high, pltpu.roll(value, size_z - 1, 1))
        beside += ops_ref[5] * jnp.where(lane == 0, z_low, pltpu.roll(value, 1, 1))
        landed = landed_ref[c * lines : (c + 1) * lines, :]
        left = residual_ref[c] - (ops_ref[6] * value - beside - landed)
        after = keep * value + gain * (left * ops_ref[7])
        solution_out[c] = solution_ref[c] + after
        if not last_round:
            residual_out[c] = left
            direction_out[c] = after
    if not last_round:
        emit(direction_out, par_ref, send_ref, faults_out, faces_out, dims)


def local(
    start_block,
    basis,
    trans_x,
    trans_y,
    trans_z,
    pore_volume,
    shift_table,
    shift_index,
    fault_send,
    fault_recv,
    fault_trans,
    well_cells,
):
    columns, size_x, size_y, size_z = start_block.shape
    devices, slots = fault_send.shape[1:]
    lines = size_x * size_y
    cells = lines * size_z
    total = devices * slots
    sizes = [lax.axis_size(axis) for axis in AXES]
    index_x, index_y, index_z = (lax.axis_index(axis) for axis in AXES)
    full_x, full_y, full_z = size_x * sizes[0], size_y * sizes[1], size_z * sizes[2]
    has_b = tuple(size > 2 for size in sizes)
    dims = (columns, size_x, size_y, size_z, slots)
    rows = columns * slots // LANES
    index = [index_x, index_y, index_z]
    par = jnp.stack(
        [i % 2 for i in index] + [(i == n - 1).astype(jnp.int32) for i, n in zip(index, sizes)]
    )

    vmem = pl.BlockSpec(memory_space=pltpu.VMEM)
    smem = pl.BlockSpec(memory_space=pltpu.SMEM)
    params = pltpu.CompilerParams(vmem_limit_bytes=VMEM_LIMIT)
    field_type = jax.ShapeDtypeStruct((columns, lines, size_z), F32)
    x_type = jax.ShapeDtypeStruct((columns, size_y, size_z), F32)
    y_type = jax.ShapeDtypeStruct((size_x, columns, size_z), F32)
    face_types = (
        [x_type] * (1 + has_b[0])
        + [y_type] * (1 + has_b[1])
        + [jax.ShapeDtypeStruct((2, columns * lines), F32)]
    )
    faults_type = jax.ShapeDtypeStruct((devices * rows, LANES), F32)

    shape2 = (lines, size_z)
    start = start_block.reshape(columns, lines, size_z)
    edge_x = from_behind(trans_x[-1], "gx")
    edge_y = from_behind(trans_y[:, -1], "gy")
    edge_z = from_behind(trans_z[:, :, -1].reshape(1, lines), "gz").reshape(lines, 1)
    send = fault_send[0].reshape(1, total)
    recv = fault_recv[0].reshape(1, total)
    weight = fault_trans[0].reshape(1, total)

    def transfers(faults, faces):
        faces = list(faces)
        out = [exchange(faults)]
        out.append(swap(faces.pop(0), "gx", False))
        if has_b[0]:
            out.append(swap(faces.pop(0), "gx", True))
        out.append(swap(faces.pop(0), "gy", False))
        if has_b[1]:
            out.append(swap(faces.pop(0), "gy", True))
        z_ab = faces.pop(0)
        out.append(swap(z_ab[0:1], "gz", False))
        if has_b[2]:
            out.append(swap(z_ab[1:2], "gz", True))
        return out

    ops, direction, faults, *faces = pl.pallas_call(
        functools.partial(setup_kernel, dims, has_b),
        out_shape=[jax.ShapeDtypeStruct((8, lines, size_z), F32), field_type, faults_type] + face_types,
        in_specs=[smem] * 3 + [vmem] * 11,
        out_specs=[vmem] * (3 + len(face_types)),
        compiler_params=params,
        name="setup",
    )(
        par, shift_table, shift_index, start, trans_x.reshape(shape2), trans_y.reshape(shape2),
        trans_z.reshape(shape2), pore_volume.reshape(shape2), edge_x, edge_y, edge_z, send, recv, weight,
    )
    sigma = 1.0 / 0.9
    weight_now = 1.0 / sigma
    solution, residual = direction, start
    for number in range(TERMS - 1):
        arrived = transfers(faults, faces)
        weight_new = 1.0 / (2.0 * sigma - weight_now)
        last_round = number == TERMS - 2
        body = functools.partial(
            round_kernel, dims, has_b, weight_new * weight_now, 2.0 * weight_new / 0.9, last_round
        )
        weight_now = weight_new
        out_types = [field_type]
        if not last_round:
            out_types += [field_type, field_type, faults_type] + face_types
        operands = [par, ops, solution, residual, direction, recv, weight] + arrived
        if not last_round:
            operands.append(send)
        outs = pl.pallas_call(
            body,
            out_shape=out_types,
            in_specs=[smem] + [vmem] * (len(operands) - 1),
            out_specs=[vmem] * len(out_types),
            scratch_shapes=[pltpu.VMEM((columns * lines, size_z), F32)],
            compiler_params=params,
            name="cheb_round",
        )(*operands)
        solution = outs[0]
        if not last_round:
            _, residual, direction, faults, *faces = outs

    plane = full_y * full_z
    well_x = well_cells // plane
    well_y = well_cells // full_z % full_y
    well_z = well_cells % full_z
    owned = (
        (well_x // size_x == index_x)
        & (well_y // size_y == index_y)
        & (well_z // size_z == index_z)
    )
    local_cell = (well_x % size_x * size_y + well_y % size_y) * size_z + well_z % size_z

    def at_wells(flat):
        return jnp.where(owned[None, :], flat[:, local_cell].astype(jnp.float32), 0.0)

    flat_basis = basis.reshape(basis.shape[0], cells)
    flat_x = solution.reshape(columns, cells)
    first_term = jnp.dot(
        flat_basis, flat_x.astype(jnp.bfloat16).T, preferred_element_type=jnp.float32
    )
    basis_term = jnp.dot(flat_basis, flat_basis.T, preferred_element_type=jnp.float32)
    first_coeffs, basis_gram = lax.psum((first_term, basis_term), ("gx", "gy", "gz"))
    first_rest = flat_x - jnp.dot(
        first_coeffs.astype(jnp.bfloat16).T, flat_basis, preferred_element_type=jnp.float32
    )
    second_term = jnp.dot(
        flat_basis, first_rest.astype(jnp.bfloat16).T, preferred_element_type=jnp.float32
    )
    rest_term = jnp.dot(first_rest, first_rest.T, precision=lax.Precision.HIGHEST)
    second_coeffs, rest_gram, wells_rest, wells_basis = lax.psum(
        (second_term, rest_term, at_wells(first_rest), at_wells(flat_basis)), ("gx", "gy", "gz")
    )
    second_round = second_coeffs.astype(jnp.bfloat16)
    rest = first_rest - jnp.dot(second_round.T, flat_basis, preferred_element_type=jnp.float32)
    second_wide = second_round.astype(jnp.float32)
    cross = jnp.dot(second_coeffs.T, second_wide, precision=lax.Precision.HIGHEST)
    middle = jnp.dot(basis_gram, second_wide, precision=lax.Precision.HIGHEST)
    gram = (
        rest_gram
        - cross
        - cross.T
        + jnp.dot(second_wide.T, middle, precision=lax.Precision.HIGHEST)
    )
    wells_value = wells_rest - jnp.dot(second_wide.T, wells_basis, precision=lax.Precision.HIGHEST)
    lower = jnp.linalg.cholesky(gram)
    scale = math.sqrt(full_x * full_y * full_z)
    new_flat = lax.linalg.triangular_solve(lower, rest, left_side=True, lower=True) * scale
    well_resp = (
        lax.linalg.triangular_solve(lower, wells_value, left_side=True, lower=True) * scale
    ).T
    return (
        new_flat.reshape(start_block.shape),
        first_coeffs,
        first_coeffs + second_coeffs,
        well_resp,
    )


def solution(mesh):
    in_specs = (
        P(None, "gx", "gy", "gz"),
        P(None, "gx", "gy", "gz"),
        P("gx", "gy", "gz"),
        P("gx", "gy", "gz"),
        P("gx", "gy", "gz"),
        P("gx", "gy", "gz"),
        P(),
        P(),
        P(("gx", "gy", "gz"), None, None),
        P(("gx", "gy", "gz"), None, None),
        P(("gx", "gy", "gz"), None, None),
        P(),
    )
    out_specs = (P(None, "gx", "gy", "gz"), P(), P(), P())
    return jax.shard_map(local, mesh=mesh, in_specs=in_specs, out_specs=out_specs, check_vma=False)
```

```python
import functools
import math

import jax
import jax.numpy as jnp
from jax import lax
from jax.experimental import pallas as pl
from jax.experimental.pallas import tpu as pltpu
from jax.sharding import PartitionSpec as P

TERMS = 8
AXES = ("gx", "gy", "gz")
LANES = 128
VMEM_LIMIT = 48 * 1024 * 1024
BF16 = jnp.bfloat16
F32 = jnp.float32


def swap_pairs(size, odd):
    pairs = []
    for low in range(1 if odd else 0, size - 1, 2):
        pairs += [(low, low + 1), (low + 1, low)]
    return pairs


def swap(value, axis, odd):
    pairs = swap_pairs(lax.axis_size(axis), odd)
    return lax.ppermute(value, axis, pairs) if pairs else value


def from_behind(value, axis):
    size = lax.axis_size(axis)
    return lax.ppermute(value, axis, [(i, i + 1) for i in range(size - 1)])


def exchange(value):
    return lax.all_to_all(value, AXES, split_axis=0, concat_axis=0, tiled=True)


def regroup(tile, rows, slots):
    groups = LANES // slots
    columns = tile.shape[0]
    row_group = lax.broadcasted_iota(jnp.int32, tile.shape, 0) // rows
    lane_group = lax.broadcasted_iota(jnp.int32, tile.shape, 1) // slots
    ahead = lax.rem(lane_group - row_group + groups, groups)
    result = tile
    for k in range(1, groups):
        moved = pltpu.roll(tile, k * slots, 1)
        moved = pltpu.roll(moved, columns - k * rows, 0)
        result = jnp.where(ahead == k, moved, result)
    return result


def split_two(value):
    high = value.astype(BF16)
    low = (value - high.astype(F32)).astype(BF16)
    return high, low


def nt_dot(left, right):
    return lax.dot_general(left, right, (((1,), (1,)), ((), ())), preferred_element_type=F32)


def emit(direction_ref, par_ref, send_ref, faults_out, faces_out, dims):
    columns, size_x, size_y, size_z, slots = dims
    lines = size_x * size_y
    rows = columns * slots // LANES
    x_a, x_b, y_a, y_b, z_ab = faces_out
    even = [par_ref[i] == 0 for i in range(3)]
    field = direction_ref[...]
    first_x, last_x = field[:, :size_y, :], field[:, lines - size_y :, :]
    x_a[...] = jnp.where(even[0], last_x, first_x)
    if x_b is not None:
        x_b[...] = jnp.where(even[0], first_x, last_x)
    for i in range(size_x):
        first_y = direction_ref[:, i * size_y, :]
        last_y = direction_ref[:, (i + 1) * size_y - 1, :]
        y_a[i] = jnp.where(even[1], last_y, first_y)
        if y_b is not None:
            y_b[i] = jnp.where(even[1], first_y, last_y)
    both = jnp.concatenate(split_two(field.reshape(columns * lines, size_z)), axis=1)
    row = lax.broadcasted_iota(jnp.int32, (8, size_z), 0)
    lane = lax.broadcasted_iota(jnp.int32, (8, size_z), 1)
    pick = ((row == 0) & (lane == size_z - 1)) | ((row == 1) & (lane == 0))
    pick = jnp.where(pick, 1.0, 0.0).astype(BF16)
    ends = nt_dot(jnp.concatenate([pick, pick], axis=1), both)
    last_z, first_z = ends[0:1, :], ends[1:2, :]
    z_ab[0:1, :] = jnp.where(even[2], last_z, first_z)
    z_ab[1:2, :] = jnp.where(even[2], first_z, last_z)
    total = send_ref.shape[1]
    width = min(256, total)
    for start in range(0, total, width):
        cell = send_ref[:, start : start + width]
        lane_of = jnp.broadcast_to(cell % size_z, (size_z, width))
        hot = lane_of == lax.broadcasted_iota(jnp.int32, (size_z, width), 0)
        hot = jnp.where(hot, 1.0, 0.0).astype(BF16)
        found = jnp.dot(both, jnp.concatenate([hot, hot], axis=0), preferred_element_type=F32)
        line_of = jnp.broadcast_to(cell // size_z, (lines, width))
        mask = line_of == lax.broadcasted_iota(jnp.int32, (lines, width), 0)
        found = jnp.where(mask[None], found.reshape(columns, lines, width), 0.0)
        values = jnp.sum(found, axis=1)
        for j in range(0, width, LANES):
            at = (start + j) // LANES * columns
            faults_out[at : at + columns, :] = regroup(values[:, j : j + LANES], rows, slots)


def setup_kernel(dims, has_b, *refs):
    (par_ref, table_ref, which_ref, start_ref, tx_ref, ty_ref, tz_ref, pore_ref, ex_ref, ey_ref, ez_ref) = refs[:11]
    send_ref, recv_ref, weight_ref = refs[11:14]
    ops_ref, direction_ref, faults_out = refs[14:17]
    faces_out = unpack_faces(refs[17:], has_b)
    columns, size_x, size_y, size_z, slots = dims
    lines = size_x * size_y
    line = lax.broadcasted_iota(jnp.int32, (lines, size_z), 0)
    lane = lax.broadcasted_iota(jnp.int32, (lines, size_z), 1)
    last = [par_ref[3 + i] == 1 for i in range(3)]
    in_y = line % size_y
    upper_x = jnp.where((line >= lines - size_y) & last[0], 0.0, tx_ref[...])
    upper_y = jnp.where((in_y == size_y - 1) & last[1], 0.0, ty_ref[...])
    upper_z = jnp.where((lane == size_z - 1) & last[2], 0.0, tz_ref[...])
    lower_x = jnp.concatenate([ex_ref[...], upper_x[: lines - size_y]], axis=0)
    edge_y = jnp.concatenate(
        [jnp.broadcast_to(ey_ref[i : i + 1, :], (size_y, size_z)) for i in range(size_x)], axis=0
    )
    lower_y = jnp.where(in_y == 0, edge_y, pltpu.roll(upper_y, 1, 0))
    lower_z = jnp.where(lane == 0, ez_ref[...], pltpu.roll(upper_z, 1, 1))
    total = recv_ref.shape[1]
    cell = recv_ref[...]
    hot_line = jnp.broadcast_to(cell // size_z, (lines, total)) == lax.broadcasted_iota(
        jnp.int32, (lines, total), 0
    )
    hot_lane = jnp.broadcast_to(cell % size_z, (size_z, total)) == lax.broadcasted_iota(
        jnp.int32, (size_z, total), 0
    )
    weight = weight_ref[...]
    high = weight.astype(BF16).astype(F32)
    middle = (weight - high).astype(BF16).astype(F32)
    low = weight - high - middle
    parts = [jnp.where(hot_line, part, 0.0).astype(BF16) for part in (high, middle, low)]
    summed = nt_dot(jnp.concatenate(parts, axis=0), jnp.where(hot_lane, 1.0, 0.0).astype(BF16))
    fault_diag = summed[:lines] + summed[lines : 2 * lines] + summed[2 * lines :]
    shift = table_ref[which_ref[0]]
    diagonal = (
        upper_x + lower_x + upper_y + lower_y + upper_z + lower_z + shift * pore_ref[...] + fault_diag
    )
    inverse = 1.0 / diagonal
    for i, value in enumerate((upper_x, lower_x, upper_y, lower_y, upper_z, lower_z, diagonal, inverse)):
        ops_ref[i] = value
    for c in range(columns):
        direction_ref[c] = start_ref[c] * inverse
    emit(direction_ref, par_ref, send_ref, faults_out, faces_out, dims)


def unpack_faces(refs, has_b):
    refs = list(refs)
    x_a = refs.pop(0)
    x_b = refs.pop(0) if has_b[0] else None
    y_a = refs.pop(0)
    y_b = refs.pop(0) if has_b[1] else None
    return x_a, x_b, y_a, y_b, refs.pop(0)


def round_kernel(dims, has_b, keep, gain, last_round, *refs):
    refs = list(refs)
    par_ref, ops_ref, solution_ref, residual_ref, direction_ref = refs[:5]
    recv_ref, weight_ref, arrived_ref = refs[5:8]
    refs = refs[8:]
    xa_ref = refs.pop(0)
    xb_ref = refs.pop(0) if has_b[0] else xa_ref
    ya_ref = refs.pop(0)
    yb_ref = refs.pop(0) if has_b[1] else ya_ref
    za_ref = refs.pop(0)
    zb_ref = refs.pop(0) if has_b[2] else za_ref
    send_ref = None if last_round else refs.pop(0)
    solution_out = refs.pop(0)
    if not last_round:
        residual_out, direction_out, faults_out = refs[:3]
        refs = refs[3:]
        faces_out = unpack_faces(refs[: 3 + has_b[0] + has_b[1]], has_b)
        refs = refs[3 + has_b[0] + has_b[1] :]
    landed_ref = refs.pop(0)
    columns, size_x, size_y, size_z, slots = dims
    lines = size_x * size_y
    rows = columns * slots // LANES
    total = recv_ref.shape[1]
    cell = recv_ref[...]
    hot_line = jnp.broadcast_to(cell // size_z, (lines, total)) == lax.broadcasted_iota(
        jnp.int32, (lines, total), 0
    )
    hot_lane = jnp.broadcast_to(cell % size_z, (size_z, total)) == lax.broadcasted_iota(
        jnp.int32, (size_z, total), 0
    )
    hot_line = jnp.where(hot_line, 1.0, 0.0).astype(BF16)
    hot_lane = jnp.where(hot_lane, 1.0, 0.0).astype(BF16)
    tiles = [
        regroup(arrived_ref[j * columns : (j + 1) * columns, :], rows, slots)
        for j in range(total // LANES)
    ]
    weighted = (jnp.concatenate(tiles, axis=1) * weight_ref[...]).astype(BF16)
    spread = weighted[:, None, :] * hot_line[None, :, :]
    landed_ref[...] = nt_dot(spread.reshape(columns * lines, total), hot_lane)

    even = [par_ref[i] == 0 for i in range(3)]
    z_rows = jnp.concatenate(
        [
            jnp.where(even[2], zb_ref[...], za_ref[...]),
            jnp.where(even[2], za_ref[...], zb_ref[...]),
            jnp.zeros((6, columns * lines), F32),
        ],
        axis=0,
    )
    z_cols = z_rows.T
    in_y = lax.broadcasted_iota(jnp.int32, (lines, size_z), 0) % size_y
    lane = lax.broadcasted_iota(jnp.int32, (lines, size_z), 1)

    def rows_of(ref, c):
        return jnp.concatenate(
            [jnp.broadcast_to(ref[i, c : c + 1, :], (size_y, size_z)) for i in range(size_x)], axis=0
        )

    for c in range(columns):
        value = direction_ref[c]
        x_low = jnp.where(even[0], xb_ref[c], xa_ref[c])
        x_high = jnp.where(even[0], xa_ref[c], xb_ref[c])
        y_a, y_b = rows_of(ya_ref, c), rows_of(yb_ref, c)
        y_low = jnp.where(even[1], y_b, y_a)
        y_high = jnp.where(even[1], y_a, y_b)
        z_low = z_cols[c * lines : (c + 1) * lines, 0:1]
        z_high = z_cols[c * lines : (c + 1) * lines, 1:2]
        beside = ops_ref[0] * jnp.concatenate([value[size_y:], x_high], axis=0)
        beside += ops_ref[1] * jnp.concatenate([x_low, value[: lines - size_y]], axis=0)
        beside += ops_ref[2] * jnp.where(in_y == size_y - 1, y_high, pltpu.roll(value, lines - 1, 0))
        beside += ops_ref[3] * jnp.where(in_y == 0, y_low, pltpu.roll(value, 1, 0))
        beside += ops_ref[4] * jnp.where(lane == size_z - 1, z_high, pltpu.roll(value, size_z - 1, 1))
        beside += ops_ref[5] * jnp.where(lane == 0, z_low, pltpu.roll(value, 1, 1))
        landed = landed_ref[c * lines : (c + 1) * lines, :]
        left = residual_ref[c] - (ops_ref[6] * value - beside - landed)
        after = keep * value + gain * (left * ops_ref[7])
        solution_out[c] = solution_ref[c] + after
        if not last_round:
            residual_out[c] = left
            direction_out[c] = after
    if not last_round:
        emit(direction_out, par_ref, send_ref, faults_out, faces_out, dims)


def split_three(value):
    high = value.astype(BF16)
    left = value - high.astype(F32)
    middle = left.astype(BF16)
    return high, middle, (left - middle.astype(F32)).astype(BF16)


def sums_kernel(dims, solution_ref, basis_ref, well_ref, flat_out, sums_out):
    columns, size_x, size_y, size_z, slots = dims
    lines = size_x * size_y
    count = basis_ref.shape[0]
    wells = well_ref.shape[1]
    for line in range(lines):
        flat_out[:, line * size_z : (line + 1) * size_z] = solution_ref[:, line, :]
    parts = jnp.concatenate(split_three(flat_out[...]), axis=0)
    with_basis = nt_dot(parts, basis_ref[...])
    with_self = nt_dot(parts, parts)
    sums_out[...] = jnp.zeros(sums_out.shape, F32)
    blocks = count // LANES
    first = with_basis[:columns]
    beyond = with_basis[columns : 2 * columns] + with_basis[2 * columns :]
    for i in range(blocks):
        lanes = slice(i * LANES, (i + 1) * LANES)
        sums_out[i * columns : (i + 1) * columns, :] = first[:, lanes]
        sums_out[(blocks + i) * columns : (blocks + i + 1) * columns, :] = beyond[:, lanes]
    rows = with_self[:columns] + with_self[columns : 2 * columns] + with_self[2 * columns :]
    square = rows[:, :columns] + rows[:, columns : 2 * columns] + rows[:, 2 * columns :]
    at = 2 * blocks * columns
    sums_out[at : at + columns, :columns] = square
    both = jnp.concatenate(split_two(solution_ref[...].reshape(columns * lines, size_z)), axis=1)
    cell = well_ref[...]
    lane_of = jnp.broadcast_to(lax.rem(cell + size_z, size_z), (size_z, wells))
    hot = lane_of == lax.broadcasted_iota(jnp.int32, (size_z, wells), 0)
    hot = jnp.where(hot, 1.0, 0.0).astype(BF16)
    found = jnp.dot(both, jnp.concatenate([hot, hot], axis=0), preferred_element_type=F32)
    line_of = jnp.broadcast_to(jnp.where(cell < 0, -1, cell // size_z), (lines, wells))
    mask = line_of == lax.broadcasted_iota(jnp.int32, (lines, wells), 0)
    found = jnp.where(mask[None], found.reshape(columns, lines, wells), 0.0)
    at += columns
    sums_out[at : at + columns, :wells] = jnp.sum(found, axis=1)


def exact_dot(left, right, transposed=False):
    axes = ((1,), (1,)) if transposed else ((1,), (0,))
    return lax.dot_general(
        left, right, (axes, ((), ())), precision=lax.Precision.HIGHEST, preferred_element_type=F32
    )


def finish_kernel(
    dims, scale, sums_ref, gram_ref, wells_basis_ref, flat_ref, basis_ref,
    block_out, first_out, coeffs_out, wells_out,
):
    columns, size_x, size_y, size_z, slots = dims
    lines = size_x * size_y
    count = basis_ref.shape[0]
    wells = wells_basis_ref.shape[1]
    blocks = count // LANES

    def block(i):
        return sums_ref[i * columns : (i + 1) * columns, :]

    first = jnp.concatenate([block(i) for i in range(blocks)], axis=1)
    beyond = jnp.concatenate([block(blocks + i) for i in range(blocks)], axis=1)
    full = first + beyond
    square = block(2 * blocks)[:, :columns]
    at_wells = block(2 * blocks + 1)[:, :wells]
    first_round = first.astype(BF16)
    second = full - exact_dot(first_round.astype(F32), gram_ref[...])
    second_round = second.astype(BF16)
    taken = first_round.astype(F32) + second_round.astype(F32)
    half = full - 0.5 * exact_dot(taken, gram_ref[...])
    cross = exact_dot(taken, half, transposed=True)
    gram = square - cross - cross.T
    rest_wells = at_wells - exact_dot(taken, wells_basis_ref[...])
    first_out[...] = first.T
    coeffs_out[...] = (first + second).T
    row = lax.broadcasted_iota(jnp.int32, (columns, columns), 0)
    lane = lax.broadcasted_iota(jnp.int32, (columns, columns), 1)
    left = gram
    right = jnp.where(row == lane, 1.0, 0.0)
    below = lax.broadcasted_iota(jnp.int32, (columns, 1), 0)
    for k in range(columns - 1):
        factor = jnp.where(below > k, left[:, k : k + 1] / left[k : k + 1, k : k + 1], 0.0)
        right = right - factor * right[k : k + 1, :]
        left = left - factor * left[k : k + 1, :]
    pivots = jnp.sum(jnp.where(row == lane, left, 0.0), axis=1, keepdims=True)
    inverse = right * (scale / jnp.sqrt(pivots))
    wells_out[...] = exact_dot(inverse, rest_wells).T
    high, low = split_two(inverse)
    factors = jnp.concatenate([high, high, low], axis=1)
    rounds = jnp.concatenate([first_round, second_round], axis=0)
    step = min(8, lines)
    for begin in range(0, lines, step):
        lanes = slice(begin * size_z, (begin + step) * size_z)
        spans = jnp.dot(rounds, basis_ref[:, lanes], preferred_element_type=F32)
        rest = flat_ref[:, lanes] - spans[:columns] - spans[columns:]
        rest_high, rest_low = split_two(rest)
        stacked = jnp.concatenate([rest_high, rest_low, rest_high], axis=0)
        done = jnp.dot(factors, stacked, preferred_element_type=F32)
        for i in range(step):
            block_out[:, begin + i, :] = done[:, i * size_z : (i + 1) * size_z]


def local(
    start_block,
    basis,
    trans_x,
    trans_y,
    trans_z,
    pore_volume,
    shift_table,
    shift_index,
    fault_send,
    fault_recv,
    fault_trans,
    well_cells,
):
    columns, size_x, size_y, size_z = start_block.shape
    devices, slots = fault_send.shape[1:]
    lines = size_x * size_y
    cells = lines * size_z
    total = devices * slots
    sizes = [lax.axis_size(axis) for axis in AXES]
    index_x, index_y, index_z = (lax.axis_index(axis) for axis in AXES)
    full_x, full_y, full_z = size_x * sizes[0], size_y * sizes[1], size_z * sizes[2]
    has_b = tuple(size > 2 for size in sizes)
    dims = (columns, size_x, size_y, size_z, slots)
    rows = columns * slots // LANES
    index = [index_x, index_y, index_z]
    par = jnp.stack(
        [i % 2 for i in index] + [(i == n - 1).astype(jnp.int32) for i, n in zip(index, sizes)]
    )

    vmem = pl.BlockSpec(memory_space=pltpu.VMEM)
    smem = pl.BlockSpec(memory_space=pltpu.SMEM)
    params = pltpu.CompilerParams(vmem_limit_bytes=VMEM_LIMIT)
    field_type = jax.ShapeDtypeStruct((columns, lines, size_z), F32)
    x_type = jax.ShapeDtypeStruct((columns, size_y, size_z), F32)
    y_type = jax.ShapeDtypeStruct((size_x, columns, size_z), F32)
    face_types = (
        [x_type] * (1 + has_b[0])
        + [y_type] * (1 + has_b[1])
        + [jax.ShapeDtypeStruct((2, columns * lines), F32)]
    )
    faults_type = jax.ShapeDtypeStruct((devices * rows, LANES), F32)

    shape2 = (lines, size_z)
    start = start_block.reshape(columns, lines, size_z)
    edge_x = from_behind(trans_x[-1], "gx")
    edge_y = from_behind(trans_y[:, -1], "gy")
    edge_z = from_behind(trans_z[:, :, -1].reshape(1, lines), "gz").reshape(lines, 1)
    send = fault_send[0].reshape(1, total)
    recv = fault_recv[0].reshape(1, total)
    weight = fault_trans[0].reshape(1, total)

    def transfers(faults, faces):
        faces = list(faces)
        out = [exchange(faults)]
        out.append(swap(faces.pop(0), "gx", False))
        if has_b[0]:
            out.append(swap(faces.pop(0), "gx", True))
        out.append(swap(faces.pop(0), "gy", False))
        if has_b[1]:
            out.append(swap(faces.pop(0), "gy", True))
        z_ab = faces.pop(0)
        out.append(swap(z_ab[0:1], "gz", False))
        if has_b[2]:
            out.append(swap(z_ab[1:2], "gz", True))
        return out

    ops, direction, faults, *faces = pl.pallas_call(
        functools.partial(setup_kernel, dims, has_b),
        out_shape=[jax.ShapeDtypeStruct((8, lines, size_z), F32), field_type, faults_type] + face_types,
        in_specs=[smem] * 3 + [vmem] * 11,
        out_specs=[vmem] * (3 + len(face_types)),
        compiler_params=params,
        name="setup",
    )(
        par, shift_table, shift_index, start, trans_x.reshape(shape2), trans_y.reshape(shape2),
        trans_z.reshape(shape2), pore_volume.reshape(shape2), edge_x, edge_y, edge_z, send, recv, weight,
    )
    sigma = 1.0 / 0.9
    weight_now = 1.0 / sigma
    solution, residual = direction, start
    for number in range(TERMS - 1):
        arrived = transfers(faults, faces)
        weight_new = 1.0 / (2.0 * sigma - weight_now)
        last_round = number == TERMS - 2
        body = functools.partial(
            round_kernel, dims, has_b, weight_new * weight_now, 2.0 * weight_new / 0.9, last_round
        )
        weight_now = weight_new
        out_types = [field_type]
        if not last_round:
            out_types += [field_type, field_type, faults_type] + face_types
        operands = [par, ops, solution, residual, direction, recv, weight] + arrived
        if not last_round:
            operands.append(send)
        outs = pl.pallas_call(
            body,
            out_shape=out_types,
            in_specs=[smem] + [vmem] * (len(operands) - 1),
            out_specs=[vmem] * len(out_types),
            scratch_shapes=[pltpu.VMEM((columns * lines, size_z), F32)],
            compiler_params=params,
            name="cheb_round",
        )(*operands)
        solution = outs[0]
        if not last_round:
            _, residual, direction, faults, *faces = outs

    plane = full_y * full_z
    well_x = well_cells // plane
    well_y = well_cells // full_z % full_y
    well_z = well_cells % full_z
    owned = (
        (well_x // size_x == index_x)
        & (well_y // size_y == index_y)
        & (well_z // size_z == index_z)
    )
    local_cell = (well_x % size_x * size_y + well_y % size_y) * size_z + well_z % size_z
    wells = well_cells.shape[0]
    flat_basis = basis.reshape(basis.shape[0], cells)
    basis_term = jnp.dot(flat_basis, flat_basis.T, preferred_element_type=F32)
    well_term = jnp.where(owned[None, :], flat_basis[:, local_cell].astype(F32), 0.0)
    basis_gram, wells_basis = lax.psum((basis_term, well_term), AXES)
    well_local = jnp.where(owned, local_cell, -1).reshape(1, wells)

    count = basis.shape[0]
    needed = columns * (2 * (count // LANES) + 2)
    per_device = -(-needed // devices)
    per_device = 1 << (per_device - 1).bit_length()
    flat, sums = pl.pallas_call(
        functools.partial(sums_kernel, dims),
        out_shape=[
            jax.ShapeDtypeStruct((columns, cells), F32),
            jax.ShapeDtypeStruct((devices * per_device, LANES), F32),
        ],
        in_specs=[vmem] * 3,
        out_specs=[vmem] * 2,
        compiler_params=params,
        name="local_sums",
    )(solution, flat_basis, well_local)
    mine = exchange(sums).reshape(devices, per_device, LANES).sum(axis=0)
    sums = exchange(jnp.tile(mine, (devices, 1)))

    scale = math.sqrt(full_x * full_y * full_z)
    new_block, first_coeffs, coeffs, well_resp = pl.pallas_call(
        functools.partial(finish_kernel, dims, scale),
        out_shape=[
            field_type,
            jax.ShapeDtypeStruct((count, columns), F32),
            jax.ShapeDtypeStruct((count, columns), F32),
            jax.ShapeDtypeStruct((wells, columns), F32),
        ],
        in_specs=[vmem] * 5,
        out_specs=[vmem] * 4,
        compiler_params=params,
        name="finish",
    )(sums, basis_gram, wells_basis, flat, flat_basis)
    return new_block.reshape(start_block.shape), first_coeffs, coeffs, well_resp


def solution(mesh):
    in_specs = (
        P(None, "gx", "gy", "gz"),
        P(None, "gx", "gy", "gz"),
        P("gx", "gy", "gz"),
        P("gx", "gy", "gz"),
        P("gx", "gy", "gz"),
        P("gx", "gy", "gz"),
        P(),
        P(),
        P(("gx", "gy", "gz"), None, None),
        P(("gx", "gy", "gz"), None, None),
        P(("gx", "gy", "gz"), None, None),
        P(),
    )
    out_specs = (P(None, "gx", "gy", "gz"), P(), P(), P())
    return jax.shard_map(local, mesh=mesh, in_specs=in_specs, out_specs=out_specs, check_vma=False)
```

```python
import functools
import math

import jax
import jax.numpy as jnp
from jax import lax
from jax.experimental import pallas as pl
from jax.experimental.pallas import tpu as pltpu
from jax.sharding import PartitionSpec as P

TERMS = 8
AXES = ("gx", "gy", "gz")
LANES = 128
BF16 = jnp.bfloat16
F32 = jnp.float32


def swap_pairs(size, odd):
    pairs = []
    for low in range(1 if odd else 0, size - 1, 2):
        pairs += [(low, low + 1), (low + 1, low)]
    return pairs


def swap(value, axis, odd):
    pairs = swap_pairs(lax.axis_size(axis), odd)
    return lax.ppermute(value, axis, pairs) if pairs else value


def from_behind(value, axis):
    size = lax.axis_size(axis)
    return lax.ppermute(value, axis, [(i, i + 1) for i in range(size - 1)])


def exchange(value):
    return lax.all_to_all(value, AXES, split_axis=0, concat_axis=0, tiled=True)


def regroup(tile, rows, slots):
    groups = LANES // slots
    columns = tile.shape[0]
    row_group = lax.broadcasted_iota(jnp.int32, tile.shape, 0) // rows
    lane_group = lax.broadcasted_iota(jnp.int32, tile.shape, 1) // slots
    ahead = lax.rem(lane_group - row_group + groups, groups)
    result = tile
    for k in range(1, groups):
        moved = pltpu.roll(tile, k * slots, 1)
        moved = pltpu.roll(moved, columns - k * rows, 0)
        result = jnp.where(ahead == k, moved, result)
    return result


def split_two(value):
    high = value.astype(BF16)
    low = (value - high.astype(F32)).astype(BF16)
    return high, low


def nt_dot(left, right):
    return lax.dot_general(left, right, (((1,), (1,)), ((), ())), preferred_element_type=F32)


def emit(direction_ref, par_ref, send_ref, faults_out, faces_out, dims, extra=0):
    columns, size_x, size_y, size_z, slots = dims
    lines = size_x * size_y
    rows = columns * slots // LANES
    x_a, x_b, y_a, y_b, z_ab = faces_out
    even = [par_ref[i] == 0 for i in range(3)]
    field = direction_ref[...]
    first_x, last_x = field[:, :size_y, :], field[:, lines - size_y :, :]
    x_a[...] = jnp.where(even[0], last_x, first_x)
    if x_b is not None:
        x_b[...] = jnp.where(even[0], first_x, last_x)
    for i in range(size_x):
        first_y = direction_ref[:, i * size_y, :]
        last_y = direction_ref[:, (i + 1) * size_y - 1, :]
        y_a[i] = jnp.where(even[1], last_y, first_y)
        if y_b is not None:
            y_b[i] = jnp.where(even[1], first_y, last_y)
    both = jnp.concatenate(split_two(field.reshape(columns * lines, size_z)), axis=1)
    row = lax.broadcasted_iota(jnp.int32, (8, size_z), 0)
    lane = lax.broadcasted_iota(jnp.int32, (8, size_z), 1)
    pick = ((row == 0) & (lane == size_z - 1)) | ((row == 1) & (lane == 0))
    pick = jnp.where(pick, 1.0, 0.0).astype(BF16)
    ends = nt_dot(jnp.concatenate([pick, pick], axis=1), both)
    last_z, first_z = ends[0:1, :], ends[1:2, :]
    z_ab[0:1, :] = jnp.where(even[2], last_z, first_z)
    z_ab[1:2, :] = jnp.where(even[2], first_z, last_z)
    total = send_ref.shape[1]
    width = min(256, total)
    for start in range(0, total, width):
        cell = send_ref[:, start : start + width]
        lane_of = jnp.broadcast_to(cell % size_z, (size_z, width))
        hot = lane_of == lax.broadcasted_iota(jnp.int32, (size_z, width), 0)
        hot = jnp.where(hot, 1.0, 0.0).astype(BF16)
        found = jnp.dot(both, jnp.concatenate([hot, hot], axis=0), preferred_element_type=F32)
        line_of = jnp.broadcast_to(cell // size_z, (lines, width))
        mask = line_of == lax.broadcasted_iota(jnp.int32, (lines, width), 0)
        found = jnp.where(mask[None], found.reshape(columns, lines, width), 0.0)
        values = jnp.sum(found, axis=1)
        for j in range(0, width, LANES):
            tile = regroup(values[:, j : j + LANES], rows, slots)
            device = (start + j) // slots
            if not extra:
                faults_out[device * rows : device * rows + columns, :] = tile
                continue
            for i in range(LANES // slots):
                at = (device + i) * (rows + extra)
                faults_out[at : at + rows, :] = tile[i * rows : (i + 1) * rows]


def setup_kernel(dims, has_b, *refs):
    (par_ref, table_ref, which_ref, start_ref, tx_ref, ty_ref, tz_ref, pore_ref, ex_ref, ey_ref, ez_ref) = refs[:11]
    send_ref, recv_ref, weight_ref = refs[11:14]
    ops_ref, direction_ref, faults_out = refs[14:17]
    faces_out = unpack_faces(refs[17:], has_b)
    columns, size_x, size_y, size_z, slots = dims
    lines = size_x * size_y
    line = lax.broadcasted_iota(jnp.int32, (lines, size_z), 0)
    lane = lax.broadcasted_iota(jnp.int32, (lines, size_z), 1)
    last = [par_ref[3 + i] == 1 for i in range(3)]
    in_y = line % size_y
    upper_x = jnp.where((line >= lines - size_y) & last[0], 0.0, tx_ref[...])
    upper_y = jnp.where((in_y == size_y - 1) & last[1], 0.0, ty_ref[...])
    upper_z = jnp.where((lane == size_z - 1) & last[2], 0.0, tz_ref[...])
    lower_x = jnp.concatenate([ex_ref[...], upper_x[: lines - size_y]], axis=0)
    edge_y = jnp.concatenate(
        [jnp.broadcast_to(ey_ref[i : i + 1, :], (size_y, size_z)) for i in range(size_x)], axis=0
    )
    lower_y = jnp.where(in_y == 0, edge_y, pltpu.roll(upper_y, 1, 0))
    lower_z = jnp.where(lane == 0, ez_ref[...], pltpu.roll(upper_z, 1, 1))
    total = recv_ref.shape[1]
    cell = recv_ref[...]
    hot_line = jnp.broadcast_to(cell // size_z, (lines, total)) == lax.broadcasted_iota(
        jnp.int32, (lines, total), 0
    )
    hot_lane = jnp.broadcast_to(cell % size_z, (size_z, total)) == lax.broadcasted_iota(
        jnp.int32, (size_z, total), 0
    )
    weight = weight_ref[...]
    high = weight.astype(BF16).astype(F32)
    middle = (weight - high).astype(BF16).astype(F32)
    low = weight - high - middle
    parts = [jnp.where(hot_line, part, 0.0).astype(BF16) for part in (high, middle, low)]
    summed = nt_dot(jnp.concatenate(parts, axis=0), jnp.where(hot_lane, 1.0, 0.0).astype(BF16))
    fault_diag = summed[:lines] + summed[lines : 2 * lines] + summed[2 * lines :]
    shift = table_ref[which_ref[0]]
    diagonal = (
        upper_x + lower_x + upper_y + lower_y + upper_z + lower_z + shift * pore_ref[...] + fault_diag
    )
    inverse = 1.0 / diagonal
    for i, value in enumerate((upper_x, lower_x, upper_y, lower_y, upper_z, lower_z, diagonal, inverse)):
        ops_ref[i] = value
    for c in range(columns):
        direction_ref[c] = start_ref[c] * inverse
    emit(direction_ref, par_ref, send_ref, faults_out, faces_out, dims)


def unpack_faces(refs, has_b):
    refs = list(refs)
    x_a = refs.pop(0)
    x_b = refs.pop(0) if has_b[0] else None
    y_a = refs.pop(0)
    y_b = refs.pop(0) if has_b[1] else None
    return x_a, x_b, y_a, y_b, refs.pop(0)


def round_kernel(dims, has_b, keep, gain, last_round, early, *refs):
    refs = list(refs)
    extra, comes, goes = early
    par_ref, ops_ref, solution_ref, residual_ref, direction_ref = refs[:5]
    recv_ref, weight_ref, arrived_ref = refs[5:8]
    refs = refs[8:]
    xa_ref = refs.pop(0)
    xb_ref = refs.pop(0) if has_b[0] else xa_ref
    ya_ref = refs.pop(0)
    yb_ref = refs.pop(0) if has_b[1] else ya_ref
    za_ref = refs.pop(0)
    zb_ref = refs.pop(0) if has_b[2] else za_ref
    send_ref = None if last_round else refs.pop(0)
    parts_ref = refs.pop(0) if goes == "parts" else None
    solution_out = refs.pop(0)
    table_out = refs.pop(0) if comes == "sums" else None
    if not last_round:
        residual_out, direction_out, faults_out = refs[:3]
        refs = refs[3:]
        faces_out = unpack_faces(refs[: 3 + has_b[0] + has_b[1]], has_b)
        refs = refs[3 + has_b[0] + has_b[1] :]
    landed_ref = refs.pop(0)
    columns, size_x, size_y, size_z, slots = dims
    lines = size_x * size_y
    rows = columns * slots // LANES
    total = recv_ref.shape[1]
    cell = recv_ref[...]
    hot_line = jnp.broadcast_to(cell // size_z, (lines, total)) == lax.broadcasted_iota(
        jnp.int32, (lines, total), 0
    )
    hot_lane = jnp.broadcast_to(cell % size_z, (size_z, total)) == lax.broadcasted_iota(
        jnp.int32, (size_z, total), 0
    )
    hot_line = jnp.where(hot_line, 1.0, 0.0).astype(BF16)
    hot_lane = jnp.where(hot_lane, 1.0, 0.0).astype(BF16)
    tiles = []
    devices = total // slots
    if comes:
        per_device = rows + extra
        for i in range(devices):
            landed_ref[i * rows : (i + 1) * rows, :] = arrived_ref[i * per_device : i * per_device + rows, :]
        source_ref = landed_ref
    else:
        source_ref = arrived_ref
    for j in range(total // LANES):
        tiles.append(regroup(source_ref[j * columns : (j + 1) * columns, :], rows, slots))
    if comes == "parts":
        added = arrived_ref[rows : rows + extra, :]
        for i in range(1, devices):
            at = i * per_device + rows
            added = added + arrived_ref[at : at + extra, :]
    if comes == "sums":
        for i in range(devices):
            at = i * per_device + rows
            table_out[i * extra : (i + 1) * extra, :] = arrived_ref[at : at + extra, :]
    weighted = (jnp.concatenate(tiles, axis=1) * weight_ref[...]).astype(BF16)
    spread = weighted[:, None, :] * hot_line[None, :, :]
    landed_ref[...] = nt_dot(spread.reshape(columns * lines, total), hot_lane)

    even = [par_ref[i] == 0 for i in range(3)]
    z_rows = jnp.concatenate(
        [
            jnp.where(even[2], zb_ref[...], za_ref[...]),
            jnp.where(even[2], za_ref[...], zb_ref[...]),
            jnp.zeros((6, columns * lines), F32),
        ],
        axis=0,
    )
    z_cols = z_rows.T
    in_y = lax.broadcasted_iota(jnp.int32, (lines, size_z), 0) % size_y
    lane = lax.broadcasted_iota(jnp.int32, (lines, size_z), 1)

    def rows_of(ref, c):
        return jnp.concatenate(
            [jnp.broadcast_to(ref[i, c : c + 1, :], (size_y, size_z)) for i in range(size_x)], axis=0
        )

    for c in range(columns):
        value = direction_ref[c]
        x_low = jnp.where(even[0], xb_ref[c], xa_ref[c])
        x_high = jnp.where(even[0], xa_ref[c], xb_ref[c])
        y_a, y_b = rows_of(ya_ref, c), rows_of(yb_ref, c)
        y_low = jnp.where(even[1], y_b, y_a)
        y_high = jnp.where(even[1], y_a, y_b)
        z_low = z_cols[c * lines : (c + 1) * lines, 0:1]
        z_high = z_cols[c * lines : (c + 1) * lines, 1:2]
        beside = ops_ref[0] * jnp.concatenate([value[size_y:], x_high], axis=0)
        beside += ops_ref[1] * jnp.concatenate([x_low, value[: lines - size_y]], axis=0)
        beside += ops_ref[2] * jnp.where(in_y == size_y - 1, y_high, pltpu.roll(value, lines - 1, 0))
        beside += ops_ref[3] * jnp.where(in_y == 0, y_low, pltpu.roll(value, 1, 0))
        beside += ops_ref[4] * jnp.where(lane == size_z - 1, z_high, pltpu.roll(value, size_z - 1, 1))
        beside += ops_ref[5] * jnp.where(lane == 0, z_low, pltpu.roll(value, 1, 1))
        landed = landed_ref[c * lines : (c + 1) * lines, :]
        left = residual_ref[c] - (ops_ref[6] * value - beside - landed)
        after = keep * value + gain * (left * ops_ref[7])
        solution_out[c] = solution_ref[c] + after
        if not last_round:
            residual_out[c] = left
            direction_out[c] = after
    if not last_round:
        emit(direction_out, par_ref, send_ref, faults_out, faces_out, dims, extra if goes else 0)
        for i in range(devices if goes else 0):
            at = i * (rows + extra) + rows
            mine = added if goes == "sums" else parts_ref[i * extra : (i + 1) * extra, :]
            faults_out[at : at + extra, :] = mine


def basis_kernel(dims, basis_ref, well_ref, flat_out, parts_out, wide_ref, hot_ref):
    columns, size_x, size_y, size_z, slots = dims
    lines = size_x * size_y
    count = basis_ref.shape[0]
    wells = well_ref.shape[1]
    wide_ref[...] = basis_ref[...].astype(F32)
    cell = well_ref[...]
    lane_of = jnp.broadcast_to(lax.rem(cell + size_z, size_z), (size_z, wells))
    lane_of = lane_of == lax.broadcasted_iota(jnp.int32, (size_z, wells), 0)
    line_of = jnp.broadcast_to(jnp.where(cell < 0, -1, cell // size_z), (size_z, wells))
    for line in range(lines):
        flat_out[:, line * size_z : (line + 1) * size_z] = wide_ref[:, line, :].astype(BF16)
        hot = jnp.where(lane_of & (line_of == line), 1.0, 0.0)
        hot_ref[line * size_z : (line + 1) * size_z, :] = hot.astype(BF16)
    flat = flat_out[...]
    gram = nt_dot(flat, flat)
    at_wells = jnp.dot(flat, hot_ref[...], preferred_element_type=F32)
    parts_out[...] = jnp.zeros(parts_out.shape, F32)
    blocks = count // LANES
    at = 0
    for i in range(blocks):
        for j in range(i, blocks):
            parts_out[at : at + LANES, :] = gram[i * LANES : (i + 1) * LANES, j * LANES : (j + 1) * LANES]
            at += LANES
    beside = LANES // wells
    for i in range(blocks):
        place = at + i // beside * LANES
        lanes = slice(i % beside * wells, (i % beside + 1) * wells)
        parts_out[place : place + LANES, lanes] = at_wells[i * LANES : (i + 1) * LANES, :]


def split_three(value):
    high = value.astype(BF16)
    left = value - high.astype(F32)
    middle = left.astype(BF16)
    return high, middle, (left - middle.astype(F32)).astype(BF16)


def sums_kernel(dims, solution_ref, basis_ref, well_ref, flat_out, sums_out):
    columns, size_x, size_y, size_z, slots = dims
    lines = size_x * size_y
    count = basis_ref.shape[0]
    wells = well_ref.shape[1]
    for line in range(lines):
        flat_out[:, line * size_z : (line + 1) * size_z] = solution_ref[:, line, :]
    parts = jnp.concatenate(split_three(flat_out[...]), axis=0)
    with_basis = nt_dot(parts, basis_ref[...])
    with_self = nt_dot(parts, parts)
    sums_out[...] = jnp.zeros(sums_out.shape, F32)
    blocks = count // LANES
    first = with_basis[:columns]
    beyond = with_basis[columns : 2 * columns] + with_basis[2 * columns :]
    for i in range(blocks):
        lanes = slice(i * LANES, (i + 1) * LANES)
        sums_out[i * columns : (i + 1) * columns, :] = first[:, lanes]
        sums_out[(blocks + i) * columns : (blocks + i + 1) * columns, :] = beyond[:, lanes]
    rows = with_self[:columns] + with_self[columns : 2 * columns] + with_self[2 * columns :]
    square = rows[:, :columns] + rows[:, columns : 2 * columns] + rows[:, 2 * columns :]
    at = 2 * blocks * columns
    sums_out[at : at + columns, :columns] = square
    both = jnp.concatenate(split_two(solution_ref[...].reshape(columns * lines, size_z)), axis=1)
    cell = well_ref[...]
    lane_of = jnp.broadcast_to(lax.rem(cell + size_z, size_z), (size_z, wells))
    hot = lane_of == lax.broadcasted_iota(jnp.int32, (size_z, wells), 0)
    hot = jnp.where(hot, 1.0, 0.0).astype(BF16)
    found = jnp.dot(both, jnp.concatenate([hot, hot], axis=0), preferred_element_type=F32)
    line_of = jnp.broadcast_to(jnp.where(cell < 0, -1, cell // size_z), (lines, wells))
    mask = line_of == lax.broadcasted_iota(jnp.int32, (lines, wells), 0)
    found = jnp.where(mask[None], found.reshape(columns, lines, wells), 0.0)
    at += columns
    sums_out[at : at + columns, :wells] = jnp.sum(found, axis=1)


def exact_dot(left, right, transposed=False):
    axes = ((1,), (1,)) if transposed else ((1,), (0,))
    return lax.dot_general(
        left, right, (axes, ((), ())), precision=lax.Precision.HIGHEST, preferred_element_type=F32
    )


def finish_kernel(
    dims, scale, wells, sums_ref, table_ref, flat_ref, basis_ref,
    block_out, first_out, coeffs_out, wells_out,
):
    columns, size_x, size_y, size_z, slots = dims
    lines = size_x * size_y
    count = basis_ref.shape[0]
    blocks = count // LANES
    pieces, at = {}, 0
    for i in range(blocks):
        for j in range(i, blocks):
            pieces[i, j] = table_ref[at : at + LANES, :]
            pieces[j, i] = pieces[i, j] if i == j else pieces[i, j].T
            at += LANES
    basis_gram = jnp.concatenate(
        [jnp.concatenate([pieces[i, j] for j in range(blocks)], axis=1) for i in range(blocks)], axis=0
    )
    beside = LANES // wells
    wells_basis = []
    for i in range(blocks):
        place = at + i // beside * LANES
        wells_basis.append(table_ref[place : place + LANES, i % beside * wells : (i % beside + 1) * wells])
    wells_basis = jnp.concatenate(wells_basis, axis=0)

    def block(i):
        return sums_ref[i * columns : (i + 1) * columns, :]

    first = jnp.concatenate([block(i) for i in range(blocks)], axis=1)
    beyond = jnp.concatenate([block(blocks + i) for i in range(blocks)], axis=1)
    full = first + beyond
    square = block(2 * blocks)[:, :columns]
    at_wells = block(2 * blocks + 1)[:, :wells]
    first_round = first.astype(BF16)
    second = full - exact_dot(first_round.astype(F32), basis_gram)
    second_round = second.astype(BF16)
    taken = first_round.astype(F32) + second_round.astype(F32)
    half = full - 0.5 * exact_dot(taken, basis_gram)
    cross = exact_dot(taken, half, transposed=True)
    gram = square - cross - cross.T
    rest_wells = at_wells - exact_dot(taken, wells_basis)
    first_out[...] = first.T
    coeffs_out[...] = (first + second).T
    row = lax.broadcasted_iota(jnp.int32, (columns, columns), 0)
    lane = lax.broadcasted_iota(jnp.int32, (columns, columns), 1)
    left = gram
    right = jnp.where(row == lane, 1.0, 0.0)
    below = lax.broadcasted_iota(jnp.int32, (columns, 1), 0)
    for k in range(columns - 1):
        factor = jnp.where(below > k, left[:, k : k + 1] / left[k : k + 1, k : k + 1], 0.0)
        right = right - factor * right[k : k + 1, :]
        left = left - factor * left[k : k + 1, :]
    pivots = jnp.sum(jnp.where(row == lane, left, 0.0), axis=1, keepdims=True)
    inverse = right * (scale / jnp.sqrt(pivots))
    wells_out[...] = exact_dot(inverse, rest_wells).T
    high, low = split_two(inverse)
    factors = jnp.concatenate([high, high, low], axis=1)
    rounds = jnp.concatenate([first_round, second_round], axis=0)
    step = min(8, lines)
    for begin in range(0, lines, step):
        lanes = slice(begin * size_z, (begin + step) * size_z)
        spans = jnp.dot(rounds, basis_ref[:, lanes], preferred_element_type=F32)
        rest = flat_ref[:, lanes] - spans[:columns] - spans[columns:]
        rest_high, rest_low = split_two(rest)
        stacked = jnp.concatenate([rest_high, rest_low, rest_high], axis=0)
        done = jnp.dot(factors, stacked, preferred_element_type=F32)
        for i in range(step):
            block_out[:, begin + i, :] = done[:, i * size_z : (i + 1) * size_z]


def local(
    start_block,
    basis,
    trans_x,
    trans_y,
    trans_z,
    pore_volume,
    shift_table,
    shift_index,
    fault_send,
    fault_recv,
    fault_trans,
    well_cells,
):
    columns, size_x, size_y, size_z = start_block.shape
    devices, slots = fault_send.shape[1:]
    lines = size_x * size_y
    cells = lines * size_z
    total = devices * slots
    sizes = [lax.axis_size(axis) for axis in AXES]
    index_x, index_y, index_z = (lax.axis_index(axis) for axis in AXES)
    full_x, full_y, full_z = size_x * sizes[0], size_y * sizes[1], size_z * sizes[2]
    has_b = tuple(size > 2 for size in sizes)
    dims = (columns, size_x, size_y, size_z, slots)
    rows = columns * slots // LANES
    index = [index_x, index_y, index_z]
    par = jnp.stack(
        [i % 2 for i in index] + [(i == n - 1).astype(jnp.int32) for i, n in zip(index, sizes)]
    )

    vmem = pl.BlockSpec(memory_space=pltpu.VMEM)
    smem = pl.BlockSpec(memory_space=pltpu.SMEM)
    params = pltpu.CompilerParams(vmem_limit_bytes=12 * 2**20 + 6144 * total)
    wide_params = pltpu.CompilerParams(vmem_limit_bytes=32 * 2**20)
    field_type = jax.ShapeDtypeStruct((columns, lines, size_z), F32)
    x_type = jax.ShapeDtypeStruct((columns, size_y, size_z), F32)
    y_type = jax.ShapeDtypeStruct((size_x, columns, size_z), F32)
    face_types = (
        [x_type] * (1 + has_b[0])
        + [y_type] * (1 + has_b[1])
        + [jax.ShapeDtypeStruct((2, columns * lines), F32)]
    )
    faults_type = jax.ShapeDtypeStruct((devices * rows, LANES), F32)

    shape2 = (lines, size_z)
    start = start_block.reshape(columns, lines, size_z)
    edge_x = from_behind(trans_x[-1], "gx")
    edge_y = from_behind(trans_y[:, -1], "gy")
    edge_z = from_behind(trans_z[:, :, -1].reshape(1, lines), "gz").reshape(lines, 1)
    send = fault_send[0].reshape(1, total)
    recv = fault_recv[0].reshape(1, total)
    weight = fault_trans[0].reshape(1, total)

    def transfers(faults, faces):
        faces = list(faces)
        out = [exchange(faults)]
        out.append(swap(faces.pop(0), "gx", False))
        if has_b[0]:
            out.append(swap(faces.pop(0), "gx", True))
        out.append(swap(faces.pop(0), "gy", False))
        if has_b[1]:
            out.append(swap(faces.pop(0), "gy", True))
        z_ab = faces.pop(0)
        out.append(swap(z_ab[0:1], "gz", False))
        if has_b[2]:
            out.append(swap(z_ab[1:2], "gz", True))
        return out

    ops, direction, faults, *faces = pl.pallas_call(
        functools.partial(setup_kernel, dims, has_b),
        out_shape=[jax.ShapeDtypeStruct((8, lines, size_z), F32), field_type, faults_type] + face_types,
        in_specs=[smem] * 3 + [vmem] * 11,
        out_specs=[vmem] * (3 + len(face_types)),
        compiler_params=params,
        name="setup",
    )(
        par, shift_table, shift_index, start, trans_x.reshape(shape2), trans_y.reshape(shape2),
        trans_z.reshape(shape2), pore_volume.reshape(shape2), edge_x, edge_y, edge_z, send, recv, weight,
    )
    plane = full_y * full_z
    well_x = well_cells // plane
    well_y = well_cells // full_z % full_y
    well_z = well_cells % full_z
    owned = (
        (well_x // size_x == index_x)
        & (well_y // size_y == index_y)
        & (well_z // size_z == index_z)
    )
    local_cell = (well_x % size_x * size_y + well_y % size_y) * size_z + well_z % size_z
    wells = well_cells.shape[0]
    well_local = jnp.where(owned, local_cell, -1).reshape(1, wells)
    count = basis.shape[0]
    blocks = count // LANES
    early_rows = LANES * (blocks * (blocks + 1) // 2 + -(-blocks // (LANES // wells)))
    extra = -(-early_rows // devices)
    flat_basis, parts = pl.pallas_call(
        functools.partial(basis_kernel, dims),
        out_shape=[
            jax.ShapeDtypeStruct((count, cells), BF16),
            jax.ShapeDtypeStruct((devices * extra, LANES), F32),
        ],
        in_specs=[vmem] * 2,
        out_specs=[vmem] * 2,
        scratch_shapes=[pltpu.VMEM((count, lines, size_z), F32), pltpu.VMEM((cells, wells), BF16)],
        compiler_params=wide_params,
        cost_estimate=pl.CostEstimate(
            flops=2 * count * cells * (count + wells), bytes_accessed=4 * count * cells, transcendentals=0
        ),
        name="basis_gram",
    )(basis.reshape(count, lines, size_z), well_local)

    sigma = 1.0 / 0.9
    weight_now = 1.0 / sigma
    solution, residual = direction, start
    for number in range(TERMS - 1):
        arrived = transfers(faults, faces)
        weight_new = 1.0 / (2.0 * sigma - weight_now)
        last_round = number == TERMS - 2
        comes = {2: "parts", 3: "sums"}.get(number, "")
        goes = {1: "parts", 2: "sums"}.get(number, "")
        body = functools.partial(
            round_kernel, dims, has_b, weight_new * weight_now, 2.0 * weight_new / 0.9, last_round,
            (extra, comes, goes),
        )
        weight_now = weight_new
        out_types = [field_type]
        if comes == "sums":
            out_types.append(jax.ShapeDtypeStruct((devices * extra, LANES), F32))
        if not last_round:
            sent_rows = devices * (rows + (extra if goes else 0))
            out_types += [field_type, field_type, jax.ShapeDtypeStruct((sent_rows, LANES), F32)]
            out_types += face_types
        operands = [par, ops, solution, residual, direction, recv, weight] + arrived
        if not last_round:
            operands.append(send)
        if goes == "parts":
            operands.append(parts)
        outs = pl.pallas_call(
            body,
            out_shape=out_types,
            in_specs=[smem] + [vmem] * (len(operands) - 1),
            out_specs=[vmem] * len(out_types),
            scratch_shapes=[pltpu.VMEM((columns * lines, size_z), F32)],
            compiler_params=params,
            name="cheb_round",
        )(*operands)
        solution, *outs = outs
        if comes == "sums":
            table, *outs = outs
        if not last_round:
            residual, direction, faults, *faces = outs

    needed = columns * (2 * (count // LANES) + 2)
    per_device = -(-needed // devices)
    per_device = 1 << (per_device - 1).bit_length()
    flat, sums = pl.pallas_call(
        functools.partial(sums_kernel, dims),
        out_shape=[
            jax.ShapeDtypeStruct((columns, cells), F32),
            jax.ShapeDtypeStruct((devices * per_device, LANES), F32),
        ],
        in_specs=[vmem] * 3,
        out_specs=[vmem] * 2,
        compiler_params=wide_params,
        name="local_sums",
    )(solution, flat_basis, well_local)
    mine = exchange(sums).reshape(devices, per_device, LANES).sum(axis=0)
    sums = exchange(jnp.tile(mine, (devices, 1)))

    scale = math.sqrt(full_x * full_y * full_z)
    new_block, first_coeffs, coeffs, well_resp = pl.pallas_call(
        functools.partial(finish_kernel, dims, scale, wells),
        out_shape=[
            field_type,
            jax.ShapeDtypeStruct((count, columns), F32),
            jax.ShapeDtypeStruct((count, columns), F32),
            jax.ShapeDtypeStruct((wells, columns), F32),
        ],
        in_specs=[vmem] * 4,
        out_specs=[vmem] * 4,
        compiler_params=wide_params,
        name="finish",
    )(sums, table, flat, flat_basis)
    return new_block.reshape(start_block.shape), first_coeffs, coeffs, well_resp


def solution(mesh):
    in_specs = (
        P(None, "gx", "gy", "gz"),
        P(None, "gx", "gy", "gz"),
        P("gx", "gy", "gz"),
        P("gx", "gy", "gz"),
        P("gx", "gy", "gz"),
        P("gx", "gy", "gz"),
        P(),
        P(),
        P(("gx", "gy", "gz"), None, None),
        P(("gx", "gy", "gz"), None, None),
        P(("gx", "gy", "gz"), None, None),
        P(),
    )
    out_specs = (P(None, "gx", "gy", "gz"), P(), P(), P())
    return jax.shard_map(local, mesh=mesh, in_specs=in_specs, out_specs=out_specs, check_vma=False)
```

```python
import functools
import math

import jax
import jax.numpy as jnp
from jax import lax
from jax.experimental import pallas as pl
from jax.experimental.pallas import tpu as pltpu
from jax.sharding import PartitionSpec as P

TERMS = 8
AXES = ("gx", "gy", "gz")
LANES = 128
BF16 = jnp.bfloat16
F32 = jnp.float32


def swap_pairs(size, odd):
    pairs = []
    for low in range(1 if odd else 0, size - 1, 2):
        pairs += [(low, low + 1), (low + 1, low)]
    return pairs


def swap(value, axis, odd):
    pairs = swap_pairs(lax.axis_size(axis), odd)
    return lax.ppermute(value, axis, pairs) if pairs else value


def swap_rest(value, first, axis):
    size = lax.axis_size(axis)
    if size == 4:
        return [first, lax.ppermute(first, axis, [(i, i ^ 2) for i in range(size)])]
    return [first, swap(value, axis, True)] if size > 2 else [first]


def from_behind(value, axis):
    size = lax.axis_size(axis)
    return lax.ppermute(value, axis, [(i, i + 1) for i in range(size - 1)])


def exchange(value):
    return lax.all_to_all(value, AXES, split_axis=0, concat_axis=0, tiled=True)


def regroup(tile, rows, slots):
    groups = LANES // slots
    columns = tile.shape[0]
    row_group = lax.broadcasted_iota(jnp.int32, tile.shape, 0) // rows
    lane_group = lax.broadcasted_iota(jnp.int32, tile.shape, 1) // slots
    ahead = lax.rem(lane_group - row_group + groups, groups)
    result = tile
    for k in range(1, groups):
        moved = pltpu.roll(tile, k * slots, 1)
        moved = pltpu.roll(moved, columns - k * rows, 0)
        result = jnp.where(ahead == k, moved, result)
    return result


def split_two(value):
    high = value.astype(BF16)
    low = (value - high.astype(F32)).astype(BF16)
    return high, low


def nt_dot(left, right):
    return lax.dot_general(left, right, (((1,), (1,)), ((), ())), preferred_element_type=F32)


def emit_faces(direction_ref, par_ref, faces_out, dims):
    columns, size_x, size_y, size_z, slots = dims
    lines = size_x * size_y
    x_a, x_b, y_ab, z_ab = faces_out
    even = [par_ref[i] == 0 for i in range(3)]
    field = direction_ref[...]
    first_x, last_x = field[:, :size_y, :], field[:, lines - size_y :, :]
    x_a[...] = jnp.where(even[0], last_x, first_x)
    if x_b is not None:
        x_b[...] = jnp.where(even[0], first_x, last_x)
    for i in range(size_x):
        first_y = direction_ref[:, i * size_y, :]
        last_y = direction_ref[:, (i + 1) * size_y - 1, :]
        y_ab[i] = jnp.where(even[1], last_y, first_y)
        y_ab[size_x + i] = jnp.where(even[1], first_y, last_y)
    both = jnp.concatenate(split_two(field.reshape(columns * lines, size_z)), axis=1)
    row = lax.broadcasted_iota(jnp.int32, (8, size_z), 0)
    lane = lax.broadcasted_iota(jnp.int32, (8, size_z), 1)
    pick = ((row == 0) & (lane == size_z - 1)) | ((row == 1) & (lane == 0))
    pick = jnp.where(pick, 1.0, 0.0).astype(BF16)
    ends = nt_dot(jnp.concatenate([pick, pick], axis=1), both)
    last_z, first_z = ends[0:1, :], ends[1:2, :]
    z_ab[0:1, :] = jnp.where(even[2], last_z, first_z)
    z_ab[1:2, :] = jnp.where(even[2], first_z, last_z)


def gather_kernel(dims, early, *refs):
    extra, goes = early
    direction_ref, send_ref = refs[:2]
    faults_out = refs[-1]
    columns, size_x, size_y, size_z, slots = dims
    lines = size_x * size_y
    rows = columns * slots // LANES
    field = direction_ref[...]
    both = jnp.concatenate(split_two(field.reshape(columns * lines, size_z)), axis=1)
    if goes:
        for i in range(send_ref.shape[1] // slots):
            at = i * (rows + extra) + rows
            source = refs[2][...] if goes == "sums" else refs[2][i * extra : (i + 1) * extra, :]
            faults_out[at : at + extra, :] = source
    total = send_ref.shape[1]
    width = min(256, total)
    for start in range(0, total, width):
        cell = send_ref[:, start : start + width]
        lane_of = jnp.broadcast_to(cell % size_z, (size_z, width))
        hot = lane_of == lax.broadcasted_iota(jnp.int32, (size_z, width), 0)
        hot = jnp.where(hot, 1.0, 0.0).astype(BF16)
        found = jnp.dot(both, jnp.concatenate([hot, hot], axis=0), preferred_element_type=F32)
        line_of = jnp.broadcast_to(cell // size_z, (lines, width))
        mask = line_of == lax.broadcasted_iota(jnp.int32, (lines, width), 0)
        found = jnp.where(mask[None], found.reshape(columns, lines, width), 0.0)
        values = jnp.sum(found, axis=1)
        for j in range(0, width, LANES):
            tile = regroup(values[:, j : j + LANES], rows, slots)
            device = (start + j) // slots
            if not goes:
                faults_out[device * rows : device * rows + columns, :] = tile
                continue
            for i in range(LANES // slots):
                at = (device + i) * (rows + extra)
                faults_out[at : at + rows, :] = tile[i * rows : (i + 1) * rows]


def start_copies(pairs, sem):
    copies = [pltpu.make_async_copy(source, target, sem.at[i]) for i, (source, target) in enumerate(pairs)]
    for copy in copies:
        copy.start()
    return copies


def edges_kernel(dims, *refs):
    columns, size_x, size_y, size_z, slots = dims
    ex_out, ey_out, ez_out = refs[6:9]
    tables_out, held, sem = refs[9:12], refs[12:18], refs[18]
    copies = start_copies(zip(refs[:6], held), sem)
    for copy in copies:
        copy.wait()
    tx, ty, tz = held[:3]
    lines = size_x * size_y
    ex_out[...] = tx[lines - size_y :, :]
    for i in range(size_x):
        ey_out[i : i + 1, :] = ty[(i + 1) * size_y - 1 : (i + 1) * size_y, :]
    ez_out[...] = tz[...].T[size_z - 1 : size_z, :]
    for table, out in zip(held[3:], tables_out):
        value = table[0]
        out[...] = jnp.concatenate([value[i : i + 1, :] for i in range(value.shape[0])], axis=1)


def setup_kernel(dims, has_b, *refs):
    (par_ref, shifts_ref, which_ref, ex_ref, ey_ref, ez_ref, recv_ref, weight_ref) = refs[:8]
    sources = refs[8:13]
    ops_ref, residual_ref, direction_ref = refs[13:16]
    faces_out = unpack_faces(refs[16 : 19 + has_b[0]], has_b)
    held, sem = refs[19 + has_b[0] : -1], refs[-1]
    tx_ref, ty_ref, tz_ref, pore_ref = held
    copies = start_copies(zip(sources, held + (residual_ref,)), sem)
    columns, size_x, size_y, size_z, slots = dims
    lines = size_x * size_y
    line = lax.broadcasted_iota(jnp.int32, (lines, size_z), 0)
    lane = lax.broadcasted_iota(jnp.int32, (lines, size_z), 1)
    last = [par_ref[3 + i] == 1 for i in range(3)]
    in_y = line % size_y
    for copy in copies[:4]:
        copy.wait()
    upper_x = jnp.where((line >= lines - size_y) & last[0], 0.0, tx_ref[...])
    upper_y = jnp.where((in_y == size_y - 1) & last[1], 0.0, ty_ref[...])
    upper_z = jnp.where((lane == size_z - 1) & last[2], 0.0, tz_ref[...])
    lower_x = jnp.concatenate([ex_ref[...], upper_x[: lines - size_y]], axis=0)
    edge_y = jnp.concatenate(
        [jnp.broadcast_to(ey_ref[i : i + 1, :], (size_y, size_z)) for i in range(size_x)], axis=0
    )
    lower_y = jnp.where(in_y == 0, edge_y, pltpu.roll(upper_y, 1, 0))
    lower_z = jnp.where(lane == 0, jnp.broadcast_to(ez_ref[...], (8, lines)).T[:, 0:1], pltpu.roll(upper_z, 1, 1))
    total = recv_ref.shape[1]
    cell = recv_ref[...]
    hot_line = jnp.broadcast_to(cell // size_z, (lines, total)) == lax.broadcasted_iota(
        jnp.int32, (lines, total), 0
    )
    hot_lane = jnp.broadcast_to(cell % size_z, (size_z, total)) == lax.broadcasted_iota(
        jnp.int32, (size_z, total), 0
    )
    weight = weight_ref[...]
    high = weight.astype(BF16).astype(F32)
    middle = (weight - high).astype(BF16).astype(F32)
    low = weight - high - middle
    parts = [jnp.where(hot_line, part, 0.0).astype(BF16) for part in (high, middle, low)]
    summed = nt_dot(jnp.concatenate(parts, axis=0), jnp.where(hot_lane, 1.0, 0.0).astype(BF16))
    fault_diag = summed[:lines] + summed[lines : 2 * lines] + summed[2 * lines :]
    shift = shifts_ref[which_ref[0]]
    diagonal = (
        upper_x + lower_x + upper_y + lower_y + upper_z + lower_z + shift * pore_ref[...] + fault_diag
    )
    inverse = 1.0 / diagonal
    for i, value in enumerate((upper_x, lower_x, upper_y, lower_y, upper_z, lower_z, diagonal, inverse)):
        ops_ref[i] = value
    copies[4].wait()
    for c in range(columns):
        direction_ref[c] = residual_ref[c] * inverse
    emit_faces(direction_ref, par_ref, faces_out, dims)


def unpack_faces(refs, has_b):
    refs = list(refs)
    x_a = refs.pop(0)
    x_b = refs.pop(0) if has_b[0] else None
    return x_a, x_b, refs.pop(0), refs.pop(0)


def stencil_kernel(dims, has_b, *refs):
    refs = list(refs)
    columns, size_x, size_y, size_z, slots = dims
    par_ref, ops_ref, residual_ref, direction_ref = refs[:4]
    refs = refs[4:]
    xa_ref = refs.pop(0)
    xb_ref = refs.pop(0) if has_b[0] else xa_ref
    ya_ref = refs.pop(0)
    yb_ref = refs.pop(0) if has_b[1] else ya_ref
    y_b_at = size_x if has_b[1] else 0
    za_ref = refs.pop(0)
    zb_ref = refs.pop(0) if has_b[2] else za_ref
    (residual_out,) = refs
    lines = size_x * size_y
    even = [par_ref[i] == 0 for i in range(3)]
    z_a, z_b = za_ref[0:1, :], zb_ref[1:2, :] if has_b[2] else za_ref[0:1, :]
    z_rows = jnp.concatenate(
        [jnp.where(even[2], z_b, z_a), jnp.where(even[2], z_a, z_b), jnp.zeros((6, columns * lines), F32)],
        axis=0,
    )
    z_cols = z_rows.T
    in_y = lax.broadcasted_iota(jnp.int32, (lines, size_z), 0) % size_y
    lane = lax.broadcasted_iota(jnp.int32, (lines, size_z), 1)

    def rows_of(ref, at, c):
        return jnp.concatenate(
            [jnp.broadcast_to(ref[at + i, c : c + 1, :], (size_y, size_z)) for i in range(size_x)], axis=0
        )

    for c in range(columns):
        value = direction_ref[c]
        x_low = jnp.where(even[0], xb_ref[c], xa_ref[c])
        x_high = jnp.where(even[0], xa_ref[c], xb_ref[c])
        y_a, y_b = rows_of(ya_ref, 0, c), rows_of(yb_ref, y_b_at, c)
        y_low = jnp.where(even[1], y_b, y_a)
        y_high = jnp.where(even[1], y_a, y_b)
        z_low = z_cols[c * lines : (c + 1) * lines, 0:1]
        z_high = z_cols[c * lines : (c + 1) * lines, 1:2]
        beside = ops_ref[0] * jnp.concatenate([value[size_y:], x_high], axis=0)
        beside += ops_ref[1] * jnp.concatenate([x_low, value[: lines - size_y]], axis=0)
        beside += ops_ref[2] * jnp.where(in_y == size_y - 1, y_high, pltpu.roll(value, lines - 1, 0))
        beside += ops_ref[3] * jnp.where(in_y == 0, y_low, pltpu.roll(value, 1, 0))
        beside += ops_ref[4] * jnp.where(lane == size_z - 1, z_high, pltpu.roll(value, size_z - 1, 1))
        beside += ops_ref[5] * jnp.where(lane == 0, z_low, pltpu.roll(value, 1, 1))
        residual_out[c] = residual_ref[c] - (ops_ref[6] * value - beside)


def update_kernel(dims, has_b, keep, gain, first_round, last_round, early, *refs):
    refs = list(refs)
    columns, size_x, size_y, size_z, slots = dims
    extra, comes = early
    par_ref, ops_ref, residual_ref, direction_ref, recv_ref, weight_ref, arrived_ref = refs[:7]
    refs = refs[7:]
    solution_ref = direction_ref if first_round else refs.pop(0)
    if last_round:
        well_ref, basis_source, sums_out, flat_out, landed_ref, solution_out, basis_ref, sem = refs
        (basis_copy,) = start_copies([(basis_source, basis_ref)], sem)
    else:
        landed_ref = refs.pop()
        solution_out = refs.pop(0)
    table_out = refs.pop(0) if comes else None
    if not last_round:
        residual_out, direction_out = refs[:2]
        faces_out = unpack_faces(refs[2:], has_b)
    lines = size_x * size_y
    rows = columns * slots // LANES
    total = recv_ref.shape[1]
    cell = recv_ref[...]
    hot_line = jnp.broadcast_to(cell // size_z, (lines, total)) == lax.broadcasted_iota(
        jnp.int32, (lines, total), 0
    )
    hot_lane = jnp.broadcast_to(cell % size_z, (size_z, total)) == lax.broadcasted_iota(
        jnp.int32, (size_z, total), 0
    )
    hot_line = jnp.where(hot_line, 1.0, 0.0).astype(BF16)
    hot_lane = jnp.where(hot_lane, 1.0, 0.0).astype(BF16)
    tiles = []
    devices = total // slots
    if comes:
        per_device = rows + extra
        for i in range(devices):
            landed_ref[i * rows : (i + 1) * rows, :] = arrived_ref[i * per_device : i * per_device + rows, :]
        source_ref = landed_ref
    else:
        source_ref = arrived_ref
    for j in range(total // LANES):
        tiles.append(regroup(source_ref[j * columns : (j + 1) * columns, :], rows, slots))
    if comes == "parts":
        added = arrived_ref[rows : rows + extra, :]
        for i in range(1, devices):
            at = i * per_device + rows
            added = added + arrived_ref[at : at + extra, :]
        table_out[...] = added
    if comes == "sums":
        for i in range(devices):
            at = i * per_device + rows
            table_out[i * extra : (i + 1) * extra, :] = arrived_ref[at : at + extra, :]
    weighted = (jnp.concatenate(tiles, axis=1) * weight_ref[...]).astype(BF16)
    spread = weighted[:, None, :] * hot_line[None, :, :]
    landed_ref[...] = nt_dot(spread.reshape(columns * lines, total), hot_lane)
    for c in range(columns):
        left = residual_ref[c] + landed_ref[c * lines : (c + 1) * lines, :]
        after = keep * direction_ref[c] + gain * (left * ops_ref[7])
        solution_out[c] = solution_ref[c] + after
        if not last_round:
            residual_out[c] = left
            direction_out[c] = after
    if not last_round:
        emit_faces(direction_out, par_ref, faces_out, dims)
    else:
        basis_copy.wait()
        sums_of(dims, solution_out, basis_ref, well_ref, flat_out, sums_out)


def basis_kernel(dims, well_ref, source_ref, parts_out, flat_target, basis_ref, flat_out, hot_ref, sem, out_sem):
    columns, size_x, size_y, size_z, slots = dims
    lines = size_x * size_y
    count = basis_ref.shape[0]
    wells = well_ref.shape[1]
    side = 16
    groups = [pl.ds(first, side) for first in range(0, count, side)]
    copies = start_copies([(source_ref.at[g], basis_ref.at[g]) for g in groups], sem)
    row = lax.broadcasted_iota(jnp.int32, (side * side, side * side), 0)
    lane = lax.broadcasted_iota(jnp.int32, (side * side, side * side), 1)
    turn = jnp.where((row % side == lane // side) & (row // side == lane % side), 1.0, 0.0).astype(BF16)
    stores = []
    for index, first in enumerate(range(0, count, side)):
        copies[index].wait()
        for begin in range(0, lines, side):
            tile = basis_ref[first : first + side, begin : begin + side, :].reshape(side * side, size_z)
            tile = jnp.dot(turn, tile, preferred_element_type=F32).astype(BF16)
            for i in range(side):
                lanes = slice((begin + i) * size_z, (begin + i + 1) * size_z)
                flat_out[first : first + side, lanes] = tile[i * side : (i + 1) * side, :]
        stores.append(
            pltpu.make_async_copy(
                flat_out.at[groups[index]], flat_target.at[groups[index]], out_sem.at[index]
            )
        )
        stores[-1].start()
    cell = well_ref[...]
    lane_of = jnp.broadcast_to(lax.rem(cell + size_z, size_z), (size_z, wells))
    lane_of = lane_of == lax.broadcasted_iota(jnp.int32, (size_z, wells), 0)
    line_of = jnp.broadcast_to(jnp.where(cell < 0, -1, cell // size_z), (size_z, wells))
    for line in range(lines):
        hot = jnp.where(lane_of & (line_of == line), 1.0, 0.0)
        hot_ref[line * size_z : (line + 1) * size_z, :] = hot.astype(BF16)
    flat = flat_out[...]
    gram = nt_dot(flat, flat)
    at_wells = jnp.dot(flat, hot_ref[...], preferred_element_type=F32)
    parts_out[...] = jnp.zeros(parts_out.shape, F32)
    blocks = count // LANES
    at = 0
    for i in range(blocks):
        for j in range(i, blocks):
            parts_out[at : at + LANES, :] = gram[i * LANES : (i + 1) * LANES, j * LANES : (j + 1) * LANES]
            at += LANES
    beside = LANES // wells
    for i in range(blocks):
        place = at + i // beside * LANES
        lanes = slice(i % beside * wells, (i % beside + 1) * wells)
        parts_out[place : place + LANES, lanes] = at_wells[i * LANES : (i + 1) * LANES, :]
    for store in stores:
        store.wait()


def split_three(value):
    high = value.astype(BF16)
    left = value - high.astype(F32)
    middle = left.astype(BF16)
    return high, middle, (left - middle.astype(F32)).astype(BF16)


def sums_of(dims, solution_ref, basis_ref, well_ref, flat_out, sums_out):
    columns, size_x, size_y, size_z, slots = dims
    lines = size_x * size_y
    count = basis_ref.shape[0]
    wells = well_ref.shape[1]
    for line in range(lines):
        flat_out[:, line * size_z : (line + 1) * size_z] = solution_ref[:, line, :]
    parts = jnp.concatenate(split_three(flat_out[...]), axis=0)
    with_basis = nt_dot(parts, basis_ref[...])
    with_self = nt_dot(parts, parts)
    sums_out[...] = jnp.zeros(sums_out.shape, F32)
    blocks = count // LANES
    first = with_basis[:columns]
    beyond = with_basis[columns : 2 * columns] + with_basis[2 * columns :]
    for i in range(blocks):
        lanes = slice(i * LANES, (i + 1) * LANES)
        sums_out[i * columns : (i + 1) * columns, :] = first[:, lanes]
        sums_out[(blocks + i) * columns : (blocks + i + 1) * columns, :] = beyond[:, lanes]
    rows = with_self[:columns] + with_self[columns : 2 * columns] + with_self[2 * columns :]
    square = rows[:, :columns] + rows[:, columns : 2 * columns] + rows[:, 2 * columns :]
    at = 2 * blocks * columns
    sums_out[at : at + columns, :columns] = square
    both = jnp.concatenate(split_two(solution_ref[...].reshape(columns * lines, size_z)), axis=1)
    cell = well_ref[...]
    lane_of = jnp.broadcast_to(lax.rem(cell + size_z, size_z), (size_z, wells))
    hot = lane_of == lax.broadcasted_iota(jnp.int32, (size_z, wells), 0)
    hot = jnp.where(hot, 1.0, 0.0).astype(BF16)
    found = jnp.dot(both, jnp.concatenate([hot, hot], axis=0), preferred_element_type=F32)
    line_of = jnp.broadcast_to(jnp.where(cell < 0, -1, cell // size_z), (lines, wells))
    mask = line_of == lax.broadcasted_iota(jnp.int32, (lines, wells), 0)
    found = jnp.where(mask[None], found.reshape(columns, lines, wells), 0.0)
    at += columns
    sums_out[at : at + columns, :wells] = jnp.sum(found, axis=1)


def exact_dot(left, right, transposed=False):
    axes = ((1,), (1,)) if transposed else ((1,), (0,))
    return lax.dot_general(
        left, right, (axes, ((), ())), precision=lax.Precision.HIGHEST, preferred_element_type=F32
    )


def finish_kernel(
    dims, scale, wells, sums_ref, table_ref, flat_ref, basis_source,
    block_out, first_out, coeffs_out, wells_out, basis_ref, sem,
):
    (basis_copy,) = start_copies([(basis_source, basis_ref)], sem)
    columns, size_x, size_y, size_z, slots = dims
    lines = size_x * size_y
    count = basis_ref.shape[0]
    blocks = count // LANES
    pieces, at = {}, 0
    for i in range(blocks):
        for j in range(i, blocks):
            pieces[i, j] = table_ref[at : at + LANES, :]
            pieces[j, i] = pieces[i, j] if i == j else pieces[i, j].T
            at += LANES
    basis_gram = jnp.concatenate(
        [jnp.concatenate([pieces[i, j] for j in range(blocks)], axis=1) for i in range(blocks)], axis=0
    )
    beside = LANES // wells
    wells_basis = []
    for i in range(blocks):
        place = at + i // beside * LANES
        wells_basis.append(table_ref[place : place + LANES, i % beside * wells : (i % beside + 1) * wells])
    wells_basis = jnp.concatenate(wells_basis, axis=0)

    def block(i):
        return sums_ref[i * columns : (i + 1) * columns, :]

    first = jnp.concatenate([block(i) for i in range(blocks)], axis=1)
    beyond = jnp.concatenate([block(blocks + i) for i in range(blocks)], axis=1)
    full = first + beyond
    square = block(2 * blocks)[:, :columns]
    at_wells = block(2 * blocks + 1)[:, :wells]
    first_round = first.astype(BF16)
    second = full - exact_dot(first_round.astype(F32), basis_gram)
    second_round = second.astype(BF16)
    taken = first_round.astype(F32) + second_round.astype(F32)
    half = full - 0.5 * exact_dot(taken, basis_gram)
    cross = exact_dot(taken, half, transposed=True)
    gram = square - cross - cross.T
    rest_wells = at_wells - exact_dot(taken, wells_basis)
    first_out[...] = first
    coeffs_out[...] = first + second
    row = lax.broadcasted_iota(jnp.int32, (columns, columns), 0)
    lane = lax.broadcasted_iota(jnp.int32, (columns, columns), 1)
    left = gram
    right = jnp.where(row == lane, 1.0, 0.0)
    below = lax.broadcasted_iota(jnp.int32, (columns, 1), 0)
    for k in range(columns - 1):
        factor = jnp.where(below > k, left[:, k : k + 1] / left[k : k + 1, k : k + 1], 0.0)
        right = right - factor * right[k : k + 1, :]
        left = left - factor * left[k : k + 1, :]
    pivots = jnp.sum(jnp.where(row == lane, left, 0.0), axis=1, keepdims=True)
    inverse = right * (scale / jnp.sqrt(pivots))
    wells_out[...] = exact_dot(inverse, rest_wells)
    high, low = split_two(inverse)
    factors = jnp.concatenate([high, high, low], axis=1)
    basis_copy.wait()
    rounds = jnp.concatenate([first_round, second_round], axis=0)
    step = min(8, lines)
    for begin in range(0, lines, step):
        lanes = slice(begin * size_z, (begin + step) * size_z)
        spans = jnp.dot(rounds, basis_ref[:, lanes], preferred_element_type=F32)
        rest = flat_ref[:, lanes] - spans[:columns] - spans[columns:]
        rest_high, rest_low = split_two(rest)
        stacked = jnp.concatenate([rest_high, rest_low, rest_high], axis=0)
        done = jnp.dot(factors, stacked, preferred_element_type=F32)
        for i in range(step):
            block_out[:, begin + i, :] = done[:, i * size_z : (i + 1) * size_z]


def local(
    start_block,
    basis,
    trans_x,
    trans_y,
    trans_z,
    pore_volume,
    shift_table,
    shift_index,
    fault_send,
    fault_recv,
    fault_trans,
    well_cells,
):
    columns, size_x, size_y, size_z = start_block.shape
    devices, slots = fault_send.shape[1:]
    lines = size_x * size_y
    cells = lines * size_z
    total = devices * slots
    sizes = [lax.axis_size(axis) for axis in AXES]
    index_x, index_y, index_z = (lax.axis_index(axis) for axis in AXES)
    full_x, full_y, full_z = size_x * sizes[0], size_y * sizes[1], size_z * sizes[2]
    has_b = tuple(size > 2 for size in sizes)
    dims = (columns, size_x, size_y, size_z, slots)
    rows = columns * slots // LANES
    index = [index_x, index_y, index_z]
    par = jnp.stack(
        [i % 2 for i in index] + [(i == n - 1).astype(jnp.int32) for i, n in zip(index, sizes)]
    )

    vmem = pl.BlockSpec(memory_space=pltpu.VMEM)
    smem = pl.BlockSpec(memory_space=pltpu.SMEM)
    params = pltpu.CompilerParams(vmem_limit_bytes=8 * 2**20 + 4096 * total)
    wide_params = pltpu.CompilerParams(vmem_limit_bytes=16 * 2**20 + 4096 * total)
    field_type = jax.ShapeDtypeStruct((columns, lines, size_z), F32)
    x_type = jax.ShapeDtypeStruct((columns, size_y, size_z), F32)
    y_type = jax.ShapeDtypeStruct((2 * size_x, columns, size_z), F32)
    face_types = (
        [x_type] * (1 + has_b[0])
        + [y_type]
        + [jax.ShapeDtypeStruct((2, columns * lines), F32)]
    )

    def in_hbm(*values):
        return [pltpu.with_memory_space_constraint(value, pltpu.HBM) for value in values]

    shape2 = (lines, size_z)
    start = start_block.reshape(columns, lines, size_z)
    anywhere = pl.BlockSpec(memory_space=pltpu.HBM)
    trans = [value.reshape(shape2) for value in (trans_x, trans_y, trans_z)]
    row_types = [jax.ShapeDtypeStruct((1, total), kind) for kind in (jnp.int32, jnp.int32, F32)]
    edge_types = [
        jax.ShapeDtypeStruct(shape, F32) for shape in ((size_y, size_z), (size_x, size_z), (1, lines))
    ]
    edge_x, edge_y, edge_z, send, recv, weight = pl.pallas_call(
        functools.partial(edges_kernel, dims),
        out_shape=edge_types + row_types,
        in_specs=[anywhere] * 6,
        out_specs=[vmem] * 6,
        scratch_shapes=[pltpu.VMEM(shape2, F32)] * 3
        + [pltpu.VMEM(fault_send.shape, kind) for kind in (jnp.int32, jnp.int32, F32)]
        + [pltpu.SemaphoreType.DMA((6,))],
        compiler_params=params,
        name="edges",
    )(*in_hbm(*trans, fault_send, fault_recv, fault_trans))
    edge_x, edge_y, edge_z = from_behind(edge_x, "gx"), from_behind(edge_y, "gy"), from_behind(edge_z, "gz")

    def gather(direction, goes="", source=()):
        sent_rows = devices * (rows + (extra if goes else 0))
        return pl.pallas_call(
            functools.partial(gather_kernel, dims, (extra, goes)),
            out_shape=jax.ShapeDtypeStruct((sent_rows, LANES), F32),
            in_specs=[vmem] * (2 + len(source)),
            out_specs=vmem,
            compiler_params=params,
            cost_estimate=pl.CostEstimate(
                flops=4 * columns * cells * total, bytes_accessed=4 * columns * cells, transcendentals=0
            ),
            name="fault_gather",
        )(direction, send, *source)

    def transfers(faults, faces):
        *x_faces, y_ab, z_ab = faces
        y_first, z_first = swap(y_ab, "gy", False), swap(z_ab, "gz", False)
        came = [swap(face, "gx", odd) for face, odd in zip(x_faces, (False, True))]
        faults, y_first, z_first = lax.optimization_barrier((faults, y_first, z_first))
        arrived = exchange(faults)
        return arrived, came + swap_rest(y_ab, y_first, "gy") + swap_rest(z_ab, z_first, "gz")

    def stencil(residual, direction, came):
        return pl.pallas_call(
            functools.partial(stencil_kernel, dims, has_b),
            out_shape=field_type,
            in_specs=[smem] + [vmem] * (3 + len(came)),
            out_specs=vmem,
            input_output_aliases={2: 0},
            compiler_params=params,
            cost_estimate=pl.CostEstimate(
                flops=20 * columns * cells, bytes_accessed=12 * columns * cells, transcendentals=0
            ),
            name="stencil",
        )(par, ops, residual, direction, *came)

    ops, residual, direction, *faces = pl.pallas_call(
        functools.partial(setup_kernel, dims, has_b),
        out_shape=[jax.ShapeDtypeStruct((8, lines, size_z), F32), field_type, field_type] + face_types,
        in_specs=[smem] * 3 + [vmem] * 5 + [anywhere] * 5,
        out_specs=[vmem] * (3 + len(face_types)),
        scratch_shapes=[pltpu.VMEM(shape2, F32)] * 4 + [pltpu.SemaphoreType.DMA((5,))],
        compiler_params=params,
        name="setup",
    )(
        par, shift_table, shift_index, edge_x, edge_y, edge_z, recv, weight,
        *in_hbm(*trans, pore_volume.reshape(shape2), start),
    )
    plane = full_y * full_z
    well_x = well_cells // plane
    well_y = well_cells // full_z % full_y
    well_z = well_cells % full_z
    owned = (
        (well_x // size_x == index_x)
        & (well_y // size_y == index_y)
        & (well_z // size_z == index_z)
    )
    local_cell = (well_x % size_x * size_y + well_y % size_y) * size_z + well_z % size_z
    wells = well_cells.shape[0]
    well_local = jnp.where(owned, local_cell, -1).reshape(1, wells)
    count = basis.shape[0]
    blocks = count // LANES
    early_rows = LANES * (blocks * (blocks + 1) // 2 + -(-blocks // (LANES // wells)))
    extra = -(-early_rows // devices)
    flat_basis_type = pltpu.HBM((count, cells), BF16)
    parts, flat_basis = pl.pallas_call(
        functools.partial(basis_kernel, dims),
        out_shape=[jax.ShapeDtypeStruct((devices * extra, LANES), F32), flat_basis_type],
        in_specs=[vmem, anywhere],
        out_specs=[vmem, anywhere],
        scratch_shapes=[
            pltpu.VMEM((count, lines, size_z), BF16),
            pltpu.VMEM((count, cells), BF16),
            pltpu.VMEM((cells, wells), BF16),
            pltpu.SemaphoreType.DMA((count // 16,)),
            pltpu.SemaphoreType.DMA((count // 16,)),
        ],
        compiler_params=wide_params,
        cost_estimate=pl.CostEstimate(
            flops=2 * count * cells * (count + wells), bytes_accessed=4 * count * cells, transcendentals=0
        ),
        name="basis_gram",
    )(well_local, *in_hbm(basis.reshape(count, lines, size_z)))

    needed = columns * (2 * blocks + 2)
    per_device = 1 << (-(-needed // devices) - 1).bit_length()
    sums_type = jax.ShapeDtypeStruct((devices * per_device, LANES), F32)
    flat_type = jax.ShapeDtypeStruct((columns, cells), F32)
    sigma = 1.0 / 0.9
    weight_now = 1.0 / sigma
    solution = None
    for number in range(TERMS - 1):
        goes = {2: "parts", 3: "sums"}.get(number, "")
        faults = gather(direction, goes, [parts] if goes == "parts" else [table] if goes else [])
        arrived, came = transfers(faults, faces)
        residual = stencil(residual, direction, came)
        weight_new = 1.0 / (2.0 * sigma - weight_now)
        last_round = number == TERMS - 2
        body = functools.partial(
            update_kernel, dims, has_b, weight_new * weight_now, 2.0 * weight_new / 0.9,
            number == 0, last_round, (extra, goes),
        )
        weight_now = weight_new
        scratch = [pltpu.VMEM((columns * lines, size_z), F32)]
        out_types = [sums_type, flat_type] if last_round else [field_type]
        if goes:
            table_rows = extra if goes == "parts" else devices * extra
            out_types.append(jax.ShapeDtypeStruct((table_rows, LANES), F32))
        operands = [par, ops, residual, direction, recv, weight, arrived]
        aliases = {}
        if number:
            if not last_round:
                aliases[len(operands)] = 0
            operands.append(solution)
        in_specs = [smem] + [vmem] * (len(operands) - 1)
        if not last_round:
            aliases[2], aliases[3] = len(out_types), len(out_types) + 1
            out_types += [field_type, field_type] + face_types
        else:
            operands += [well_local, *in_hbm(flat_basis)]
            in_specs += [vmem, anywhere]
            scratch += [
                pltpu.VMEM((columns, lines, size_z), F32),
                pltpu.VMEM((count, cells), BF16),
                pltpu.SemaphoreType.DMA((1,)),
            ]
        outs = pl.pallas_call(
            body,
            out_shape=out_types,
            in_specs=in_specs,
            out_specs=[vmem] * len(out_types),
            scratch_shapes=scratch,
            input_output_aliases=aliases,
            compiler_params=wide_params if last_round else params,
            name="update",
        )(*operands)
        if last_round:
            sums, flat = outs
            break
        solution, *outs = outs
        if goes:
            table, *outs = outs
        residual, direction, *faces = outs

    mine = exchange(sums).reshape(devices, per_device, LANES).sum(axis=0)
    sums = exchange(jnp.tile(mine, (devices, 1)))

    scale = math.sqrt(full_x * full_y * full_z)
    new_block, first_coeffs, coeffs, well_resp = pl.pallas_call(
        functools.partial(finish_kernel, dims, scale, wells),
        out_shape=[
            field_type,
            jax.ShapeDtypeStruct((columns, count), F32),
            jax.ShapeDtypeStruct((columns, count), F32),
            jax.ShapeDtypeStruct((columns, wells), F32),
        ],
        in_specs=[vmem] * 3 + [anywhere],
        out_specs=[vmem] * 4,
        scratch_shapes=[pltpu.VMEM((count, cells), BF16), pltpu.SemaphoreType.DMA((1,))],
        compiler_params=wide_params,
        name="finish",
    )(sums, table, flat, *in_hbm(flat_basis))
    return new_block.reshape(start_block.shape), first_coeffs.T, coeffs.T, well_resp.T


def solution(mesh):
    in_specs = (
        P(None, "gx", "gy", "gz"),
        P(None, "gx", "gy", "gz"),
        P("gx", "gy", "gz"),
        P("gx", "gy", "gz"),
        P("gx", "gy", "gz"),
        P("gx", "gy", "gz"),
        P(),
        P(),
        P(("gx", "gy", "gz"), None, None),
        P(("gx", "gy", "gz"), None, None),
        P(("gx", "gy", "gz"), None, None),
        P(),
    )
    out_specs = (P(None, "gx", "gy", "gz"), P(), P(), P())
    return jax.shard_map(local, mesh=mesh, in_specs=in_specs, out_specs=out_specs, check_vma=False)
```

```python
import functools
import math

import jax
import jax.numpy as jnp
from jax import lax
from jax.experimental import pallas as pl
from jax.experimental.pallas import tpu as pltpu
from jax.sharding import PartitionSpec as P

TERMS = 8
AXES = ("gx", "gy", "gz")
LANES = 128
BF16 = jnp.bfloat16
F32 = jnp.float32


def swap_even(value, axis):
    size = lax.axis_size(axis)
    pairs = [(i, i ^ 1) for i in range(size) if i ^ 1 < size]
    return lax.ppermute(value, axis, pairs)


def swap_odd(value, axis):
    size = lax.axis_size(axis)
    other = "gy" if axis == "gx" else "gx"
    across = lax.axis_size(other)
    names = (axis, other) if axis == "gx" else (other, axis)

    def number(i, o):
        return i * across + o if axis == "gx" else o * size + i

    pairs = []
    for o in range(across):
        for i in range(size):
            to = (i + 1 if i % 2 else i - 1, o)
            if not 0 <= to[0] < size:
                to = (i, o ^ 1)
            if to[1] < across:
                pairs.append((number(i, o), number(*to)))
    return lax.ppermute(value, names, pairs)


def exchange(value):
    return lax.all_to_all(value, AXES, split_axis=0, concat_axis=0, tiled=True)


def regroup(tile, rows, slots):
    groups = LANES // slots
    columns = tile.shape[0]
    row_group = lax.broadcasted_iota(jnp.int32, tile.shape, 0) // rows
    lane_group = lax.broadcasted_iota(jnp.int32, tile.shape, 1) // slots
    ahead = lax.rem(lane_group - row_group + groups, groups)
    result = tile
    for k in range(1, groups):
        moved = pltpu.roll(tile, k * slots, 1)
        moved = pltpu.roll(moved, columns - k * rows, 0)
        result = jnp.where(ahead == k, moved, result)
    return result


def split_two(value):
    high = value.astype(BF16)
    low = (value - high.astype(F32)).astype(BF16)
    return high, low


def one_hots(cell, lines, size_z):
    half = lines // 2
    total = cell.shape[1]
    line = cell // size_z
    key = line // half * size_z + cell % size_z
    rows = jnp.broadcast_to(line % half, (half, total)) == lax.broadcasted_iota(jnp.int32, (half, total), 0)
    keys = lax.broadcasted_iota(jnp.int32, (2 * size_z, total), 0)
    keys = jnp.where(jnp.broadcast_to(key, (2 * size_z, total)) == keys, 1.0, 0.0).astype(BF16)
    return rows, keys


def nt_dot(left, right):
    return lax.dot_general(left, right, (((1,), (1,)), ((), ())), preferred_element_type=F32)


def even_places():
    return [lax.axis_index(axis) % 2 == 0 for axis in AXES]


def emit_faces(direction_ref, faces_out, dims):
    columns, size_x, size_y, size_z, slots = dims
    lines = size_x * size_y
    x_a, x_b, y_a, y_b, z_a, z_b = faces_out
    even = even_places()
    field = direction_ref[...]
    first_x, last_x = field[:, :size_y, :], field[:, lines - size_y :, :]
    x_a[...] = jnp.where(even[0], last_x, first_x)
    if x_b is not None:
        x_b[...] = jnp.where(even[0], first_x, last_x)
    for i in range(size_x):
        first_y = direction_ref[:, i * size_y, :]
        last_y = direction_ref[:, (i + 1) * size_y - 1, :]
        y_a[i] = jnp.where(even[1], last_y, first_y)
        if y_b is not None:
            y_b[i] = jnp.where(even[1], first_y, last_y)
    both = jnp.concatenate(split_two(field.reshape(columns * lines, size_z)), axis=1)
    row = lax.broadcasted_iota(jnp.int32, (8, size_z), 0)
    lane = lax.broadcasted_iota(jnp.int32, (8, size_z), 1)
    pick = ((row == 0) & (lane == size_z - 1)) | ((row == 1) & (lane == 0))
    pick = jnp.where(pick, 1.0, 0.0).astype(BF16)
    ends = nt_dot(jnp.concatenate([pick, pick], axis=1), both)
    last_z, first_z = ends[0:1, :], ends[1:2, :]
    z_a[...] = jnp.where(even[2], last_z, first_z)
    if z_b is not None:
        z_b[...] = jnp.where(even[2], first_z, last_z)


def gather_kernel(dims, early, *refs):
    extra, goes = early
    direction_ref, send_ref = refs[:2]
    faults_out = refs[-1]
    columns, size_x, size_y, size_z, slots = dims
    lines = size_x * size_y
    rows = columns * slots // LANES
    half = lines // 2
    field = direction_ref[...].astype(BF16)
    field = jnp.concatenate([field[:, :half, :], field[:, half:, :]], axis=2).reshape(columns * half, 2 * size_z)
    if goes:
        for i in range(send_ref.shape[1] // slots):
            at = i * (rows + extra) + rows
            source = refs[2][...] if goes == "sums" else refs[2][i * extra : (i + 1) * extra, :]
            faults_out[at : at + extra, :] = source
    total = send_ref.shape[1]
    width = min(256, total)
    for start in range(0, total, width):
        hot_row, hot_key = one_hots(send_ref[:, start : start + width], lines, size_z)
        found = jnp.dot(field, hot_key, preferred_element_type=F32)
        found = jnp.where(hot_row[None], found.reshape(columns, half, width), 0.0)
        values = jnp.sum(found, axis=1)
        for j in range(0, width, LANES):
            tile = regroup(values[:, j : j + LANES], rows, slots)
            device = (start + j) // slots
            if not goes:
                faults_out[device * rows : device * rows + columns, :] = tile
                continue
            for i in range(LANES // slots):
                at = (device + i) * (rows + extra)
                faults_out[at : at + rows, :] = tile[i * rows : (i + 1) * rows]


def start_copies(pairs, sem):
    copies = [pltpu.make_async_copy(source, target, sem.at[i]) for i, (source, target) in enumerate(pairs)]
    for copy in copies:
        copy.start()
    return copies


def edges_kernel(dims, *refs):
    columns, size_x, size_y, size_z, slots = dims
    ex_out, ey_out, ez_out = refs[6:9]
    tables_out, held, sem = refs[9:12], refs[12:18], refs[18]
    copies = start_copies(zip(refs[:6], held), sem)
    for copy in copies:
        copy.wait()
    tx, ty, tz = held[:3]
    lines = size_x * size_y
    ex_out[...] = tx[lines - size_y :, :]
    for i in range(size_x):
        ey_out[i : i + 1, :] = ty[(i + 1) * size_y - 1 : (i + 1) * size_y, :]
    ez_out[...] = tz[...].T[size_z - 1 : size_z, :]
    for table, out in zip(held[3:], tables_out):
        value = table[0]
        out[...] = jnp.concatenate([value[i : i + 1, :] for i in range(value.shape[0])], axis=1)


def setup_kernel(dims, has_b, *refs):
    shifts_ref, which_ref, recv_ref, weight_ref = refs[:4]
    sources = refs[4:9]
    faces = 3 + sum(has_b)
    edges = unpack_faces(refs[9 : 9 + faces], has_b)
    ops_ref, residual_ref, direction_ref = refs[9 + faces : 12 + faces]
    faces_out = unpack_faces(refs[12 + faces : 12 + 2 * faces], has_b)
    held, sem = refs[12 + 2 * faces : -1], refs[-1]
    tx_ref, ty_ref, tz_ref, pore_ref = held
    copies = start_copies(zip(sources, held + (residual_ref,)), sem)
    columns, size_x, size_y, size_z, slots = dims
    lines = size_x * size_y
    line = lax.broadcasted_iota(jnp.int32, (lines, size_z), 0)
    lane = lax.broadcasted_iota(jnp.int32, (lines, size_z), 1)
    last = [lax.axis_index(axis) == lax.axis_size(axis) - 1 for axis in AXES]
    even = even_places()
    in_y = line % size_y
    for copy in copies[:4]:
        copy.wait()
    upper_x = jnp.where((line >= lines - size_y) & last[0], 0.0, tx_ref[...])
    upper_y = jnp.where((in_y == size_y - 1) & last[1], 0.0, ty_ref[...])
    upper_z = jnp.where((lane == size_z - 1) & last[2], 0.0, tz_ref[...])
    behind = []
    for i in range(3):
        came = edges[2 * i][...]
        if edges[2 * i + 1] is not None:
            came = jnp.where(even[i], edges[2 * i + 1][...], came)
        behind.append(jnp.where(lax.axis_index(AXES[i]) == 0, 0.0, came))
    lower_x = jnp.concatenate([behind[0], upper_x[: lines - size_y]], axis=0)
    edge_y = jnp.concatenate(
        [jnp.broadcast_to(behind[1][i : i + 1, :], (size_y, size_z)) for i in range(size_x)], axis=0
    )
    lower_y = jnp.where(in_y == 0, edge_y, pltpu.roll(upper_y, 1, 0))
    lower_z = jnp.where(lane == 0, jnp.broadcast_to(behind[2], (8, lines)).T[:, 0:1], pltpu.roll(upper_z, 1, 1))
    total = recv_ref.shape[1]
    cell = recv_ref[...]
    hot_line = jnp.broadcast_to(cell // size_z, (lines, total)) == lax.broadcasted_iota(
        jnp.int32, (lines, total), 0
    )
    hot_lane = jnp.broadcast_to(cell % size_z, (size_z, total)) == lax.broadcasted_iota(
        jnp.int32, (size_z, total), 0
    )
    weight = weight_ref[...]
    high = weight.astype(BF16).astype(F32)
    middle = (weight - high).astype(BF16).astype(F32)
    low = weight - high - middle
    parts = [jnp.where(hot_line, part, 0.0).astype(BF16) for part in (high, middle, low)]
    summed = nt_dot(jnp.concatenate(parts, axis=0), jnp.where(hot_lane, 1.0, 0.0).astype(BF16))
    fault_diag = summed[:lines] + summed[lines : 2 * lines] + summed[2 * lines :]
    shift = shifts_ref[which_ref[0]]
    diagonal = (
        upper_x + lower_x + upper_y + lower_y + upper_z + lower_z + shift * pore_ref[...] + fault_diag
    )
    inverse = 1.0 / diagonal
    for i, value in enumerate((upper_x, lower_x, upper_y, lower_y, upper_z, lower_z, diagonal, inverse)):
        ops_ref[i] = value
    copies[4].wait()
    for c in range(columns):
        direction_ref[c] = residual_ref[c] * inverse
    emit_faces(direction_ref, faces_out, dims)


def unpack_faces(refs, has_b):
    refs = list(refs)
    faces = []
    for more in has_b:
        faces += [refs.pop(0), refs.pop(0) if more else None]
    return faces


def stencil_kernel(dims, has_b, first_round, *refs):
    refs = list(refs)
    columns, size_x, size_y, size_z, slots = dims
    ops_ref, residual_ref, direction_ref = refs[:3]
    refs = refs[3:]
    solution_out, residual_out = refs.pop(), refs.pop()
    solution_ref = None if first_round else refs.pop()
    xa_ref, xb_ref, ya_ref, yb_ref, za_ref, zb_ref = unpack_faces(refs, has_b)
    xb_ref = xa_ref if xb_ref is None else xb_ref
    yb_ref = ya_ref if yb_ref is None else yb_ref
    zb_ref = za_ref if zb_ref is None else zb_ref
    lines = size_x * size_y
    even = even_places()
    z_a, z_b = za_ref[...], zb_ref[...]
    z_rows = jnp.concatenate(
        [jnp.where(even[2], z_b, z_a), jnp.where(even[2], z_a, z_b), jnp.zeros((6, columns * lines), F32)],
        axis=0,
    )
    z_cols = z_rows.T
    in_y = lax.broadcasted_iota(jnp.int32, (lines, size_z), 0) % size_y
    lane = lax.broadcasted_iota(jnp.int32, (lines, size_z), 1)

    def rows_of(ref, c):
        return jnp.concatenate(
            [jnp.broadcast_to(ref[i, c : c + 1, :], (size_y, size_z)) for i in range(size_x)], axis=0
        )

    for c in range(columns):
        value = direction_ref[c]
        x_low = jnp.where(even[0], xb_ref[c], xa_ref[c])
        x_high = jnp.where(even[0], xa_ref[c], xb_ref[c])
        y_a, y_b = rows_of(ya_ref, c), rows_of(yb_ref, c)
        y_low = jnp.where(even[1], y_b, y_a)
        y_high = jnp.where(even[1], y_a, y_b)
        z_low = z_cols[c * lines : (c + 1) * lines, 0:1]
        z_high = z_cols[c * lines : (c + 1) * lines, 1:2]
        beside = ops_ref[0] * jnp.concatenate([value[size_y:], x_high], axis=0)
        beside += ops_ref[1] * jnp.concatenate([x_low, value[: lines - size_y]], axis=0)
        beside += ops_ref[2] * jnp.where(in_y == size_y - 1, y_high, pltpu.roll(value, lines - 1, 0))
        beside += ops_ref[3] * jnp.where(in_y == 0, y_low, pltpu.roll(value, 1, 0))
        beside += ops_ref[4] * jnp.where(lane == size_z - 1, z_high, pltpu.roll(value, size_z - 1, 1))
        beside += ops_ref[5] * jnp.where(lane == 0, z_low, pltpu.roll(value, 1, 1))
        residual_out[c] = residual_ref[c] - (ops_ref[6] * value - beside)
        solution_out[c] = value if first_round else solution_ref[c] + value


def update_kernel(dims, has_b, keep, gain, last_round, early, *refs):
    refs = list(refs)
    columns, size_x, size_y, size_z, slots = dims
    extra, comes = early
    ops_ref, residual_ref, direction_ref, recv_ref, weight_ref, arrived_ref = refs[:6]
    refs = refs[6:]
    if last_round:
        solution_ref, well_ref, basis_source, sums_out, flat_out, landed_ref, solution_out, basis_ref, sem = refs
        (basis_copy,) = start_copies([(basis_source, basis_ref)], sem)
    else:
        landed_ref = refs.pop()
    table_out = refs.pop(0) if comes else None
    if not last_round:
        residual_out, direction_out = refs[:2]
        faces_out = unpack_faces(refs[2:], has_b)
    lines = size_x * size_y
    rows = columns * slots // LANES
    total = recv_ref.shape[1]
    half = lines // 2
    hot_row, hot_key = one_hots(recv_ref[...], lines, size_z)
    hot_row = jnp.where(hot_row, 1.0, 0.0).astype(BF16)
    tiles = []
    devices = total // slots
    if comes:
        per_device = rows + extra
        for i in range(devices):
            landed_ref[i * rows : (i + 1) * rows, :LANES] = arrived_ref[i * per_device : i * per_device + rows, :]
        source_ref = landed_ref
    else:
        source_ref = arrived_ref
    for j in range(total // LANES):
        tiles.append(regroup(source_ref[j * columns : (j + 1) * columns, :LANES], rows, slots))
    if comes == "parts":
        added = arrived_ref[rows : rows + extra, :]
        for i in range(1, devices):
            at = i * per_device + rows
            added = added + arrived_ref[at : at + extra, :]
        table_out[...] = added
    if comes == "sums":
        for i in range(devices):
            at = i * per_device + rows
            table_out[i * extra : (i + 1) * extra, :] = arrived_ref[at : at + extra, :]
    weighted = (jnp.concatenate(tiles, axis=1) * weight_ref[...]).astype(BF16)
    spread = weighted[:, None, :] * hot_row[None, :, :]
    landed_ref[...] = nt_dot(spread.reshape(columns * half, total), hot_key)
    for c in range(columns):
        landed = landed_ref[c * half : (c + 1) * half, :]
        left = residual_ref[c] + jnp.concatenate([landed[:, :size_z], landed[:, size_z:]], axis=0)
        after = keep * direction_ref[c] + gain * (left * ops_ref[7])
        if last_round:
            solution_out[c] = solution_ref[c] + after
        else:
            residual_out[c] = left
            direction_out[c] = after
    if not last_round:
        emit_faces(direction_out, faces_out, dims)
    else:
        basis_copy.wait()
        sums_of(dims, solution_out, basis_ref, well_ref, flat_out, sums_out)


def basis_kernel(dims, well_ref, source_ref, parts_out, flat_target, basis_ref, flat_out, hot_ref, sem, out_sem):
    columns, size_x, size_y, size_z, slots = dims
    lines = size_x * size_y
    count = basis_ref.shape[0]
    wells = well_ref.shape[1]
    side = 16
    groups = [pl.ds(first, side) for first in range(0, count, side)]
    copies = [pltpu.make_async_copy(source_ref.at[g], basis_ref.at[g], sem.at[i]) for i, g in enumerate(groups)]
    ahead = 4
    for copy in copies[:ahead]:
        copy.start()
    row = lax.broadcasted_iota(jnp.int32, (side * side, side * side), 0)
    lane = lax.broadcasted_iota(jnp.int32, (side * side, side * side), 1)
    turn = jnp.where((row % side == lane // side) & (row // side == lane % side), 1.0, 0.0).astype(BF16)
    stores = []
    for index in range(0, len(groups), 2):
        for i in (index, index + 1):
            copies[i].wait()
            if i + ahead < len(copies):
                copies[i + ahead].start()
        first = index * side
        for begin in range(0, lines, side):
            tile = [
                basis_ref[at : at + side, begin : begin + side, :].reshape(side * side, size_z)
                for at in (first, first + side)
            ]
            tile = jnp.dot(turn, jnp.concatenate(tile, axis=1), preferred_element_type=F32).astype(BF16)
            for i in range(side):
                lanes = slice((begin + i) * size_z, (begin + i + 1) * size_z)
                flat_out[first : first + side, lanes] = tile[i * side : (i + 1) * side, :size_z]
                flat_out[first + side : first + 2 * side, lanes] = tile[i * side : (i + 1) * side, size_z:]
        for i in (index, index + 1):
            stores.append(
                pltpu.make_async_copy(flat_out.at[groups[i]], flat_target.at[groups[i]], out_sem.at[i])
            )
            stores[-1].start()
    cell = well_ref[...]
    lane_of = jnp.broadcast_to(lax.rem(cell + size_z, size_z), (size_z, wells))
    lane_of = lane_of == lax.broadcasted_iota(jnp.int32, (size_z, wells), 0)
    line_of = jnp.broadcast_to(jnp.where(cell < 0, -1, cell // size_z), (size_z, wells))
    for line in range(lines):
        hot = jnp.where(lane_of & (line_of == line), 1.0, 0.0)
        hot_ref[line * size_z : (line + 1) * size_z, :] = hot.astype(BF16)
    flat = flat_out[...]
    gram = nt_dot(flat, flat)
    at_wells = jnp.dot(flat, hot_ref[...], preferred_element_type=F32)
    parts_out[...] = jnp.zeros(parts_out.shape, F32)
    blocks = count // LANES
    at = 0
    for i in range(blocks):
        for j in range(i, blocks):
            parts_out[at : at + LANES, :] = gram[i * LANES : (i + 1) * LANES, j * LANES : (j + 1) * LANES]
            at += LANES
    beside = LANES // wells
    for i in range(blocks):
        place = at + i // beside * LANES
        lanes = slice(i % beside * wells, (i % beside + 1) * wells)
        parts_out[place : place + LANES, lanes] = at_wells[i * LANES : (i + 1) * LANES, :]
    for store in stores:
        store.wait()


def split_three(value):
    high = value.astype(BF16)
    left = value - high.astype(F32)
    middle = left.astype(BF16)
    return high, middle, (left - middle.astype(F32)).astype(BF16)


def sums_of(dims, solution_ref, basis_ref, well_ref, flat_out, sums_out):
    columns, size_x, size_y, size_z, slots = dims
    lines = size_x * size_y
    count = basis_ref.shape[0]
    wells = well_ref.shape[1]
    for line in range(lines):
        flat_out[:, line * size_z : (line + 1) * size_z] = solution_ref[:, line, :]
    parts = jnp.concatenate(split_three(flat_out[...]), axis=0)
    with_basis = nt_dot(parts, basis_ref[...])
    with_self = nt_dot(parts, parts)
    sums_out[...] = jnp.zeros(sums_out.shape, F32)
    blocks = count // LANES
    first = with_basis[:columns]
    beyond = with_basis[columns : 2 * columns] + with_basis[2 * columns :]
    for i in range(blocks):
        lanes = slice(i * LANES, (i + 1) * LANES)
        sums_out[i * columns : (i + 1) * columns, :] = first[:, lanes]
        sums_out[(blocks + i) * columns : (blocks + i + 1) * columns, :] = beyond[:, lanes]
    rows = with_self[:columns] + with_self[columns : 2 * columns] + with_self[2 * columns :]
    square = rows[:, :columns] + rows[:, columns : 2 * columns] + rows[:, 2 * columns :]
    at = 2 * blocks * columns
    sums_out[at : at + columns, :columns] = square
    both = jnp.concatenate(split_two(solution_ref[...].reshape(columns * lines, size_z)), axis=1)
    cell = well_ref[...]
    lane_of = jnp.broadcast_to(lax.rem(cell + size_z, size_z), (size_z, wells))
    hot = lane_of == lax.broadcasted_iota(jnp.int32, (size_z, wells), 0)
    hot = jnp.where(hot, 1.0, 0.0).astype(BF16)
    found = jnp.dot(both, jnp.concatenate([hot, hot], axis=0), preferred_element_type=F32)
    line_of = jnp.broadcast_to(jnp.where(cell < 0, -1, cell // size_z), (lines, wells))
    mask = line_of == lax.broadcasted_iota(jnp.int32, (lines, wells), 0)
    found = jnp.where(mask[None], found.reshape(columns, lines, wells), 0.0)
    at += columns
    sums_out[at : at + columns, :wells] = jnp.sum(found, axis=1)


def exact_dot(left, right, transposed=False):
    axes = ((1,), (1,)) if transposed else ((1,), (0,))
    return lax.dot_general(
        left, right, (axes, ((), ())), precision=lax.Precision.HIGHEST, preferred_element_type=F32
    )


def finish_kernel(
    dims, scale, wells, sums_ref, table_ref, flat_ref, basis_source,
    block_out, first_out, coeffs_out, wells_out, basis_ref, sem,
):
    (basis_copy,) = start_copies([(basis_source, basis_ref)], sem)
    columns, size_x, size_y, size_z, slots = dims
    lines = size_x * size_y
    count = basis_ref.shape[0]
    blocks = count // LANES
    pieces, at = {}, 0
    for i in range(blocks):
        for j in range(i, blocks):
            pieces[i, j] = table_ref[at : at + LANES, :]
            pieces[j, i] = pieces[i, j] if i == j else pieces[i, j].T
            at += LANES
    basis_gram = jnp.concatenate(
        [jnp.concatenate([pieces[i, j] for j in range(blocks)], axis=1) for i in range(blocks)], axis=0
    )
    beside = LANES // wells
    wells_basis = []
    for i in range(blocks):
        place = at + i // beside * LANES
        wells_basis.append(table_ref[place : place + LANES, i % beside * wells : (i % beside + 1) * wells])
    wells_basis = jnp.concatenate(wells_basis, axis=0)

    def block(i):
        return sums_ref[i * columns : (i + 1) * columns, :]

    first = jnp.concatenate([block(i) for i in range(blocks)], axis=1)
    beyond = jnp.concatenate([block(blocks + i) for i in range(blocks)], axis=1)
    full = first + beyond
    square = block(2 * blocks)[:, :columns]
    at_wells = block(2 * blocks + 1)[:, :wells]
    first_round = first.astype(BF16)
    second = full - exact_dot(first_round.astype(F32), basis_gram)
    second_round = second.astype(BF16)
    taken = first_round.astype(F32) + second_round.astype(F32)
    half = full - 0.5 * exact_dot(taken, basis_gram)
    cross = exact_dot(taken, half, transposed=True)
    gram = square - cross - cross.T
    rest_wells = at_wells - exact_dot(taken, wells_basis)
    first_out[...] = first
    coeffs_out[...] = first + second
    row = lax.broadcasted_iota(jnp.int32, (columns, columns), 0)
    lane = lax.broadcasted_iota(jnp.int32, (columns, columns), 1)
    left = gram
    right = jnp.where(row == lane, 1.0, 0.0)
    below = lax.broadcasted_iota(jnp.int32, (columns, 1), 0)
    for k in range(columns - 1):
        factor = jnp.where(below > k, left[:, k : k + 1] / left[k : k + 1, k : k + 1], 0.0)
        right = right - factor * right[k : k + 1, :]
        left = left - factor * left[k : k + 1, :]
    pivots = jnp.sum(jnp.where(row == lane, left, 0.0), axis=1, keepdims=True)
    inverse = right * (scale / jnp.sqrt(pivots))
    wells_out[...] = exact_dot(inverse, rest_wells)
    high, low = split_two(inverse)
    factors = jnp.concatenate([high, high, low], axis=1)
    basis_copy.wait()
    rounds = jnp.concatenate([first_round, second_round], axis=0)
    step = min(8, lines)
    for begin in range(0, lines, step):
        lanes = slice(begin * size_z, (begin + step) * size_z)
        spans = jnp.dot(rounds, basis_ref[:, lanes], preferred_element_type=F32)
        rest = flat_ref[:, lanes] - spans[:columns] - spans[columns:]
        rest_high, rest_low = split_two(rest)
        stacked = jnp.concatenate([rest_high, rest_low, rest_high], axis=0)
        done = jnp.dot(factors, stacked, preferred_element_type=F32)
        for i in range(step):
            block_out[:, begin + i, :] = done[:, i * size_z : (i + 1) * size_z]


def local(
    start_block,
    basis,
    trans_x,
    trans_y,
    trans_z,
    pore_volume,
    shift_table,
    shift_index,
    fault_send,
    fault_recv,
    fault_trans,
    well_cells,
):
    columns, size_x, size_y, size_z = start_block.shape
    devices, slots = fault_send.shape[1:]
    lines = size_x * size_y
    cells = lines * size_z
    total = devices * slots
    sizes = [lax.axis_size(axis) for axis in AXES]
    index_x, index_y, index_z = (lax.axis_index(axis) for axis in AXES)
    full_x, full_y, full_z = size_x * sizes[0], size_y * sizes[1], size_z * sizes[2]
    has_b = tuple(size > 2 for size in sizes)
    dims = (columns, size_x, size_y, size_z, slots)
    rows = columns * slots // LANES

    vmem = pl.BlockSpec(memory_space=pltpu.VMEM)
    smem = pl.BlockSpec(memory_space=pltpu.SMEM)
    params = pltpu.CompilerParams(vmem_limit_bytes=8 * 2**20 + 4096 * total)
    wide_params = pltpu.CompilerParams(vmem_limit_bytes=16 * 2**20 + 4096 * total)
    field_type = jax.ShapeDtypeStruct((columns, lines, size_z), F32)
    x_type = jax.ShapeDtypeStruct((columns, size_y, size_z), F32)
    y_type = jax.ShapeDtypeStruct((size_x, columns, size_z), F32)
    z_type = jax.ShapeDtypeStruct((1, columns * lines), F32)
    face_types = [x_type] * (1 + has_b[0]) + [y_type] * (1 + has_b[1]) + [z_type] * (1 + has_b[2])

    def in_hbm(*values):
        return [pltpu.with_memory_space_constraint(value, pltpu.HBM) for value in values]

    shape2 = (lines, size_z)
    start = start_block.reshape(columns, lines, size_z)
    anywhere = pl.BlockSpec(memory_space=pltpu.HBM)
    trans = [value.reshape(shape2) for value in (trans_x, trans_y, trans_z)]
    row_types = [jax.ShapeDtypeStruct((1, total), kind) for kind in (jnp.int32, jnp.int32, F32)]
    edge_types = [
        jax.ShapeDtypeStruct(shape, F32) for shape in ((size_y, size_z), (size_x, size_z), (1, lines))
    ]
    edge_x, edge_y, edge_z, send, recv, weight = pl.pallas_call(
        functools.partial(edges_kernel, dims),
        out_shape=edge_types + row_types,
        in_specs=[anywhere] * 6,
        out_specs=[vmem] * 6,
        scratch_shapes=[pltpu.VMEM(shape2, F32)] * 3
        + [pltpu.VMEM(fault_send.shape, kind) for kind in (jnp.int32, jnp.int32, F32)]
        + [pltpu.SemaphoreType.DMA((6,))],
        compiler_params=params,
        name="edges",
    )(*in_hbm(*trans, fault_send, fault_recv, fault_trans))
    edges = []
    for axis, edge, more in zip(AXES, (edge_x, edge_y, edge_z), has_b):
        edges += [swap_even(edge, axis)] + ([swap_odd(edge, axis)] if more else [])

    def gather(direction, goes="", source=()):
        sent_rows = devices * (rows + (extra if goes else 0))
        return pl.pallas_call(
            functools.partial(gather_kernel, dims, (extra, goes)),
            out_shape=jax.ShapeDtypeStruct((sent_rows, LANES), F32),
            in_specs=[vmem] * (2 + len(source)),
            out_specs=vmem,
            compiler_params=params,
            cost_estimate=pl.CostEstimate(
                flops=4 * columns * cells * total, bytes_accessed=4 * columns * cells, transcendentals=0
            ),
            name="fault_gather",
        )(direction, send, *source)

    def transfers(faults, faces):
        faces = list(faces)
        came = []
        for axis, more in zip(AXES, has_b):
            came.append(swap_even(faces.pop(0), axis))
            if more:
                came.append(swap_odd(faces.pop(0), axis))
        first = [1 + has_b[0], 2 + has_b[0] + has_b[1]]
        faults, came[first[0]], came[first[1]] = lax.optimization_barrier(
            (faults, came[first[0]], came[first[1]])
        )
        return exchange(faults), came

    def stencil(residual, direction, came, solution):
        more = [] if solution is None else [solution]
        return pl.pallas_call(
            functools.partial(stencil_kernel, dims, has_b, solution is None),
            out_shape=[field_type, field_type],
            in_specs=[vmem] * (3 + len(came) + len(more)),
            out_specs=[vmem] * 2,
            input_output_aliases={1: 0, 3 + len(came): 1} if more else {1: 0},
            compiler_params=params,
            cost_estimate=pl.CostEstimate(
                flops=20 * columns * cells, bytes_accessed=12 * columns * cells, transcendentals=0
            ),
            name="stencil",
        )(ops, residual, direction, *came, *more)

    ops, residual, direction, *faces = pl.pallas_call(
        functools.partial(setup_kernel, dims, has_b),
        out_shape=[jax.ShapeDtypeStruct((8, lines, size_z), F32), field_type, field_type] + face_types,
        in_specs=[smem] * 2 + [vmem] * 2 + [anywhere] * 5 + [vmem] * len(edges),
        out_specs=[vmem] * (3 + len(face_types)),
        scratch_shapes=[pltpu.VMEM(shape2, F32)] * 4 + [pltpu.SemaphoreType.DMA((5,))],
        compiler_params=params,
        name="setup",
    )(
        shift_table, shift_index, recv, weight,
        *in_hbm(*trans, pore_volume.reshape(shape2), start), *edges,
    )
    plane = full_y * full_z
    well_x = well_cells // plane
    well_y = well_cells // full_z % full_y
    well_z = well_cells % full_z
    owned = (
        (well_x // size_x == index_x)
        & (well_y // size_y == index_y)
        & (well_z // size_z == index_z)
    )
    local_cell = (well_x % size_x * size_y + well_y % size_y) * size_z + well_z % size_z
    wells = well_cells.shape[0]
    well_local = jnp.where(owned, local_cell, -1).reshape(1, wells)
    count = basis.shape[0]
    blocks = count // LANES
    early_rows = LANES * (blocks * (blocks + 1) // 2 + -(-blocks // (LANES // wells)))
    extra = -(-early_rows // devices)
    flat_basis_type = pltpu.HBM((count, cells), BF16)
    parts, flat_basis = pl.pallas_call(
        functools.partial(basis_kernel, dims),
        out_shape=[jax.ShapeDtypeStruct((devices * extra, LANES), F32), flat_basis_type],
        in_specs=[vmem, anywhere],
        out_specs=[vmem, anywhere],
        scratch_shapes=[
            pltpu.VMEM((count, lines, size_z), BF16),
            pltpu.VMEM((count, cells), BF16),
            pltpu.VMEM((cells, wells), BF16),
            pltpu.SemaphoreType.DMA((count // 16,)),
            pltpu.SemaphoreType.DMA((count // 16,)),
        ],
        compiler_params=wide_params,
        cost_estimate=pl.CostEstimate(
            flops=2 * count * cells * (count + wells), bytes_accessed=4 * count * cells, transcendentals=0
        ),
        name="basis_gram",
    )(well_local, *in_hbm(basis.reshape(count, lines, size_z)))

    needed = columns * (2 * blocks + 2)
    per_device = 1 << (-(-needed // devices) - 1).bit_length()
    sums_type = jax.ShapeDtypeStruct((devices * per_device, LANES), F32)
    flat_type = jax.ShapeDtypeStruct((columns, cells), F32)
    sigma = 1.0 / 0.9
    weight_now = 1.0 / sigma
    solution = None
    for number in range(TERMS - 1):
        goes = {2: "parts", 3: "sums"}.get(number, "")
        faults = gather(direction, goes, [parts] if goes == "parts" else [table] if goes else [])
        arrived, came = transfers(faults, faces)
        residual, solution = stencil(residual, direction, came, solution)
        weight_new = 1.0 / (2.0 * sigma - weight_now)
        last_round = number == TERMS - 2
        body = functools.partial(
            update_kernel, dims, has_b, weight_new * weight_now, 2.0 * weight_new / 0.9,
            last_round, (extra, goes),
        )
        weight_now = weight_new
        scratch = [pltpu.VMEM((columns * lines // 2, 2 * size_z), F32)]
        out_types = [sums_type, flat_type] if last_round else []
        if goes:
            table_rows = extra if goes == "parts" else devices * extra
            out_types.append(jax.ShapeDtypeStruct((table_rows, LANES), F32))
        operands = [ops, residual, direction, recv, weight, arrived]
        aliases = {}
        if last_round:
            operands.append(solution)
        in_specs = [vmem] * len(operands)
        if not last_round:
            aliases[1], aliases[2] = len(out_types), len(out_types) + 1
            out_types += [field_type, field_type] + face_types
        else:
            operands += [well_local, *in_hbm(flat_basis)]
            in_specs += [vmem, anywhere]
            scratch += [
                pltpu.VMEM((columns, lines, size_z), F32),
                pltpu.VMEM((count, cells), BF16),
                pltpu.SemaphoreType.DMA((1,)),
            ]
        outs = pl.pallas_call(
            body,
            out_shape=out_types,
            in_specs=in_specs,
            out_specs=[vmem] * len(out_types),
            scratch_shapes=scratch,
            input_output_aliases=aliases,
            compiler_params=wide_params if last_round else params,
            name="update",
        )(*operands)
        if last_round:
            sums, flat = outs
            break
        if goes:
            table, *outs = outs
        residual, direction, *faces = outs

    mine = exchange(sums).reshape(devices, per_device, LANES).sum(axis=0)
    sums = exchange(jnp.tile(mine, (devices, 1)))

    scale = math.sqrt(full_x * full_y * full_z)
    new_block, first_coeffs, coeffs, well_resp = pl.pallas_call(
        functools.partial(finish_kernel, dims, scale, wells),
        out_shape=[
            field_type,
            jax.ShapeDtypeStruct((columns, count), F32),
            jax.ShapeDtypeStruct((columns, count), F32),
            jax.ShapeDtypeStruct((columns, wells), F32),
        ],
        in_specs=[vmem] * 3 + [anywhere],
        out_specs=[vmem] * 4,
        scratch_shapes=[pltpu.VMEM((count, cells), BF16), pltpu.SemaphoreType.DMA((1,))],
        compiler_params=wide_params,
        name="finish",
    )(sums, table, flat, *in_hbm(flat_basis))
    return new_block.reshape(start_block.shape), first_coeffs.T, coeffs.T, well_resp.T


def solution(mesh):
    in_specs = (
        P(None, "gx", "gy", "gz"),
        P(None, "gx", "gy", "gz"),
        P("gx", "gy", "gz"),
        P("gx", "gy", "gz"),
        P("gx", "gy", "gz"),
        P("gx", "gy", "gz"),
        P(),
        P(),
        P(("gx", "gy", "gz"), None, None),
        P(("gx", "gy", "gz"), None, None),
        P(("gx", "gy", "gz"), None, None),
        P(),
    )
    out_specs = (P(None, "gx", "gy", "gz"), P(), P(), P())
    return jax.shard_map(local, mesh=mesh, in_specs=in_specs, out_specs=out_specs, check_vma=False)
```

```python
import functools
import math

import jax
import jax.numpy as jnp
from jax import lax
from jax.experimental import pallas as pl
from jax.experimental.pallas import tpu as pltpu
from jax.sharding import PartitionSpec as P

TERMS = 8
AXES = ("gx", "gy", "gz")
LANES = 128
BF16 = jnp.bfloat16
F32 = jnp.float32


def swap_even(value, axis):
    size = lax.axis_size(axis)
    pairs = [(i, i ^ 1) for i in range(size) if i ^ 1 < size]
    return lax.ppermute(value, axis, pairs)


def swap_odd(value, axis):
    size = lax.axis_size(axis)
    other = "gy" if axis == "gx" else "gx"
    across = lax.axis_size(other)
    names = (axis, other) if axis == "gx" else (other, axis)

    def number(i, o):
        return i * across + o if axis == "gx" else o * size + i

    pairs = []
    for o in range(across):
        for i in range(size):
            to = (i + 1 if i % 2 else i - 1, o)
            if not 0 <= to[0] < size:
                to = (i, o ^ 1)
            if to[1] < across:
                pairs.append((number(i, o), number(*to)))
    return lax.ppermute(value, names, pairs)


def exchange(value):
    return lax.all_to_all(value, AXES, split_axis=0, concat_axis=0, tiled=True)


def regroup(tile, rows, slots):
    groups = LANES // slots
    columns = tile.shape[0]
    row_group = lax.broadcasted_iota(jnp.int32, tile.shape, 0) // rows
    lane_group = lax.broadcasted_iota(jnp.int32, tile.shape, 1) // slots
    ahead = lax.rem(lane_group - row_group + groups, groups)
    result = tile
    for k in range(1, groups):
        moved = pltpu.roll(tile, k * slots, 1)
        moved = pltpu.roll(moved, columns - k * rows, 0)
        result = jnp.where(ahead == k, moved, result)
    return result


def split_two(value):
    high = value.astype(BF16)
    low = (value - high.astype(F32)).astype(BF16)
    return high, low


def one_hots(cell, lines, size_z):
    half = lines // 2
    total = cell.shape[1]
    line = cell // size_z
    key = line // half * size_z + cell % size_z
    rows = jnp.broadcast_to(line % half, (half, total)) == lax.broadcasted_iota(jnp.int32, (half, total), 0)
    keys = lax.broadcasted_iota(jnp.int32, (2 * size_z, total), 0)
    keys = jnp.where(jnp.broadcast_to(key, (2 * size_z, total)) == keys, 1.0, 0.0).astype(BF16)
    return rows, keys


def nt_dot(left, right):
    return lax.dot_general(left, right, (((1,), (1,)), ((), ())), preferred_element_type=F32)


def even_places():
    return [lax.axis_index(axis) % 2 == 0 for axis in AXES]


def emit_faces(direction_ref, faces_out, dims):
    columns, size_x, size_y, size_z, slots = dims
    lines = size_x * size_y
    x_a, x_b, y_a, y_b, z_a, z_b = faces_out
    even = even_places()
    field = direction_ref[...]
    first_x, last_x = field[:, :size_y, :], field[:, lines - size_y :, :]
    x_a[...] = jnp.where(even[0], last_x, first_x)
    if x_b is not None:
        x_b[...] = jnp.where(even[0], first_x, last_x)
    for i in range(size_x):
        first_y = direction_ref[:, i * size_y, :]
        last_y = direction_ref[:, (i + 1) * size_y - 1, :]
        y_a[i] = jnp.where(even[1], last_y, first_y)
        if y_b is not None:
            y_b[i] = jnp.where(even[1], first_y, last_y)
    both = jnp.concatenate(split_two(field.reshape(columns * lines, size_z)), axis=1)
    row = lax.broadcasted_iota(jnp.int32, (8, size_z), 0)
    lane = lax.broadcasted_iota(jnp.int32, (8, size_z), 1)
    pick = ((row == 0) & (lane == size_z - 1)) | ((row == 1) & (lane == 0))
    pick = jnp.where(pick, 1.0, 0.0).astype(BF16)
    ends = nt_dot(jnp.concatenate([pick, pick], axis=1), both)
    last_z, first_z = ends[0:1, :], ends[1:2, :]
    z_a[...] = jnp.where(even[2], last_z, first_z)
    if z_b is not None:
        z_b[...] = jnp.where(even[2], first_z, last_z)


def gather_kernel(dims, early, *refs):
    extra, goes = early
    direction_ref, send_ref = refs[:2]
    faults_out = refs[-1]
    columns, size_x, size_y, size_z, slots = dims
    lines = size_x * size_y
    rows = columns * slots // LANES
    half = lines // 2
    field = direction_ref[...].astype(BF16)
    field = jnp.concatenate([field[:, :half, :], field[:, half:, :]], axis=2).reshape(columns * half, 2 * size_z)
    if goes:
        for i in range(send_ref.shape[1] // slots):
            at = i * (rows + extra) + rows
            source = refs[2][...] if goes == "sums" else refs[2][i * extra : (i + 1) * extra, :]
            faults_out[at : at + extra, :] = source
    total = send_ref.shape[1]
    width = min(256, total)
    for start in range(0, total, width):
        hot_row, hot_key = one_hots(send_ref[:, start : start + width], lines, size_z)
        found = jnp.dot(field, hot_key, preferred_element_type=F32)
        found = jnp.where(hot_row[None], found.reshape(columns, half, width), 0.0)
        values = jnp.sum(found, axis=1)
        for j in range(0, width, LANES):
            tile = regroup(values[:, j : j + LANES], rows, slots)
            device = (start + j) // slots
            if not goes:
                faults_out[device * rows : device * rows + columns, :] = tile
                continue
            for i in range(LANES // slots):
                at = (device + i) * (rows + extra)
                faults_out[at : at + rows, :] = tile[i * rows : (i + 1) * rows]


def start_copies(pairs, sem):
    copies = [pltpu.make_async_copy(source, target, sem.at[i]) for i, (source, target) in enumerate(pairs)]
    for copy in copies:
        copy.start()
    return copies


def edges_kernel(dims, *refs):
    columns, size_x, size_y, size_z, slots = dims
    ex_out, ey_out, ez_out = refs[6:9]
    tables_out, held, sem = refs[9:12], refs[12:18], refs[18]
    copies = start_copies(zip(refs[:6], held), sem)
    for copy in copies:
        copy.wait()
    tx, ty, tz = held[:3]
    lines = size_x * size_y
    ex_out[...] = tx[lines - size_y :, :]
    for i in range(size_x):
        ey_out[i : i + 1, :] = ty[(i + 1) * size_y - 1 : (i + 1) * size_y, :]
    ez_out[...] = tz[...].T[size_z - 1 : size_z, :]
    for table, out in zip(held[3:], tables_out):
        value = table[0]
        out[...] = jnp.concatenate([value[i : i + 1, :] for i in range(value.shape[0])], axis=1)


def setup_kernel(dims, has_b, *refs):
    shifts_ref, which_ref, recv_ref, weight_ref = refs[:4]
    sources = refs[4:9]
    faces = 3 + sum(has_b)
    edges = unpack_faces(refs[9 : 9 + faces], has_b)
    ops_ref, residual_ref, direction_ref = refs[9 + faces : 12 + faces]
    faces_out = unpack_faces(refs[12 + faces : 12 + 2 * faces], has_b)
    held, sem = refs[12 + 2 * faces : -1], refs[-1]
    tx_ref, ty_ref, tz_ref, pore_ref = held
    copies = start_copies(zip(sources, held + (residual_ref,)), sem)
    columns, size_x, size_y, size_z, slots = dims
    lines = size_x * size_y
    line = lax.broadcasted_iota(jnp.int32, (lines, size_z), 0)
    lane = lax.broadcasted_iota(jnp.int32, (lines, size_z), 1)
    last = [lax.axis_index(axis) == lax.axis_size(axis) - 1 for axis in AXES]
    even = even_places()
    in_y = line % size_y
    for copy in copies[:-1]:
        copy.wait()
    upper_x = jnp.where((line >= lines - size_y) & last[0], 0.0, tx_ref[...])
    upper_y = jnp.where((in_y == size_y - 1) & last[1], 0.0, ty_ref[...])
    upper_z = jnp.where((lane == size_z - 1) & last[2], 0.0, tz_ref[...])
    behind = []
    for i in range(3):
        came = edges[2 * i][...]
        if edges[2 * i + 1] is not None:
            came = jnp.where(even[i], edges[2 * i + 1][...], came)
        behind.append(jnp.where(lax.axis_index(AXES[i]) == 0, 0.0, came))
    lower_x = jnp.concatenate([behind[0], upper_x[: lines - size_y]], axis=0)
    edge_y = jnp.concatenate(
        [jnp.broadcast_to(behind[1][i : i + 1, :], (size_y, size_z)) for i in range(size_x)], axis=0
    )
    lower_y = jnp.where(in_y == 0, edge_y, pltpu.roll(upper_y, 1, 0))
    lower_z = jnp.where(lane == 0, jnp.broadcast_to(behind[2], (8, lines)).T[:, 0:1], pltpu.roll(upper_z, 1, 1))
    total = recv_ref.shape[1]
    cell = recv_ref[...]
    hot_line = jnp.broadcast_to(cell // size_z, (lines, total)) == lax.broadcasted_iota(
        jnp.int32, (lines, total), 0
    )
    hot_lane = jnp.broadcast_to(cell % size_z, (size_z, total)) == lax.broadcasted_iota(
        jnp.int32, (size_z, total), 0
    )
    weight = weight_ref[...]
    high = weight.astype(BF16).astype(F32)
    middle = (weight - high).astype(BF16).astype(F32)
    low = weight - high - middle
    parts = [jnp.where(hot_line, part, 0.0).astype(BF16) for part in (high, middle, low)]
    summed = nt_dot(jnp.concatenate(parts, axis=0), jnp.where(hot_lane, 1.0, 0.0).astype(BF16))
    fault_diag = summed[:lines] + summed[lines : 2 * lines] + summed[2 * lines :]
    number = lax.broadcasted_iota(jnp.int32, shifts_ref.shape, 1)
    shift = jnp.sum(jnp.where(number == which_ref[...], shifts_ref[...], 0.0), axis=1, keepdims=True)
    diagonal = (
        upper_x + lower_x + upper_y + lower_y + upper_z + lower_z + shift * pore_ref[...] + fault_diag
    )
    inverse = 1.0 / diagonal
    inner_y = jnp.where(in_y == size_y - 1, 0.0, upper_y), jnp.where(in_y == 0, 0.0, lower_y)
    inner_z = jnp.where(lane == size_z - 1, 0.0, upper_z), jnp.where(lane == 0, 0.0, lower_z)
    face_y = upper_y - inner_y[0] + (lower_y - inner_y[1])
    face_z = upper_z - inner_z[0] + (lower_z - inner_z[1])
    for i, value in enumerate((upper_x, lower_x, *inner_y, *inner_z, diagonal, inverse, face_y, face_z)):
        ops_ref[i] = value
    copies[-1].wait()
    for c in range(columns):
        direction_ref[c] = residual_ref[c] * inverse
    emit_faces(direction_ref, faces_out, dims)


def unpack_faces(refs, has_b):
    refs = list(refs)
    faces = []
    for more in has_b:
        faces += [refs.pop(0), refs.pop(0) if more else None]
    return faces


def stencil_kernel(dims, has_b, first_round, *refs):
    refs = list(refs)
    columns, size_x, size_y, size_z, slots = dims
    ops_ref, residual_ref, direction_ref = refs[:3]
    refs = refs[3:]
    solution_out, residual_out = refs.pop(), refs.pop()
    solution_ref = None if first_round else refs.pop()
    xa_ref, xb_ref = refs[0], refs[-1]
    lines = size_x * size_y
    even = lax.axis_index(AXES[0]) % 2 == 0
    for c in range(columns):
        value = direction_ref[c]
        x_low = jnp.where(even, xb_ref[c], xa_ref[c])
        x_high = jnp.where(even, xa_ref[c], xb_ref[c])
        beside = ops_ref[0] * jnp.concatenate([value[size_y:], x_high], axis=0)
        beside += ops_ref[1] * jnp.concatenate([x_low, value[: lines - size_y]], axis=0)
        beside += ops_ref[2] * pltpu.roll(value, lines - 1, 0)
        beside += ops_ref[3] * pltpu.roll(value, 1, 0)
        beside += ops_ref[4] * pltpu.roll(value, size_z - 1, 1)
        beside += ops_ref[5] * pltpu.roll(value, 1, 1)
        residual_out[c] = residual_ref[c] - (ops_ref[6] * value - beside)
        solution_out[c] = value if first_round else solution_ref[c] + value


def update_kernel(dims, has_b, keep, gain, last_round, early, *refs):
    refs = list(refs)
    columns, size_x, size_y, size_z, slots = dims
    extra, comes = early
    ops_ref, residual_ref, direction_ref, recv_ref, weight_ref, arrived_ref = refs[:6]
    refs = refs[6:]
    ya_ref, yb_ref, za_ref, zb_ref = unpack_faces(refs[: 2 + has_b[1] + has_b[2]], has_b[1:])
    refs = refs[2 + has_b[1] + has_b[2] :]
    yb_ref = ya_ref if yb_ref is None else yb_ref
    zb_ref = za_ref if zb_ref is None else zb_ref
    if last_round:
        solution_ref, well_ref, basis_source, sums_out, flat_out, landed_ref, solution_out, basis_ref, sem = refs
        (basis_copy,) = start_copies([(basis_source, basis_ref)], sem)
    else:
        landed_ref = refs.pop()
    table_out = refs.pop(0) if comes else None
    if not last_round:
        residual_out, direction_out = refs[:2]
        faces_out = unpack_faces(refs[2:], has_b)
    lines = size_x * size_y
    rows = columns * slots // LANES
    total = recv_ref.shape[1]
    half = lines // 2
    hot_row, hot_key = one_hots(recv_ref[...], lines, size_z)
    hot_row = jnp.where(hot_row, 1.0, 0.0).astype(BF16)
    tiles = []
    devices = total // slots
    if comes:
        per_device = rows + extra
        for i in range(devices):
            landed_ref[i * rows : (i + 1) * rows, :LANES] = arrived_ref[i * per_device : i * per_device + rows, :]
        source_ref = landed_ref
    else:
        source_ref = arrived_ref
    for j in range(total // LANES):
        tiles.append(regroup(source_ref[j * columns : (j + 1) * columns, :LANES], rows, slots))
    if comes == "parts":
        added = arrived_ref[rows : rows + extra, :]
        for i in range(1, devices):
            at = i * per_device + rows
            added = added + arrived_ref[at : at + extra, :]
        table_out[...] = added
    if comes == "sums":
        for i in range(devices):
            at = i * per_device + rows
            table_out[i * extra : (i + 1) * extra, :] = arrived_ref[at : at + extra, :]
    weighted = (jnp.concatenate(tiles, axis=1) * weight_ref[...]).astype(BF16)
    spread = weighted[:, None, :] * hot_row[None, :, :]
    landed_ref[...] = nt_dot(spread.reshape(columns * half, total), hot_key)
    even = even_places()
    in_slab = lax.broadcasted_iota(jnp.int32, (size_y, size_z), 0)
    lane = lax.broadcasted_iota(jnp.int32, (lines, size_z), 1)
    z_a, z_b = za_ref[...], zb_ref[...]
    z_rows = [jnp.where(even[2], z_b, z_a), jnp.where(even[2], z_a, z_b), jnp.zeros((6, columns * lines), F32)]
    z_cols = jnp.concatenate(z_rows, axis=0).T
    for c in range(columns):
        landed = landed_ref[c * half : (c + 1) * half, :]
        left = residual_ref[c] + jnp.concatenate([landed[:, :size_z], landed[:, size_z:]], axis=0)
        beside_y = []
        for i in range(size_x):
            y_a, y_b = ya_ref[i, c : c + 1, :], yb_ref[i, c : c + 1, :]
            y_low, y_high = jnp.where(even[1], y_b, y_a), jnp.where(even[1], y_a, y_b)
            beside_y.append(jnp.where(in_slab < size_y // 2, y_low, y_high))
        z_low = z_cols[c * lines : (c + 1) * lines, 0:1]
        z_high = z_cols[c * lines : (c + 1) * lines, 1:2]
        left = left + ops_ref[8] * jnp.concatenate(beside_y, axis=0)
        left = left + ops_ref[9] * jnp.where(lane < size_z // 2, z_low, z_high)
        after = keep * direction_ref[c] + gain * (left * ops_ref[7])
        if last_round:
            solution_out[c] = solution_ref[c] + after
        else:
            residual_out[c] = left
            direction_out[c] = after
    if not last_round:
        emit_faces(direction_out, faces_out, dims)
    else:
        basis_copy.wait()
        sums_of(dims, solution_out, basis_ref, well_ref, flat_out, sums_out)


def basis_kernel(dims, well_ref, source_ref, parts_out, flat_target, basis_ref, flat_out, hot_ref, sem, out_sem):
    columns, size_x, size_y, size_z, slots = dims
    lines = size_x * size_y
    count = basis_ref.shape[0]
    wells = well_ref.shape[1]
    side = 16
    groups = [pl.ds(first, side) for first in range(0, count, side)]
    copies = [pltpu.make_async_copy(source_ref.at[g], basis_ref.at[g], sem.at[i]) for i, g in enumerate(groups)]
    ahead = 4
    for copy in copies[:ahead]:
        copy.start()
    row = lax.broadcasted_iota(jnp.int32, (side * side, side * side), 0)
    lane = lax.broadcasted_iota(jnp.int32, (side * side, side * side), 1)
    turn = jnp.where((row % side == lane // side) & (row // side == lane % side), 1.0, 0.0).astype(BF16)
    stores = []
    for index in range(0, len(groups), 2):
        for i in (index, index + 1):
            copies[i].wait()
            if i + ahead < len(copies):
                copies[i + ahead].start()
        first = index * side
        for begin in range(0, lines, side):
            tile = [
                basis_ref[at : at + side, begin : begin + side, :].reshape(side * side, size_z)
                for at in (first, first + side)
            ]
            tile = jnp.dot(turn, jnp.concatenate(tile, axis=1), preferred_element_type=F32).astype(BF16)
            for i in range(side):
                lanes = slice((begin + i) * size_z, (begin + i + 1) * size_z)
                flat_out[first : first + side, lanes] = tile[i * side : (i + 1) * side, :size_z]
                flat_out[first + side : first + 2 * side, lanes] = tile[i * side : (i + 1) * side, size_z:]
        for i in (index, index + 1):
            stores.append(
                pltpu.make_async_copy(flat_out.at[groups[i]], flat_target.at[groups[i]], out_sem.at[i])
            )
            stores[-1].start()
    cell = well_ref[...]
    lane_of = jnp.broadcast_to(lax.rem(cell + size_z, size_z), (size_z, wells))
    lane_of = lane_of == lax.broadcasted_iota(jnp.int32, (size_z, wells), 0)
    line_of = jnp.broadcast_to(jnp.where(cell < 0, -1, cell // size_z), (size_z, wells))
    for line in range(lines):
        hot = jnp.where(lane_of & (line_of == line), 1.0, 0.0)
        hot_ref[line * size_z : (line + 1) * size_z, :] = hot.astype(BF16)
    flat = flat_out[...]
    gram = nt_dot(flat, flat)
    at_wells = jnp.dot(flat, hot_ref[...], preferred_element_type=F32)
    parts_out[...] = jnp.zeros(parts_out.shape, F32)
    blocks = count // LANES
    at = 0
    for i in range(blocks):
        for j in range(i, blocks):
            parts_out[at : at + LANES, :] = gram[i * LANES : (i + 1) * LANES, j * LANES : (j + 1) * LANES]
            at += LANES
    beside = LANES // wells
    for i in range(blocks):
        place = at + i // beside * LANES
        lanes = slice(i % beside * wells, (i % beside + 1) * wells)
        parts_out[place : place + LANES, lanes] = at_wells[i * LANES : (i + 1) * LANES, :]
    for store in stores:
        store.wait()


def split_three(value):
    high = value.astype(BF16)
    left = value - high.astype(F32)
    middle = left.astype(BF16)
    return high, middle, (left - middle.astype(F32)).astype(BF16)


def sums_of(dims, solution_ref, basis_ref, well_ref, flat_out, sums_out):
    columns, size_x, size_y, size_z, slots = dims
    lines = size_x * size_y
    count = basis_ref.shape[0]
    wells = well_ref.shape[1]
    for line in range(lines):
        flat_out[:, line * size_z : (line + 1) * size_z] = solution_ref[:, line, :]
    parts = jnp.concatenate(split_three(flat_out[...]), axis=0)
    with_basis = nt_dot(parts, basis_ref[...])
    with_self = nt_dot(parts, parts)
    sums_out[...] = jnp.zeros(sums_out.shape, F32)
    blocks = count // LANES
    first = with_basis[:columns]
    beyond = with_basis[columns : 2 * columns] + with_basis[2 * columns :]
    for i in range(blocks):
        lanes = slice(i * LANES, (i + 1) * LANES)
        sums_out[i * columns : (i + 1) * columns, :] = first[:, lanes]
        sums_out[(blocks + i) * columns : (blocks + i + 1) * columns, :] = beyond[:, lanes]
    rows = with_self[:columns] + with_self[columns : 2 * columns] + with_self[2 * columns :]
    square = rows[:, :columns] + rows[:, columns : 2 * columns] + rows[:, 2 * columns :]
    at = 2 * blocks * columns
    sums_out[at : at + columns, :columns] = square
    both = jnp.concatenate(split_two(solution_ref[...].reshape(columns * lines, size_z)), axis=1)
    cell = well_ref[...]
    lane_of = jnp.broadcast_to(lax.rem(cell + size_z, size_z), (size_z, wells))
    hot = lane_of == lax.broadcasted_iota(jnp.int32, (size_z, wells), 0)
    hot = jnp.where(hot, 1.0, 0.0).astype(BF16)
    found = jnp.dot(both, jnp.concatenate([hot, hot], axis=0), preferred_element_type=F32)
    line_of = jnp.broadcast_to(jnp.where(cell < 0, -1, cell // size_z), (lines, wells))
    mask = line_of == lax.broadcasted_iota(jnp.int32, (lines, wells), 0)
    found = jnp.where(mask[None], found.reshape(columns, lines, wells), 0.0)
    at += columns
    sums_out[at : at + columns, :wells] = jnp.sum(found, axis=1)


def exact_dot(left, right, transposed=False):
    axes = ((1,), (1,)) if transposed else ((1,), (0,))
    return lax.dot_general(
        left, right, (axes, ((), ())), precision=lax.Precision.HIGHEST, preferred_element_type=F32
    )


def finish_kernel(
    dims, scale, wells, sums_ref, table_ref, flat_ref, basis_source,
    block_out, first_out, coeffs_out, wells_out, basis_ref, sem,
):
    (basis_copy,) = start_copies([(basis_source, basis_ref)], sem)
    columns, size_x, size_y, size_z, slots = dims
    lines = size_x * size_y
    count = basis_ref.shape[0]
    blocks = count // LANES
    pieces, at = {}, 0
    for i in range(blocks):
        for j in range(i, blocks):
            pieces[i, j] = table_ref[at : at + LANES, :]
            pieces[j, i] = pieces[i, j] if i == j else pieces[i, j].T
            at += LANES
    basis_gram = jnp.concatenate(
        [jnp.concatenate([pieces[i, j] for j in range(blocks)], axis=1) for i in range(blocks)], axis=0
    )
    beside = LANES // wells
    wells_basis = []
    for i in range(blocks):
        place = at + i // beside * LANES
        wells_basis.append(table_ref[place : place + LANES, i % beside * wells : (i % beside + 1) * wells])
    wells_basis = jnp.concatenate(wells_basis, axis=0)

    def block(i):
        return sums_ref[i * columns : (i + 1) * columns, :]

    first = jnp.concatenate([block(i) for i in range(blocks)], axis=1)
    beyond = jnp.concatenate([block(blocks + i) for i in range(blocks)], axis=1)
    full = first + beyond
    square = block(2 * blocks)[:, :columns]
    at_wells = block(2 * blocks + 1)[:, :wells]
    first_round = first.astype(BF16)
    second = full - exact_dot(first_round.astype(F32), basis_gram)
    second_round = second.astype(BF16)
    taken = first_round.astype(F32) + second_round.astype(F32)
    half = full - 0.5 * exact_dot(taken, basis_gram)
    cross = exact_dot(taken, half, transposed=True)
    gram = square - cross - cross.T
    rest_wells = at_wells - exact_dot(taken, wells_basis)
    first_out[...] = first
    coeffs_out[...] = first + second
    row = lax.broadcasted_iota(jnp.int32, (columns, columns), 0)
    lane = lax.broadcasted_iota(jnp.int32, (columns, columns), 1)
    left = gram
    right = jnp.where(row == lane, 1.0, 0.0)
    below = lax.broadcasted_iota(jnp.int32, (columns, 1), 0)
    for k in range(columns - 1):
        factor = jnp.where(below > k, left[:, k : k + 1] / left[k : k + 1, k : k + 1], 0.0)
        right = right - factor * right[k : k + 1, :]
        left = left - factor * left[k : k + 1, :]
    pivots = jnp.sum(jnp.where(row == lane, left, 0.0), axis=1, keepdims=True)
    inverse = right * (scale / jnp.sqrt(pivots))
    wells_out[...] = exact_dot(inverse, rest_wells)
    high, low = split_two(inverse)
    factors = jnp.concatenate([high, high, low], axis=1)
    basis_copy.wait()
    rounds = jnp.concatenate([first_round, second_round], axis=0)
    step = min(8, lines)
    for begin in range(0, lines, step):
        lanes = slice(begin * size_z, (begin + step) * size_z)
        spans = jnp.dot(rounds, basis_ref[:, lanes], preferred_element_type=F32)
        rest = flat_ref[:, lanes] - spans[:columns] - spans[columns:]
        rest_high, rest_low = split_two(rest)
        stacked = jnp.concatenate([rest_high, rest_low, rest_high], axis=0)
        done = jnp.dot(factors, stacked, preferred_element_type=F32)
        for i in range(step):
            block_out[:, begin + i, :] = done[:, i * size_z : (i + 1) * size_z]


def local(
    start_block,
    basis,
    trans_x,
    trans_y,
    trans_z,
    pore_volume,
    shift_table,
    shift_index,
    fault_send,
    fault_recv,
    fault_trans,
    well_cells,
):
    columns, size_x, size_y, size_z = start_block.shape
    devices, slots = fault_send.shape[1:]
    lines = size_x * size_y
    cells = lines * size_z
    total = devices * slots
    sizes = [lax.axis_size(axis) for axis in AXES]
    index_x, index_y, index_z = (lax.axis_index(axis) for axis in AXES)
    full_x, full_y, full_z = size_x * sizes[0], size_y * sizes[1], size_z * sizes[2]
    has_b = tuple(size > 2 for size in sizes)
    dims = (columns, size_x, size_y, size_z, slots)
    rows = columns * slots // LANES

    vmem = pl.BlockSpec(memory_space=pltpu.VMEM)
    params = pltpu.CompilerParams(vmem_limit_bytes=8 * 2**20 + 4096 * total)
    wide_params = pltpu.CompilerParams(vmem_limit_bytes=16 * 2**20 + 4096 * total)
    field_type = jax.ShapeDtypeStruct((columns, lines, size_z), F32)
    x_type = jax.ShapeDtypeStruct((columns, size_y, size_z), F32)
    y_type = jax.ShapeDtypeStruct((size_x, columns, size_z), F32)
    z_type = jax.ShapeDtypeStruct((1, columns * lines), F32)
    face_types = [x_type] * (1 + has_b[0]) + [y_type] * (1 + has_b[1]) + [z_type] * (1 + has_b[2])

    def in_hbm(*values):
        return [pltpu.with_memory_space_constraint(value, pltpu.HBM) for value in values]

    shape2 = (lines, size_z)
    start = start_block.reshape(columns, lines, size_z)
    anywhere = pl.BlockSpec(memory_space=pltpu.HBM)
    trans = [value.reshape(shape2) for value in (trans_x, trans_y, trans_z)]
    row_types = [jax.ShapeDtypeStruct((1, total), kind) for kind in (jnp.int32, jnp.int32, F32)]
    edge_types = [
        jax.ShapeDtypeStruct(shape, F32) for shape in ((size_y, size_z), (size_x, size_z), (1, lines))
    ]
    edge_x, edge_y, edge_z, send, recv, weight = pl.pallas_call(
        functools.partial(edges_kernel, dims),
        out_shape=edge_types + row_types,
        in_specs=[anywhere] * 6,
        out_specs=[vmem] * 6,
        scratch_shapes=[pltpu.VMEM(shape2, F32)] * 3
        + [pltpu.VMEM(fault_send.shape, kind) for kind in (jnp.int32, jnp.int32, F32)]
        + [pltpu.SemaphoreType.DMA((6,))],
        compiler_params=params,
        name="edges",
    )(*in_hbm(*trans, fault_send, fault_recv, fault_trans))
    edges = []
    for axis, edge, more in zip(AXES, (edge_x, edge_y, edge_z), has_b):
        edges += [swap_even(edge, axis)] + ([swap_odd(edge, axis)] if more else [])

    def gather(direction, goes="", source=()):
        sent_rows = devices * (rows + (extra if goes else 0))
        return pl.pallas_call(
            functools.partial(gather_kernel, dims, (extra, goes)),
            out_shape=jax.ShapeDtypeStruct((sent_rows, LANES), F32),
            in_specs=[vmem] * (2 + len(source)),
            out_specs=vmem,
            compiler_params=params,
            cost_estimate=pl.CostEstimate(
                flops=4 * columns * cells * total, bytes_accessed=4 * columns * cells, transcendentals=0
            ),
            name="fault_gather",
        )(direction, send, *source)

    def transfers(faults, faces):
        faces = list(faces)
        came = {}
        for axis, more in zip(AXES, has_b):
            came[axis] = [swap_even(faces.pop(0), axis)] + ([swap_odd(faces.pop(0), axis)] if more else [])
        faults, came["gy"][0] = lax.optimization_barrier((faults, came["gy"][0]))
        return exchange(faults), came["gx"], came["gy"] + came["gz"]

    def stencil(residual, direction, came, solution):
        more = [] if solution is None else [solution]
        return pl.pallas_call(
            functools.partial(stencil_kernel, dims, has_b, solution is None),
            out_shape=[field_type, field_type],
            in_specs=[vmem] * (3 + len(came) + len(more)),
            out_specs=[vmem] * 2,
            input_output_aliases={1: 0, 3 + len(came): 1} if more else {1: 0},
            compiler_params=params,
            cost_estimate=pl.CostEstimate(
                flops=20 * columns * cells, bytes_accessed=12 * columns * cells, transcendentals=0
            ),
            name="stencil",
        )(ops, residual, direction, *came, *more)

    ops, residual, direction, *faces = pl.pallas_call(
        functools.partial(setup_kernel, dims, has_b),
        out_shape=[jax.ShapeDtypeStruct((10, lines, size_z), F32), field_type, field_type] + face_types,
        in_specs=[vmem] * 4 + [anywhere] * 5 + [vmem] * len(edges),
        out_specs=[vmem] * (3 + len(face_types)),
        scratch_shapes=[pltpu.VMEM(shape2, F32)] * 4
        + [pltpu.SemaphoreType.DMA((5,))],
        compiler_params=params,
        name="setup",
    )(
        shift_table.reshape(1, -1), shift_index.reshape(1, 1), recv, weight,
        *in_hbm(*trans, pore_volume.reshape(shape2), start), *edges,
    )
    plane = full_y * full_z
    well_x = well_cells // plane
    well_y = well_cells // full_z % full_y
    well_z = well_cells % full_z
    owned = (
        (well_x // size_x == index_x)
        & (well_y // size_y == index_y)
        & (well_z // size_z == index_z)
    )
    local_cell = (well_x % size_x * size_y + well_y % size_y) * size_z + well_z % size_z
    wells = well_cells.shape[0]
    well_local = jnp.where(owned, local_cell, -1).reshape(1, wells)
    count = basis.shape[0]
    blocks = count // LANES
    early_rows = LANES * (blocks * (blocks + 1) // 2 + -(-blocks // (LANES // wells)))
    extra = -(-early_rows // devices)
    flat_basis_type = pltpu.HBM((count, cells), BF16)
    parts, flat_basis = pl.pallas_call(
        functools.partial(basis_kernel, dims),
        out_shape=[jax.ShapeDtypeStruct((devices * extra, LANES), F32), flat_basis_type],
        in_specs=[vmem, anywhere],
        out_specs=[vmem, anywhere],
        scratch_shapes=[
            pltpu.VMEM((count, lines, size_z), BF16),
            pltpu.VMEM((count, cells), BF16),
            pltpu.VMEM((cells, wells), BF16),
            pltpu.SemaphoreType.DMA((count // 16,)),
            pltpu.SemaphoreType.DMA((count // 16,)),
        ],
        compiler_params=wide_params,
        cost_estimate=pl.CostEstimate(
            flops=2 * count * cells * (count + wells), bytes_accessed=4 * count * cells, transcendentals=0
        ),
        name="basis_gram",
    )(well_local, *in_hbm(basis.reshape(count, lines, size_z)))

    needed = columns * (2 * blocks + 2)
    per_device = 1 << (-(-needed // devices) - 1).bit_length()
    sums_type = jax.ShapeDtypeStruct((devices * per_device, LANES), F32)
    flat_type = jax.ShapeDtypeStruct((columns, cells), F32)
    sigma = 1.0 / 0.9
    weight_now = 1.0 / sigma
    solution = None
    for number in range(TERMS - 1):
        goes = {2: "parts", 3: "sums"}.get(number, "")
        faults = gather(direction, goes, [parts] if goes == "parts" else [table] if goes else [])
        arrived, came, far = transfers(faults, faces)
        residual, solution = stencil(residual, direction, came, solution)
        weight_new = 1.0 / (2.0 * sigma - weight_now)
        last_round = number == TERMS - 2
        body = functools.partial(
            update_kernel, dims, has_b, weight_new * weight_now, 2.0 * weight_new / 0.9,
            last_round, (extra, goes),
        )
        weight_now = weight_new
        scratch = [pltpu.VMEM((columns * lines // 2, 2 * size_z), F32)]
        out_types = [sums_type, flat_type] if last_round else []
        if goes:
            table_rows = extra if goes == "parts" else devices * extra
            out_types.append(jax.ShapeDtypeStruct((table_rows, LANES), F32))
        operands = [ops, residual, direction, recv, weight, arrived, *far]
        aliases = {}
        if last_round:
            operands.append(solution)
        in_specs = [vmem] * len(operands)
        if not last_round:
            aliases[1], aliases[2] = len(out_types), len(out_types) + 1
            out_types += [field_type, field_type] + face_types
        else:
            operands += [well_local, *in_hbm(flat_basis)]
            in_specs += [vmem, anywhere]
            scratch += [
                pltpu.VMEM((columns, lines, size_z), F32),
                pltpu.VMEM((count, cells), BF16),
                pltpu.SemaphoreType.DMA((1,)),
            ]
        outs = pl.pallas_call(
            body,
            out_shape=out_types,
            in_specs=in_specs,
            out_specs=[vmem] * len(out_types),
            scratch_shapes=scratch,
            input_output_aliases=aliases,
            compiler_params=wide_params if last_round else params,
            name="update",
        )(*operands)
        if last_round:
            sums, flat = outs
            break
        if goes:
            table, *outs = outs
        residual, direction, *faces = outs

    mine = exchange(sums).reshape(devices, per_device, LANES).sum(axis=0)
    sums = exchange(jnp.tile(mine, (devices, 1)))

    scale = math.sqrt(full_x * full_y * full_z)
    new_block, first_coeffs, coeffs, well_resp = pl.pallas_call(
        functools.partial(finish_kernel, dims, scale, wells),
        out_shape=[
            field_type,
            jax.ShapeDtypeStruct((columns, count), F32),
            jax.ShapeDtypeStruct((columns, count), F32),
            jax.ShapeDtypeStruct((columns, wells), F32),
        ],
        in_specs=[vmem] * 3 + [anywhere],
        out_specs=[vmem] * 4,
        scratch_shapes=[pltpu.VMEM((count, cells), BF16), pltpu.SemaphoreType.DMA((1,))],
        compiler_params=wide_params,
        name="finish",
    )(sums, table, flat, *in_hbm(flat_basis))
    return new_block.reshape(start_block.shape), first_coeffs.T, coeffs.T, well_resp.T


def solution(mesh):
    in_specs = (
        P(None, "gx", "gy", "gz"),
        P(None, "gx", "gy", "gz"),
        P("gx", "gy", "gz"),
        P("gx", "gy", "gz"),
        P("gx", "gy", "gz"),
        P("gx", "gy", "gz"),
        P(),
        P(),
        P(("gx", "gy", "gz"), None, None),
        P(("gx", "gy", "gz"), None, None),
        P(("gx", "gy", "gz"), None, None),
        P(),
    )
    out_specs = (P(None, "gx", "gy", "gz"), P(), P(), P())
    return jax.shard_map(local, mesh=mesh, in_specs=in_specs, out_specs=out_specs, check_vma=False)
```

```python
import functools
import math

import jax
import jax.numpy as jnp
from jax import lax
from jax.experimental import pallas as pl
from jax.experimental.pallas import tpu as pltpu
from jax.sharding import PartitionSpec as P

TERMS = 8
AXES = ("gx", "gy", "gz")
LANES = 128
BF16 = jnp.bfloat16
F32 = jnp.float32


def swap_even(value, axis):
    size = lax.axis_size(axis)
    pairs = [(i, i ^ 1) for i in range(size) if i ^ 1 < size]
    return lax.ppermute(value, axis, pairs)


def swap_odd(value, axis):
    size = lax.axis_size(axis)
    other = "gy" if axis == "gx" else "gx"
    across = lax.axis_size(other)
    names = (axis, other) if axis == "gx" else (other, axis)

    def number(i, o):
        return i * across + o if axis == "gx" else o * size + i

    pairs = []
    for o in range(across):
        for i in range(size):
            to = (i + 1 if i % 2 else i - 1, o)
            if not 0 <= to[0] < size:
                to = (i, o ^ 1)
            if to[1] < across:
                pairs.append((number(i, o), number(*to)))
    return lax.ppermute(value, names, pairs)


def exchange(value):
    return lax.all_to_all(value, AXES, split_axis=0, concat_axis=0, tiled=True)


def regroup(tile, rows, slots):
    groups = LANES // slots
    columns = tile.shape[0]
    row_group = lax.broadcasted_iota(jnp.int32, tile.shape, 0) // rows
    lane_group = lax.broadcasted_iota(jnp.int32, tile.shape, 1) // slots
    ahead = lax.rem(lane_group - row_group + groups, groups)
    result = tile
    for k in range(1, groups):
        moved = pltpu.roll(tile, k * slots, 1)
        moved = pltpu.roll(moved, columns - k * rows, 0)
        result = jnp.where(ahead == k, moved, result)
    return result


def split_two(value):
    high = value.astype(BF16)
    low = (value - high.astype(F32)).astype(BF16)
    return high, low


def one_hots(cell, lines, size_z):
    half = lines // 2
    total = cell.shape[1]
    line = cell // size_z
    key = line // half * size_z + cell % size_z
    rows = jnp.broadcast_to(line % half, (half, total)) == lax.broadcasted_iota(jnp.int32, (half, total), 0)
    keys = lax.broadcasted_iota(jnp.int32, (2 * size_z, total), 0)
    keys = jnp.where(jnp.broadcast_to(key, (2 * size_z, total)) == keys, 1.0, 0.0).astype(BF16)
    return rows, keys


def nt_dot(left, right):
    return lax.dot_general(left, right, (((1,), (1,)), ((), ())), preferred_element_type=F32)


def even_places():
    return [lax.axis_index(axis) % 2 == 0 for axis in AXES]


def emit_faces(direction_ref, faces_out, dims):
    columns, size_x, size_y, size_z, slots = dims
    lines = size_x * size_y
    x_a, x_b, y_a, y_b, z_a, z_b = faces_out
    even = even_places()
    field = direction_ref[...]
    first_x, last_x = field[:, :size_y, :], field[:, lines - size_y :, :]
    x_a[...] = jnp.where(even[0], last_x, first_x)
    if x_b is not None:
        x_b[...] = jnp.where(even[0], first_x, last_x)
    for i in range(size_x):
        first_y = direction_ref[:, i * size_y, :]
        last_y = direction_ref[:, (i + 1) * size_y - 1, :]
        y_a[i] = jnp.where(even[1], last_y, first_y)
        if y_b is not None:
            y_b[i] = jnp.where(even[1], first_y, last_y)
    both = jnp.concatenate(split_two(field.reshape(columns * lines, size_z)), axis=1)
    row = lax.broadcasted_iota(jnp.int32, (8, size_z), 0)
    lane = lax.broadcasted_iota(jnp.int32, (8, size_z), 1)
    pick = ((row == 0) & (lane == size_z - 1)) | ((row == 1) & (lane == 0))
    pick = jnp.where(pick, 1.0, 0.0).astype(BF16)
    ends = nt_dot(jnp.concatenate([pick, pick], axis=1), both)
    last_z, first_z = ends[0:1, :], ends[1:2, :]
    z_a[...] = jnp.where(even[2], last_z, first_z)
    if z_b is not None:
        z_b[...] = jnp.where(even[2], first_z, last_z)


def gather_kernel(dims, early, *refs):
    extra, goes, parity, begin = early
    direction_ref, send_ref = refs[:2]
    faults_out = refs[-1]
    columns, size_x, size_y, size_z, slots = dims
    lines = size_x * size_y
    rows = columns * slots // LANES
    half = lines // 2
    field = direction_ref[...].astype(BF16)
    field = jnp.concatenate([field[:, :half, :], field[:, half:, :]], axis=2).reshape(columns * half, 2 * size_z)
    for i in range(send_ref.shape[1] // slots if goes else 0):
        at = i * (rows + extra) + rows
        if goes == "sums":
            source = refs[2][parity[i] * extra : (parity[i] + 1) * extra, :]
        else:
            own = slice(begin + i * extra, begin + (i + 1) * extra)
            source = refs[2][own, :] + refs[3][own, :]
        faults_out[at : at + extra, :] = source
    total = send_ref.shape[1]
    width = min(256, total)
    for start in range(0, total, width):
        hot_row, hot_key = one_hots(send_ref[:, start : start + width], lines, size_z)
        found = jnp.dot(field, hot_key, preferred_element_type=F32)
        found = jnp.where(hot_row[None], found.reshape(columns, half, width), 0.0)
        values = jnp.sum(found, axis=1)
        for j in range(0, width, LANES):
            tile = regroup(values[:, j : j + LANES], rows, slots)
            device = (start + j) // slots
            if not goes:
                faults_out[device * rows : device * rows + columns, :] = tile
                continue
            for i in range(LANES // slots):
                at = (device + i) * (rows + extra)
                faults_out[at : at + rows, :] = tile[i * rows : (i + 1) * rows]


def start_copies(pairs, sem):
    copies = [pltpu.make_async_copy(source, target, sem.at[i]) for i, (source, target) in enumerate(pairs)]
    for copy in copies:
        copy.start()
    return copies


def edges_kernel(dims, *refs):
    columns, size_x, size_y, size_z, slots = dims
    ex_out, ey_out, ez_out = refs[6:9]
    tables_out, held, sem = refs[9:12], refs[12:18], refs[18]
    copies = start_copies(zip(refs[:6], held), sem)
    for copy in copies:
        copy.wait()
    tx, ty, tz = held[:3]
    lines = size_x * size_y
    ex_out[...] = tx[lines - size_y :, :]
    for i in range(size_x):
        ey_out[i : i + 1, :] = ty[(i + 1) * size_y - 1 : (i + 1) * size_y, :]
    ez_out[...] = tz[...].T[size_z - 1 : size_z, :]
    for table, out in zip(held[3:], tables_out):
        value = table[0]
        out[...] = jnp.concatenate([value[i : i + 1, :] for i in range(value.shape[0])], axis=1)


def setup_kernel(dims, has_b, *refs):
    shifts_ref, which_ref, recv_ref, weight_ref = refs[:4]
    sources = refs[4:9]
    faces = 3 + sum(has_b)
    edges = unpack_faces(refs[9 : 9 + faces], has_b)
    ops_ref, residual_ref, direction_ref = refs[9 + faces : 12 + faces]
    faces_out = unpack_faces(refs[12 + faces : 12 + 2 * faces], has_b)
    held, sem = refs[12 + 2 * faces : -1], refs[-1]
    tx_ref, ty_ref, tz_ref, pore_ref = held
    copies = start_copies(zip(sources, held + (residual_ref,)), sem)
    columns, size_x, size_y, size_z, slots = dims
    lines = size_x * size_y
    line = lax.broadcasted_iota(jnp.int32, (lines, size_z), 0)
    lane = lax.broadcasted_iota(jnp.int32, (lines, size_z), 1)
    last = [lax.axis_index(axis) == lax.axis_size(axis) - 1 for axis in AXES]
    even = even_places()
    in_y = line % size_y
    for copy in copies[:-1]:
        copy.wait()
    upper_x = jnp.where((line >= lines - size_y) & last[0], 0.0, tx_ref[...])
    upper_y = jnp.where((in_y == size_y - 1) & last[1], 0.0, ty_ref[...])
    upper_z = jnp.where((lane == size_z - 1) & last[2], 0.0, tz_ref[...])
    behind = []
    for i in range(3):
        came = edges[2 * i][...]
        if edges[2 * i + 1] is not None:
            came = jnp.where(even[i], edges[2 * i + 1][...], came)
        behind.append(jnp.where(lax.axis_index(AXES[i]) == 0, 0.0, came))
    lower_x = jnp.concatenate([behind[0], upper_x[: lines - size_y]], axis=0)
    edge_y = jnp.concatenate(
        [jnp.broadcast_to(behind[1][i : i + 1, :], (size_y, size_z)) for i in range(size_x)], axis=0
    )
    lower_y = jnp.where(in_y == 0, edge_y, pltpu.roll(upper_y, 1, 0))
    lower_z = jnp.where(lane == 0, jnp.broadcast_to(behind[2], (8, lines)).T[:, 0:1], pltpu.roll(upper_z, 1, 1))
    total = recv_ref.shape[1]
    cell = recv_ref[...]
    hot_line = jnp.broadcast_to(cell // size_z, (lines, total)) == lax.broadcasted_iota(
        jnp.int32, (lines, total), 0
    )
    hot_lane = jnp.broadcast_to(cell % size_z, (size_z, total)) == lax.broadcasted_iota(
        jnp.int32, (size_z, total), 0
    )
    weight = weight_ref[...]
    high = weight.astype(BF16).astype(F32)
    middle = (weight - high).astype(BF16).astype(F32)
    low = weight - high - middle
    parts = [jnp.where(hot_line, part, 0.0).astype(BF16) for part in (high, middle, low)]
    summed = nt_dot(jnp.concatenate(parts, axis=0), jnp.where(hot_lane, 1.0, 0.0).astype(BF16))
    fault_diag = summed[:lines] + summed[lines : 2 * lines] + summed[2 * lines :]
    number = lax.broadcasted_iota(jnp.int32, shifts_ref.shape, 1)
    shift = jnp.sum(jnp.where(number == which_ref[...], shifts_ref[...], 0.0), axis=1, keepdims=True)
    diagonal = (
        upper_x + lower_x + upper_y + lower_y + upper_z + lower_z + shift * pore_ref[...] + fault_diag
    )
    inverse = 1.0 / diagonal
    inner_y = jnp.where(in_y == size_y - 1, 0.0, upper_y), jnp.where(in_y == 0, 0.0, lower_y)
    inner_z = jnp.where(lane == size_z - 1, 0.0, upper_z), jnp.where(lane == 0, 0.0, lower_z)
    face_y = upper_y - inner_y[0] + (lower_y - inner_y[1])
    face_z = upper_z - inner_z[0] + (lower_z - inner_z[1])
    for i, value in enumerate((upper_x, lower_x, *inner_y, *inner_z, diagonal, inverse, face_y, face_z)):
        ops_ref[i] = value
    copies[-1].wait()
    for c in range(columns):
        direction_ref[c] = residual_ref[c] * inverse
    emit_faces(direction_ref, faces_out, dims)


def unpack_faces(refs, has_b):
    refs = list(refs)
    faces = []
    for more in has_b:
        faces += [refs.pop(0), refs.pop(0) if more else None]
    return faces


def stencil_kernel(dims, has_b, first_round, *refs):
    refs = list(refs)
    columns, size_x, size_y, size_z, slots = dims
    ops_ref, residual_ref, direction_ref = refs[:3]
    refs = refs[3:]
    solution_out, residual_out = refs.pop(), refs.pop()
    solution_ref = None if first_round else refs.pop()
    xa_ref, xb_ref = refs[0], refs[-1]
    lines = size_x * size_y
    even = lax.axis_index(AXES[0]) % 2 == 0
    for c in range(columns):
        value = direction_ref[c]
        x_low = jnp.where(even, xb_ref[c], xa_ref[c])
        x_high = jnp.where(even, xa_ref[c], xb_ref[c])
        beside = ops_ref[0] * jnp.concatenate([value[size_y:], x_high], axis=0)
        beside += ops_ref[1] * jnp.concatenate([x_low, value[: lines - size_y]], axis=0)
        beside += ops_ref[2] * pltpu.roll(value, lines - 1, 0)
        beside += ops_ref[3] * pltpu.roll(value, 1, 0)
        beside += ops_ref[4] * pltpu.roll(value, size_z - 1, 1)
        beside += ops_ref[5] * pltpu.roll(value, 1, 1)
        residual_out[c] = residual_ref[c] - (ops_ref[6] * value - beside)
        solution_out[c] = value if first_round else solution_ref[c] + value


def update_kernel(dims, has_b, keep, gain, last_round, early, *refs):
    refs = list(refs)
    columns, size_x, size_y, size_z, slots = dims
    extra, comes, parity = early
    ops_ref, residual_ref, direction_ref, recv_ref, weight_ref, arrived_ref = refs[:6]
    refs = refs[6:]
    ya_ref, yb_ref, za_ref, zb_ref = unpack_faces(refs[: 2 + has_b[1] + has_b[2]], has_b[1:])
    refs = refs[2 + has_b[1] + has_b[2] :]
    yb_ref = ya_ref if yb_ref is None else yb_ref
    zb_ref = za_ref if zb_ref is None else zb_ref
    if last_round:
        solution_ref, well_ref, *refs = refs
        blocks = (len(refs) - 5) // 2
        sources, (sums_out, flat_out, landed_ref, solution_out) = refs[:blocks], refs[blocks : blocks + 4]
        basis_refs, sem = refs[blocks + 4 : -1], refs[-1]
        fetches = start_copies(zip(sources, basis_refs), sem)
    else:
        landed_ref = refs.pop()
    table_out = refs.pop(0) if comes else None
    if not last_round:
        residual_out, direction_out = refs[:2]
        faces_out = unpack_faces(refs[2:], has_b)
    lines = size_x * size_y
    rows = columns * slots // LANES
    total = recv_ref.shape[1]
    half = lines // 2
    hot_row, hot_key = one_hots(recv_ref[...], lines, size_z)
    hot_row = jnp.where(hot_row, 1.0, 0.0).astype(BF16)
    tiles = []
    devices = total // slots
    if comes:
        per_device = rows + extra
        for i in range(devices):
            landed_ref[i * rows : (i + 1) * rows, :LANES] = arrived_ref[i * per_device : i * per_device + rows, :]
        source_ref = landed_ref
    else:
        source_ref = arrived_ref
    for j in range(total // LANES):
        tiles.append(regroup(source_ref[j * columns : (j + 1) * columns, :LANES], rows, slots))
    if comes == "parts":
        added = [jnp.zeros((extra, LANES), F32)] * 2
        for i in range(devices):
            at = i * per_device + rows
            added[parity[i]] = added[parity[i]] + arrived_ref[at : at + extra, :]
        table_out[:extra, :], table_out[extra:, :] = added
    if comes == "sums":
        for i in range(devices):
            at = i * per_device + rows
            table_out[i * extra : (i + 1) * extra, :] = arrived_ref[at : at + extra, :]
    weighted = (jnp.concatenate(tiles, axis=1) * weight_ref[...]).astype(BF16)
    spread = weighted[:, None, :] * hot_row[None, :, :]
    landed_ref[...] = nt_dot(spread.reshape(columns * half, total), hot_key)
    even = even_places()
    in_slab = lax.broadcasted_iota(jnp.int32, (size_y, size_z), 0)
    lane = lax.broadcasted_iota(jnp.int32, (lines, size_z), 1)
    z_a, z_b = za_ref[...], zb_ref[...]
    z_rows = [jnp.where(even[2], z_b, z_a), jnp.where(even[2], z_a, z_b), jnp.zeros((6, columns * lines), F32)]
    z_cols = jnp.concatenate(z_rows, axis=0).T
    for c in range(columns):
        landed = landed_ref[c * half : (c + 1) * half, :]
        left = residual_ref[c] + jnp.concatenate([landed[:, :size_z], landed[:, size_z:]], axis=0)
        beside_y = []
        for i in range(size_x):
            y_a, y_b = ya_ref[i, c : c + 1, :], yb_ref[i, c : c + 1, :]
            y_low, y_high = jnp.where(even[1], y_b, y_a), jnp.where(even[1], y_a, y_b)
            beside_y.append(jnp.where(in_slab < size_y // 2, y_low, y_high))
        z_low = z_cols[c * lines : (c + 1) * lines, 0:1]
        z_high = z_cols[c * lines : (c + 1) * lines, 1:2]
        left = left + ops_ref[8] * jnp.concatenate(beside_y, axis=0)
        left = left + ops_ref[9] * jnp.where(lane < size_z // 2, z_low, z_high)
        after = keep * direction_ref[c] + gain * (left * ops_ref[7])
        if last_round:
            solution_out[c] = solution_ref[c] + after
        else:
            residual_out[c] = left
            direction_out[c] = after
    if not last_round:
        emit_faces(direction_out, faces_out, dims)
    else:
        for copy in fetches:
            copy.wait()
        sums_of(dims, solution_out, basis_refs, well_ref, flat_out, sums_out)


def basis_kernel(dims, piece, blocks, *refs):
    well_ref, source_ref = refs[:2]
    others = refs[2 : 2 + piece]
    last = piece == blocks - 1
    before = refs[2 + piece : 2 + 3 * piece] if last else ()
    refs = refs[2 + piece + len(before) :]
    flat_target, gram_out, wells_out, basis_ref, hot_ref, flat_out, sem, out_sem = refs[:8]
    held = refs[8 : 8 + piece]
    columns, size_x, size_y, size_z, slots = dims
    lines = size_x * size_y
    wells = well_ref.shape[1]
    side = 16
    groups = [pl.ds(first, side) for first in range(0, LANES, side)]
    copies = [
        pltpu.make_async_copy(source_ref.at[pl.ds(piece * LANES + i * side, side)], basis_ref.at[g], sem.at[i])
        for i, g in enumerate(groups)
    ]
    for copy in copies:
        copy.start()
    fetches = start_copies(zip(others, held), refs[8 + piece]) if piece else []
    stores = []
    row = lax.broadcasted_iota(jnp.int32, (side * side, side * side), 0)
    lane = lax.broadcasted_iota(jnp.int32, (side * side, side * side), 1)
    turn = jnp.where((row % side == lane // side) & (row // side == lane % side), 1.0, 0.0).astype(BF16)
    cell = well_ref[...]
    lane_of = jnp.broadcast_to(lax.rem(cell + size_z, size_z), (size_z, wells))
    lane_of = lane_of == lax.broadcasted_iota(jnp.int32, (size_z, wells), 0)
    line_of = jnp.broadcast_to(jnp.where(cell < 0, -1, cell // size_z), (size_z, wells))
    for line in range(lines):
        hot = jnp.where(lane_of & (line_of == line), 1.0, 0.0)
        hot_ref[line * size_z : (line + 1) * size_z, :] = hot.astype(BF16)
    for index in range(0, len(groups), 2):
        copies[index].wait()
        copies[index + 1].wait()
        first = index * side
        for begin in range(0, lines, side):
            tile = [
                basis_ref[at : at + side, begin : begin + side, :].reshape(side * side, size_z)
                for at in (first, first + side)
            ]
            tile = jnp.dot(turn, jnp.concatenate(tile, axis=1), preferred_element_type=F32).astype(BF16)
            for i in range(side):
                lanes = slice((begin + i) * size_z, (begin + i + 1) * size_z)
                flat_out[first : first + side, lanes] = tile[i * side : (i + 1) * side, :size_z]
                flat_out[first + side : first + 2 * side, lanes] = tile[i * side : (i + 1) * side, size_z:]
        pair = pl.ds(first, 2 * side)
        stores.append(pltpu.make_async_copy(flat_out.at[pair], flat_target.at[pair], out_sem.at[index // 2]))
        stores[-1].start()
    flat = flat_out[...]
    for copy in fetches:
        copy.wait()
    for i, other in enumerate(held + (flat_out,)):
        product = nt_dot(other[...], flat)
        if last:
            place = (piece * (piece + 1) // 2 + i) * LANES
            refs[-1][place : place + LANES, :] = product
        else:
            gram_out[i * LANES : (i + 1) * LANES, :] = product
    at_wells = jnp.dot(flat, hot_ref[...], preferred_element_type=F32)
    if last:
        full_ref, beside, place = refs[-1], LANES // wells, 0
        for i in range(piece):
            full_ref[place : place + (i + 1) * LANES, :] = before[2 * i][...]
            place += (i + 1) * LANES
        place += (piece + 1) * LANES
        full_ref[place:, :] = jnp.zeros((full_ref.shape[0] - place, LANES), F32)
        for i in range(blocks):
            value = at_wells if i == piece else before[2 * i + 1][...]
            at, lanes = place + i // beside * LANES, slice(i % beside * wells, (i % beside + 1) * wells)
            full_ref[at : at + LANES, lanes] = value
        half, even = full_ref.shape[0] // 2, even_places()[1]
        gram_out[...] = jnp.where(even, full_ref[:half, :], full_ref[half:, :])
        wells_out[...] = jnp.where(even, full_ref[half:, :], full_ref[:half, :])
    else:
        wells_out[...] = at_wells
    for store in stores:
        store.wait()


def split_three(value):
    high = value.astype(BF16)
    left = value - high.astype(F32)
    middle = left.astype(BF16)
    return high, middle, (left - middle.astype(F32)).astype(BF16)


def sums_of(dims, solution_ref, basis_refs, well_ref, flat_out, sums_out):
    columns, size_x, size_y, size_z, slots = dims
    lines = size_x * size_y
    wells = well_ref.shape[1]
    for line in range(lines):
        flat_out[:, line * size_z : (line + 1) * size_z] = solution_ref[:, line, :]
    parts = jnp.concatenate(split_three(flat_out[...]), axis=0)
    with_basis = jnp.concatenate([nt_dot(parts, ref[...]) for ref in basis_refs], axis=1)
    with_self = nt_dot(parts, parts)
    sums_out[...] = jnp.zeros(sums_out.shape, F32)
    blocks = len(basis_refs)
    first = with_basis[:columns]
    beyond = with_basis[columns : 2 * columns] + with_basis[2 * columns :]
    for i in range(blocks):
        lanes = slice(i * LANES, (i + 1) * LANES)
        sums_out[i * columns : (i + 1) * columns, :] = first[:, lanes]
        sums_out[(blocks + i) * columns : (blocks + i + 1) * columns, :] = beyond[:, lanes]
    rows = with_self[:columns] + with_self[columns : 2 * columns] + with_self[2 * columns :]
    square = rows[:, :columns] + rows[:, columns : 2 * columns] + rows[:, 2 * columns :]
    at = 2 * blocks * columns
    sums_out[at : at + columns, :columns] = square
    both = jnp.concatenate(split_two(solution_ref[...].reshape(columns * lines, size_z)), axis=1)
    cell = well_ref[...]
    lane_of = jnp.broadcast_to(lax.rem(cell + size_z, size_z), (size_z, wells))
    hot = lane_of == lax.broadcasted_iota(jnp.int32, (size_z, wells), 0)
    hot = jnp.where(hot, 1.0, 0.0).astype(BF16)
    found = jnp.dot(both, jnp.concatenate([hot, hot], axis=0), preferred_element_type=F32)
    line_of = jnp.broadcast_to(jnp.where(cell < 0, -1, cell // size_z), (lines, wells))
    mask = line_of == lax.broadcasted_iota(jnp.int32, (lines, wells), 0)
    found = jnp.where(mask[None], found.reshape(columns, lines, wells), 0.0)
    at += columns
    sums_out[at : at + columns, :wells] = jnp.sum(found, axis=1)


def exact_dot(left, right, transposed=False):
    axes = ((1,), (1,)) if transposed else ((1,), (0,))
    return lax.dot_general(
        left, right, (axes, ((), ())), precision=lax.Precision.HIGHEST, preferred_element_type=F32
    )


def finish_kernel(
    dims, scale, wells, blocks, groups, sums_ref, flat_ref, *refs
):
    mine, other = ([ref[...] for ref in refs[i * groups : (i + 1) * groups]] for i in range(2))
    mine, other, refs = jnp.concatenate(mine, axis=0), jnp.concatenate(other, axis=0), refs[2 * groups :]
    even = even_places()[1]
    table = [jnp.where(even, mine, other), jnp.where(even, other, mine)]
    table = jnp.concatenate(table, axis=0)
    block_out, first_out, coeffs_out, wells_out = refs[blocks : blocks + 4]
    basis_refs = refs[blocks + 4 : -1]
    fetches = start_copies(zip(refs[:blocks], basis_refs), refs[-1])
    columns, size_x, size_y, size_z, slots = dims
    lines = size_x * size_y
    pieces, at = {}, 0
    for i in range(blocks):
        for j in range(i + 1):
            pieces[j, i] = table[at : at + LANES, :]
            pieces[i, j] = pieces[j, i] if i == j else pieces[j, i].T
            at += LANES
    basis_gram = jnp.concatenate(
        [jnp.concatenate([pieces[i, j] for j in range(blocks)], axis=1) for i in range(blocks)], axis=0
    )
    beside = LANES // wells
    wells_basis = []
    for i in range(blocks):
        place = at + i // beside * LANES
        wells_basis.append(table[place : place + LANES, i % beside * wells : (i % beside + 1) * wells])
    wells_basis = jnp.concatenate(wells_basis, axis=0)

    def block(i):
        return sums_ref[i * columns : (i + 1) * columns, :]

    first = jnp.concatenate([block(i) for i in range(blocks)], axis=1)
    beyond = jnp.concatenate([block(blocks + i) for i in range(blocks)], axis=1)
    full = first + beyond
    square = block(2 * blocks)[:, :columns]
    at_wells = block(2 * blocks + 1)[:, :wells]
    first_round = first.astype(BF16)
    second = full - exact_dot(first_round.astype(F32), basis_gram)
    second_round = second.astype(BF16)
    taken = first_round.astype(F32) + second_round.astype(F32)
    half = full - 0.5 * exact_dot(taken, basis_gram)
    cross = exact_dot(taken, half, transposed=True)
    gram = square - cross - cross.T
    rest_wells = at_wells - exact_dot(taken, wells_basis)
    first_out[...] = first
    coeffs_out[...] = first + second
    row = lax.broadcasted_iota(jnp.int32, (columns, columns), 0)
    lane = lax.broadcasted_iota(jnp.int32, (columns, columns), 1)
    left = gram
    right = jnp.where(row == lane, 1.0, 0.0)
    below = lax.broadcasted_iota(jnp.int32, (columns, 1), 0)
    for k in range(columns - 1):
        factor = jnp.where(below > k, left[:, k : k + 1] / left[k : k + 1, k : k + 1], 0.0)
        right = right - factor * right[k : k + 1, :]
        left = left - factor * left[k : k + 1, :]
    pivots = jnp.sum(jnp.where(row == lane, left, 0.0), axis=1, keepdims=True)
    inverse = right * (scale / jnp.sqrt(pivots))
    wells_out[...] = exact_dot(inverse, rest_wells)
    high, low = split_two(inverse)
    factors = jnp.concatenate([high, high, low], axis=1)
    for copy in fetches:
        copy.wait()
    rounds = jnp.concatenate([first_round, second_round], axis=0)
    step = min(8, lines)
    for begin in range(0, lines, step):
        lanes = slice(begin * size_z, (begin + step) * size_z)
        basis_part = jnp.concatenate([ref[:, lanes] for ref in basis_refs], axis=0)
        spans = jnp.dot(rounds, basis_part, preferred_element_type=F32)
        rest = flat_ref[:, lanes] - spans[:columns] - spans[columns:]
        rest_high, rest_low = split_two(rest)
        stacked = jnp.concatenate([rest_high, rest_low, rest_high], axis=0)
        done = jnp.dot(factors, stacked, preferred_element_type=F32)
        for i in range(step):
            block_out[:, begin + i, :] = done[:, i * size_z : (i + 1) * size_z]


def local(
    start_block,
    basis,
    trans_x,
    trans_y,
    trans_z,
    pore_volume,
    shift_table,
    shift_index,
    fault_send,
    fault_recv,
    fault_trans,
    well_cells,
):
    columns, size_x, size_y, size_z = start_block.shape
    devices, slots = fault_send.shape[1:]
    lines = size_x * size_y
    cells = lines * size_z
    total = devices * slots
    sizes = [lax.axis_size(axis) for axis in AXES]
    index_x, index_y, index_z = (lax.axis_index(axis) for axis in AXES)
    full_x, full_y, full_z = size_x * sizes[0], size_y * sizes[1], size_z * sizes[2]
    has_b = tuple(size > 2 for size in sizes)
    dims = (columns, size_x, size_y, size_z, slots)
    rows = columns * slots // LANES

    vmem = pl.BlockSpec(memory_space=pltpu.VMEM)
    params = pltpu.CompilerParams(vmem_limit_bytes=8 * 2**20 + 4096 * total)
    wide_params = pltpu.CompilerParams(vmem_limit_bytes=16 * 2**20 + 4096 * total)
    field_type = jax.ShapeDtypeStruct((columns, lines, size_z), F32)
    x_type = jax.ShapeDtypeStruct((columns, size_y, size_z), F32)
    y_type = jax.ShapeDtypeStruct((size_x, columns, size_z), F32)
    z_type = jax.ShapeDtypeStruct((1, columns * lines), F32)
    face_types = [x_type] * (1 + has_b[0]) + [y_type] * (1 + has_b[1]) + [z_type] * (1 + has_b[2])

    def in_hbm(*values):
        return [pltpu.with_memory_space_constraint(value, pltpu.HBM) for value in values]

    shape2 = (lines, size_z)
    start = start_block.reshape(columns, lines, size_z)
    anywhere = pl.BlockSpec(memory_space=pltpu.HBM)
    trans = [value.reshape(shape2) for value in (trans_x, trans_y, trans_z)]
    row_types = [jax.ShapeDtypeStruct((1, total), kind) for kind in (jnp.int32, jnp.int32, F32)]
    edge_types = [
        jax.ShapeDtypeStruct(shape, F32) for shape in ((size_y, size_z), (size_x, size_z), (1, lines))
    ]
    edge_x, edge_y, edge_z, send, recv, weight = pl.pallas_call(
        functools.partial(edges_kernel, dims),
        out_shape=edge_types + row_types,
        in_specs=[anywhere] * 6,
        out_specs=[vmem] * 6,
        scratch_shapes=[pltpu.VMEM(shape2, F32)] * 3
        + [pltpu.VMEM(fault_send.shape, kind) for kind in (jnp.int32, jnp.int32, F32)]
        + [pltpu.SemaphoreType.DMA((6,))],
        compiler_params=params,
        name="edges",
    )(*in_hbm(*trans, fault_send, fault_recv, fault_trans))
    edges = []
    for axis, edge, more in zip(AXES, (edge_x, edge_y, edge_z), has_b):
        edges += [swap_even(edge, axis)] + ([swap_odd(edge, axis)] if more else [])

    plane = full_y * full_z
    well_x = well_cells // plane
    well_y = well_cells // full_z % full_y
    well_z = well_cells % full_z
    owned = (
        (well_x // size_x == index_x)
        & (well_y // size_y == index_y)
        & (well_z // size_z == index_z)
    )
    local_cell = (well_x % size_x * size_y + well_y % size_y) * size_z + well_z % size_z
    wells = well_cells.shape[0]
    well_local = jnp.where(owned, local_cell, -1).reshape(1, wells)
    count = basis.shape[0]
    blocks = count // LANES
    early_rows = LANES * (blocks * (blocks + 1) // 2 + -(-blocks // (LANES // wells)))
    groups = 2
    extra = -(-early_rows // (2 * groups * devices))
    half_rows = groups * devices * extra
    parity = [i // sizes[2] % sizes[1] % 2 for i in range(devices)]
    flats, parts = [], []
    for piece in range(blocks):
        last = piece == blocks - 1
        shapes = [(half_rows, LANES)] * 2 if last else [((piece + 1) * LANES, LANES), (LANES, wells)]
        before = parts if last else []
        flat_piece, *part = pl.pallas_call(
            functools.partial(basis_kernel, dims, piece, blocks),
            out_shape=[pltpu.HBM((LANES, cells), BF16)] + [jax.ShapeDtypeStruct(shape, F32) for shape in shapes],
            in_specs=[vmem] + [anywhere] * (1 + piece) + [vmem] * len(before),
            out_specs=[anywhere, vmem, vmem],
            scratch_shapes=[
                pltpu.VMEM((LANES, lines, size_z), BF16),
                pltpu.VMEM((cells, wells), BF16),
                pltpu.VMEM((LANES, cells), BF16),
                pltpu.SemaphoreType.DMA((LANES // 16,)),
                pltpu.SemaphoreType.DMA((LANES // 32,)),
            ]
            + [pltpu.VMEM((LANES, cells), BF16)] * piece
            + [pltpu.SemaphoreType.DMA((max(piece, 1),))]
            + [pltpu.VMEM((2 * half_rows, LANES), F32)] * last,
            compiler_params=wide_params,
            cost_estimate=pl.CostEstimate(
                flops=2 * LANES * cells * ((piece + 1) * LANES + wells),
                bytes_accessed=4 * LANES * cells,
                transcendentals=0,
            ),
            name="basis_gram",
        )(well_local, *in_hbm(basis.reshape(count, lines, size_z), *flats), *before)
        flats.append(flat_piece)
        if not piece:
            part[0], *edges = lax.optimization_barrier((part[0], *edges))
        parts += part

    keep_parts, give_parts = parts[-2:]

    def gather(direction, goes, source, group):
        sent_rows = devices * (rows + (extra if goes else 0))
        return pl.pallas_call(
            functools.partial(gather_kernel, dims, (extra, goes, parity, group * devices * extra)),
            out_shape=jax.ShapeDtypeStruct((sent_rows, LANES), F32),
            in_specs=[vmem] * (2 + len(source)),
            out_specs=vmem,
            compiler_params=params,
            cost_estimate=pl.CostEstimate(
                flops=4 * columns * cells * total, bytes_accessed=4 * columns * cells, transcendentals=0
            ),
            name="fault_gather",
        )(direction, send, *source)

    def transfers(faults, faces):
        faces = list(faces)
        came = {}
        for axis, more in zip(AXES, has_b):
            came[axis] = [swap_even(faces.pop(0), axis)] + ([swap_odd(faces.pop(0), axis)] if more else [])
        faults, came["gy"][0] = lax.optimization_barrier((faults, came["gy"][0]))
        return exchange(faults), came["gx"], came["gy"] + came["gz"]

    def stencil(residual, direction, came, solution):
        more = [] if solution is None else [solution]
        return pl.pallas_call(
            functools.partial(stencil_kernel, dims, has_b, solution is None),
            out_shape=[field_type, field_type],
            in_specs=[vmem] * (3 + len(came) + len(more)),
            out_specs=[vmem] * 2,
            input_output_aliases={1: 0, 3 + len(came): 1} if more else {1: 0},
            compiler_params=params,
            cost_estimate=pl.CostEstimate(
                flops=20 * columns * cells, bytes_accessed=12 * columns * cells, transcendentals=0
            ),
            name="stencil",
        )(ops, residual, direction, *came, *more)

    ops, residual, direction, *faces = pl.pallas_call(
        functools.partial(setup_kernel, dims, has_b),
        out_shape=[jax.ShapeDtypeStruct((10, lines, size_z), F32), field_type, field_type] + face_types,
        in_specs=[vmem] * 4 + [anywhere] * 5 + [vmem] * len(edges),
        out_specs=[vmem] * (3 + len(face_types)),
        scratch_shapes=[pltpu.VMEM(shape2, F32)] * 4
        + [pltpu.SemaphoreType.DMA((5,))],
        compiler_params=params,
        name="setup",
    )(
        shift_table.reshape(1, -1), shift_index.reshape(1, 1), recv, weight,
        *in_hbm(*trans, pore_volume.reshape(shape2), start), *edges,
    )
    needed = columns * (2 * blocks + 2)
    per_device = 1 << (-(-needed // devices) - 1).bit_length()
    sums_type = jax.ShapeDtypeStruct((devices * per_device, LANES), F32)
    flat_type = jax.ShapeDtypeStruct((columns, cells), F32)
    sigma = 1.0 / 0.9
    weight_now = 1.0 / sigma
    solution = None
    tables = {}
    came_parts = swap_even(give_parts, "gy")
    for number in range(TERMS - 1):
        goes = ("", "parts", "sums", "")[number // 2]
        group = number % groups
        source = {"parts": [keep_parts, came_parts], "sums": [tables.get(group)]}.get(goes, [])
        faults = gather(direction, goes, source, group)
        arrived, came, far = transfers(faults, faces)
        residual, solution = stencil(residual, direction, came, solution)
        weight_new = 1.0 / (2.0 * sigma - weight_now)
        last_round = number == TERMS - 2
        body = functools.partial(
            update_kernel, dims, has_b, weight_new * weight_now, 2.0 * weight_new / 0.9,
            last_round, (extra, goes, parity),
        )
        weight_now = weight_new
        scratch = [pltpu.VMEM((columns * lines // 2, 2 * size_z), F32)]
        out_types = [sums_type, flat_type] if last_round else []
        if goes:
            table_rows = 2 * extra if goes == "parts" else devices * extra
            out_types.append(jax.ShapeDtypeStruct((table_rows, LANES), F32))
        operands = [ops, residual, direction, recv, weight, arrived, *far]
        aliases = {}
        if last_round:
            operands.append(solution)
        in_specs = [vmem] * len(operands)
        if not last_round:
            aliases[1], aliases[2] = len(out_types), len(out_types) + 1
            out_types += [field_type, field_type] + face_types
        else:
            operands += [well_local, *in_hbm(*flats)]
            in_specs += [vmem] + [anywhere] * blocks
            scratch.append(pltpu.VMEM((columns, lines, size_z), F32))
            scratch += [pltpu.VMEM((LANES, cells), BF16)] * blocks + [pltpu.SemaphoreType.DMA((blocks,))]
        outs = pl.pallas_call(
            body,
            out_shape=out_types,
            in_specs=in_specs,
            out_specs=[vmem] * len(out_types),
            scratch_shapes=scratch,
            input_output_aliases=aliases,
            compiler_params=wide_params if last_round else params,
            name="update",
        )(*operands)
        if last_round:
            sums, flat = outs
            break
        if goes:
            table, *outs = outs
            tables[group] = table
        residual, direction, *faces = outs

    mine = exchange(sums).reshape(devices, per_device, LANES).sum(axis=0)
    sums = exchange(jnp.tile(mine, (devices, 1)))

    mine = [tables[group] for group in range(groups)]
    scale = math.sqrt(full_x * full_y * full_z)
    new_block, first_coeffs, coeffs, well_resp = pl.pallas_call(
        functools.partial(finish_kernel, dims, scale, wells, blocks, groups),
        out_shape=[
            field_type,
            jax.ShapeDtypeStruct((columns, count), F32),
            jax.ShapeDtypeStruct((columns, count), F32),
            jax.ShapeDtypeStruct((columns, wells), F32),
        ],
        in_specs=[vmem] * (2 + 2 * groups) + [anywhere] * blocks,
        out_specs=[vmem] * 4,
        scratch_shapes=[pltpu.VMEM((LANES, cells), BF16)] * blocks + [pltpu.SemaphoreType.DMA((blocks,))],
        compiler_params=wide_params,
        name="finish",
    )(sums, flat, *mine, *[swap_even(table, "gy") for table in mine], *in_hbm(*flats))
    return new_block.reshape(start_block.shape), first_coeffs.T, coeffs.T, well_resp.T


def solution(mesh):
    in_specs = (
        P(None, "gx", "gy", "gz"),
        P(None, "gx", "gy", "gz"),
        P("gx", "gy", "gz"),
        P("gx", "gy", "gz"),
        P("gx", "gy", "gz"),
        P("gx", "gy", "gz"),
        P(),
        P(),
        P(("gx", "gy", "gz"), None, None),
        P(("gx", "gy", "gz"), None, None),
        P(("gx", "gy", "gz"), None, None),
        P(),
    )
    out_specs = (P(None, "gx", "gy", "gz"), P(), P(), P())
    return jax.shard_map(local, mesh=mesh, in_specs=in_specs, out_specs=out_specs, check_vma=False)
```

```python
import functools
import math

import jax
import jax.numpy as jnp
from jax import lax
from jax.experimental import pallas as pl
from jax.experimental.pallas import tpu as pltpu
from jax.sharding import PartitionSpec as P

TERMS = 8
AXES = ("gx", "gy", "gz")
LANES = 128
BF16 = jnp.bfloat16
F32 = jnp.float32


def swap_even(value, axis):
    size = lax.axis_size(axis)
    pairs = [(i, i ^ 1) for i in range(size) if i ^ 1 < size]
    return lax.ppermute(value, axis, pairs)


def swap_odd(value, axis):
    size = lax.axis_size(axis)
    other = "gy" if axis == "gx" else "gx"
    across = lax.axis_size(other)
    names = (axis, other) if axis == "gx" else (other, axis)

    def number(i, o):
        return i * across + o if axis == "gx" else o * size + i

    pairs = []
    for o in range(across):
        for i in range(size):
            to = (i + 1 if i % 2 else i - 1, o)
            if not 0 <= to[0] < size:
                to = (i, o ^ 1)
            if to[1] < across:
                pairs.append((number(i, o), number(*to)))
    return lax.ppermute(value, names, pairs)


def exchange(value):
    return lax.all_to_all(value, AXES, split_axis=0, concat_axis=0, tiled=True)


def regroup(tile, rows, slots):
    groups = LANES // slots
    columns = tile.shape[0]
    row_group = lax.broadcasted_iota(jnp.int32, tile.shape, 0) // rows
    lane_group = lax.broadcasted_iota(jnp.int32, tile.shape, 1) // slots
    ahead = lax.rem(lane_group - row_group + groups, groups)
    result = tile
    for k in range(1, groups):
        moved = pltpu.roll(tile, k * slots, 1)
        moved = pltpu.roll(moved, columns - k * rows, 0)
        result = jnp.where(ahead == k, moved, result)
    return result


def split_two(value):
    high = value.astype(BF16)
    low = (value - high.astype(F32)).astype(BF16)
    return high, low


def one_hots(cell, lines, size_z):
    half = lines // 2
    total = cell.shape[1]
    line = cell // size_z
    key = line // half * size_z + cell % size_z
    rows = jnp.broadcast_to(line % half, (half, total)) == lax.broadcasted_iota(jnp.int32, (half, total), 0)
    keys = lax.broadcasted_iota(jnp.int32, (2 * size_z, total), 0)
    keys = jnp.where(jnp.broadcast_to(key, (2 * size_z, total)) == keys, 1.0, 0.0).astype(BF16)
    return rows, keys


def nt_dot(left, right):
    return lax.dot_general(left, right, (((1,), (1,)), ((), ())), preferred_element_type=F32)


def even_places():
    return [lax.axis_index(axis) % 2 == 0 for axis in AXES]


def emit_faces(direction_ref, faces_out, dims):
    columns, size_x, size_y, size_z, slots = dims
    lines = size_x * size_y
    x_a, x_b, y_a, y_b, z_a, z_b = faces_out
    even = even_places()
    field = direction_ref[...]
    first_x, last_x = field[:, :size_y, :], field[:, lines - size_y :, :]
    x_a[...] = jnp.where(even[0], last_x, first_x)
    if x_b is not None:
        x_b[...] = jnp.where(even[0], first_x, last_x)
    for i in range(size_x):
        first_y = direction_ref[:, i * size_y, :]
        last_y = direction_ref[:, (i + 1) * size_y - 1, :]
        y_a[i] = jnp.where(even[1], last_y, first_y)
        if y_b is not None:
            y_b[i] = jnp.where(even[1], first_y, last_y)
    both = jnp.concatenate(split_two(field.reshape(columns * lines, size_z)), axis=1)
    row = lax.broadcasted_iota(jnp.int32, (8, size_z), 0)
    lane = lax.broadcasted_iota(jnp.int32, (8, size_z), 1)
    pick = ((row == 0) & (lane == size_z - 1)) | ((row == 1) & (lane == 0))
    pick = jnp.where(pick, 1.0, 0.0).astype(BF16)
    ends = nt_dot(jnp.concatenate([pick, pick], axis=1), both)
    last_z, first_z = ends[0:1, :], ends[1:2, :]
    z_a[...] = jnp.where(even[2], last_z, first_z)
    if z_b is not None:
        z_b[...] = jnp.where(even[2], first_z, last_z)


def gather_kernel(dims, early, *refs):
    extra, goes, parity, begin = early
    direction_ref, send_ref = refs[:2]
    faults_out = refs[-1]
    columns, size_x, size_y, size_z, slots = dims
    lines = size_x * size_y
    rows = columns * slots // LANES
    half = lines // 2
    field = direction_ref[...].astype(BF16)
    field = jnp.concatenate([field[:, :half, :], field[:, half:, :]], axis=2).reshape(columns * half, 2 * size_z)
    for i in range(send_ref.shape[1] // slots if goes else 0):
        at = i * (rows + extra) + rows
        if goes == "sums":
            source = refs[2][parity[i] * extra : (parity[i] + 1) * extra, :]
        else:
            own = slice(begin + i * extra, begin + (i + 1) * extra)
            source = refs[2][own, :] + refs[3][own, :]
        faults_out[at : at + extra, :] = source
    total = send_ref.shape[1]
    width = min(256, total)
    for start in range(0, total, width):
        hot_row, hot_key = one_hots(send_ref[:, start : start + width], lines, size_z)
        found = jnp.dot(field, hot_key, preferred_element_type=F32)
        found = jnp.where(hot_row[None], found.reshape(columns, half, width), 0.0)
        values = jnp.sum(found, axis=1)
        for j in range(0, width, LANES):
            tile = regroup(values[:, j : j + LANES], rows, slots)
            device = (start + j) // slots
            if not goes:
                faults_out[device * rows : device * rows + columns, :] = tile
                continue
            for i in range(LANES // slots):
                at = (device + i) * (rows + extra)
                faults_out[at : at + rows, :] = tile[i * rows : (i + 1) * rows]


def start_copies(pairs, sem):
    copies = [pltpu.make_async_copy(source, target, sem.at[i]) for i, (source, target) in enumerate(pairs)]
    for copy in copies:
        copy.start()
    return copies


def local_wells(cell, dims):
    _, size_x, size_y, size_z, _ = dims
    full_y, full_z = size_y * lax.axis_size("gy"), size_z * lax.axis_size("gz")
    at_x, at_y, at_z = cell // (full_y * full_z), cell // full_z % full_y, cell % full_z
    owned = (
        (at_x // size_x == lax.axis_index("gx"))
        & (at_y // size_y == lax.axis_index("gy"))
        & (at_z // size_z == lax.axis_index("gz"))
    )
    return jnp.where(owned, (at_x % size_x * size_y + at_y % size_y) * size_z + at_z % size_z, -1)


def edges_kernel(dims, *refs):
    columns, size_x, size_y, size_z, slots = dims
    ex_out, ey_out, ez_out = refs[7:10]
    tables_out, wells_out, held, sem = refs[10:13], refs[13], refs[14:21], refs[21]
    copies = start_copies(zip(refs[:7], held), sem)
    for copy in copies:
        copy.wait()
    tx, ty, tz = held[:3]
    lines = size_x * size_y
    ex_out[...] = tx[lines - size_y :, :]
    for i in range(size_x):
        ey_out[i : i + 1, :] = ty[(i + 1) * size_y - 1 : (i + 1) * size_y, :]
    ez_out[...] = tz[...].T[size_z - 1 : size_z, :]
    wells_out[...] = local_wells(held[6][...], dims)
    for table, out in zip(held[3:6], tables_out):
        value = table[0]
        out[...] = jnp.concatenate([value[i : i + 1, :] for i in range(value.shape[0])], axis=1)


def setup_kernel(dims, has_b, *refs):
    shifts_ref, which_ref, recv_ref, weight_ref = refs[:4]
    sources = refs[4:9]
    faces = 3 + sum(has_b)
    edges = unpack_faces(refs[9 : 9 + faces], has_b)
    ops_ref, residual_ref, direction_ref = refs[9 + faces : 12 + faces]
    faces_out = unpack_faces(refs[12 + faces : 12 + 2 * faces], has_b)
    held, sem = refs[12 + 2 * faces : -1], refs[-1]
    tx_ref, ty_ref, tz_ref, pore_ref = held
    copies = start_copies(zip(sources, held + (residual_ref,)), sem)
    columns, size_x, size_y, size_z, slots = dims
    lines = size_x * size_y
    line = lax.broadcasted_iota(jnp.int32, (lines, size_z), 0)
    lane = lax.broadcasted_iota(jnp.int32, (lines, size_z), 1)
    last = [lax.axis_index(axis) == lax.axis_size(axis) - 1 for axis in AXES]
    even = even_places()
    in_y = line % size_y
    for copy in copies[:-1]:
        copy.wait()
    upper_x = jnp.where((line >= lines - size_y) & last[0], 0.0, tx_ref[...])
    upper_y = jnp.where((in_y == size_y - 1) & last[1], 0.0, ty_ref[...])
    upper_z = jnp.where((lane == size_z - 1) & last[2], 0.0, tz_ref[...])
    behind = []
    for i in range(3):
        came = edges[2 * i][...]
        if edges[2 * i + 1] is not None:
            came = jnp.where(even[i], edges[2 * i + 1][...], came)
        behind.append(jnp.where(lax.axis_index(AXES[i]) == 0, 0.0, came))
    lower_x = jnp.concatenate([behind[0], upper_x[: lines - size_y]], axis=0)
    edge_y = jnp.concatenate(
        [jnp.broadcast_to(behind[1][i : i + 1, :], (size_y, size_z)) for i in range(size_x)], axis=0
    )
    lower_y = jnp.where(in_y == 0, edge_y, pltpu.roll(upper_y, 1, 0))
    lower_z = jnp.where(lane == 0, jnp.broadcast_to(behind[2], (8, lines)).T[:, 0:1], pltpu.roll(upper_z, 1, 1))
    total = recv_ref.shape[1]
    cell = recv_ref[...]
    hot_line = jnp.broadcast_to(cell // size_z, (lines, total)) == lax.broadcasted_iota(
        jnp.int32, (lines, total), 0
    )
    hot_lane = jnp.broadcast_to(cell % size_z, (size_z, total)) == lax.broadcasted_iota(
        jnp.int32, (size_z, total), 0
    )
    weight = weight_ref[...]
    high = weight.astype(BF16).astype(F32)
    middle = (weight - high).astype(BF16).astype(F32)
    low = weight - high - middle
    parts = [jnp.where(hot_line, part, 0.0).astype(BF16) for part in (high, middle, low)]
    summed = nt_dot(jnp.concatenate(parts, axis=0), jnp.where(hot_lane, 1.0, 0.0).astype(BF16))
    fault_diag = summed[:lines] + summed[lines : 2 * lines] + summed[2 * lines :]
    number = lax.broadcasted_iota(jnp.int32, shifts_ref.shape, 1)
    shift = jnp.sum(jnp.where(number == which_ref[...], shifts_ref[...], 0.0), axis=1, keepdims=True)
    diagonal = (
        upper_x + lower_x + upper_y + lower_y + upper_z + lower_z + shift * pore_ref[...] + fault_diag
    )
    inverse = 1.0 / diagonal
    inner_y = jnp.where(in_y == size_y - 1, 0.0, upper_y), jnp.where(in_y == 0, 0.0, lower_y)
    inner_z = jnp.where(lane == size_z - 1, 0.0, upper_z), jnp.where(lane == 0, 0.0, lower_z)
    face_y = upper_y - inner_y[0] + (lower_y - inner_y[1])
    face_z = upper_z - inner_z[0] + (lower_z - inner_z[1])
    for i, value in enumerate((upper_x, lower_x, *inner_y, *inner_z, diagonal, inverse, face_y, face_z)):
        ops_ref[i] = value
    copies[-1].wait()
    for c in range(columns):
        direction_ref[c] = residual_ref[c] * inverse
    emit_faces(direction_ref, faces_out, dims)


def unpack_faces(refs, has_b):
    refs = list(refs)
    faces = []
    for more in has_b:
        faces += [refs.pop(0), refs.pop(0) if more else None]
    return faces


def stencil_kernel(dims, has_b, first_round, *refs):
    refs = list(refs)
    columns, size_x, size_y, size_z, slots = dims
    ops_ref, residual_ref, direction_ref = refs[:3]
    refs = refs[3:]
    solution_out, residual_out = refs.pop(), refs.pop()
    solution_ref = None if first_round else refs.pop()
    xa_ref, xb_ref = refs[0], refs[-1]
    lines = size_x * size_y
    even = lax.axis_index(AXES[0]) % 2 == 0
    for c in range(columns):
        value = direction_ref[c]
        x_low = jnp.where(even, xb_ref[c], xa_ref[c])
        x_high = jnp.where(even, xa_ref[c], xb_ref[c])
        beside = ops_ref[0] * jnp.concatenate([value[size_y:], x_high], axis=0)
        beside += ops_ref[1] * jnp.concatenate([x_low, value[: lines - size_y]], axis=0)
        beside += ops_ref[2] * pltpu.roll(value, lines - 1, 0)
        beside += ops_ref[3] * pltpu.roll(value, 1, 0)
        beside += ops_ref[4] * pltpu.roll(value, size_z - 1, 1)
        beside += ops_ref[5] * pltpu.roll(value, 1, 1)
        residual_out[c] = residual_ref[c] - (ops_ref[6] * value - beside)
        solution_out[c] = value if first_round else solution_ref[c] + value


def update_kernel(dims, has_b, keep, gain, last_round, early, *refs):
    refs = list(refs)
    columns, size_x, size_y, size_z, slots = dims
    extra, comes, parity = early
    ops_ref, residual_ref, direction_ref, recv_ref, weight_ref, arrived_ref = refs[:6]
    refs = refs[6:]
    ya_ref, yb_ref, za_ref, zb_ref = unpack_faces(refs[: 2 + has_b[1] + has_b[2]], has_b[1:])
    refs = refs[2 + has_b[1] + has_b[2] :]
    yb_ref = ya_ref if yb_ref is None else yb_ref
    zb_ref = za_ref if zb_ref is None else zb_ref
    if last_round:
        solution_ref, well_ref, *refs = refs
        blocks = (len(refs) - 5) // 2
        sources, (sums_out, flat_out, landed_ref, solution_out) = refs[:blocks], refs[blocks : blocks + 4]
        basis_refs, sem = refs[blocks + 4 : -1], refs[-1]
        fetches = start_copies(zip(sources, basis_refs), sem)
    else:
        landed_ref = refs.pop()
    table_out = refs.pop(0) if comes else None
    if not last_round:
        residual_out, direction_out = refs[:2]
        faces_out = unpack_faces(refs[2:], has_b)
    lines = size_x * size_y
    rows = columns * slots // LANES
    total = recv_ref.shape[1]
    half = lines // 2
    hot_row, hot_key = one_hots(recv_ref[...], lines, size_z)
    hot_row = jnp.where(hot_row, 1.0, 0.0).astype(BF16)
    tiles = []
    devices = total // slots
    if comes:
        per_device = rows + extra
        for i in range(devices):
            landed_ref[i * rows : (i + 1) * rows, :LANES] = arrived_ref[i * per_device : i * per_device + rows, :]
        source_ref = landed_ref
    else:
        source_ref = arrived_ref
    for j in range(total // LANES):
        tiles.append(regroup(source_ref[j * columns : (j + 1) * columns, :LANES], rows, slots))
    if comes == "parts":
        added = [jnp.zeros((extra, LANES), F32)] * 2
        for i in range(devices):
            at = i * per_device + rows
            added[parity[i]] = added[parity[i]] + arrived_ref[at : at + extra, :]
        table_out[:extra, :], table_out[extra:, :] = added
    if comes == "sums":
        for i in range(devices):
            at = i * per_device + rows
            table_out[i * extra : (i + 1) * extra, :] = arrived_ref[at : at + extra, :]
    weighted = (jnp.concatenate(tiles, axis=1) * weight_ref[...]).astype(BF16)
    spread = weighted[:, None, :] * hot_row[None, :, :]
    landed_ref[...] = nt_dot(spread.reshape(columns * half, total), hot_key)
    even = even_places()
    in_slab = lax.broadcasted_iota(jnp.int32, (size_y, size_z), 0)
    lane = lax.broadcasted_iota(jnp.int32, (lines, size_z), 1)
    z_a, z_b = za_ref[...], zb_ref[...]
    z_rows = [jnp.where(even[2], z_b, z_a), jnp.where(even[2], z_a, z_b), jnp.zeros((6, columns * lines), F32)]
    z_cols = jnp.concatenate(z_rows, axis=0).T
    for c in range(columns):
        landed = landed_ref[c * half : (c + 1) * half, :]
        left = residual_ref[c] + jnp.concatenate([landed[:, :size_z], landed[:, size_z:]], axis=0)
        beside_y = []
        for i in range(size_x):
            y_a, y_b = ya_ref[i, c : c + 1, :], yb_ref[i, c : c + 1, :]
            y_low, y_high = jnp.where(even[1], y_b, y_a), jnp.where(even[1], y_a, y_b)
            beside_y.append(jnp.where(in_slab < size_y // 2, y_low, y_high))
        z_low = z_cols[c * lines : (c + 1) * lines, 0:1]
        z_high = z_cols[c * lines : (c + 1) * lines, 1:2]
        left = left + ops_ref[8] * jnp.concatenate(beside_y, axis=0)
        left = left + ops_ref[9] * jnp.where(lane < size_z // 2, z_low, z_high)
        after = keep * direction_ref[c] + gain * (left * ops_ref[7])
        if last_round:
            solution_out[c] = solution_ref[c] + after
        else:
            residual_out[c] = left
            direction_out[c] = after
    if not last_round:
        emit_faces(direction_out, faces_out, dims)
    else:
        for copy in fetches:
            copy.wait()
        sums_of(dims, solution_out, basis_refs, well_ref, flat_out, sums_out)


def basis_kernel(dims, piece, blocks, *refs):
    well_ref, source_ref = refs[:2]
    others = refs[2 : 2 + piece]
    last = piece == blocks - 1
    before = refs[2 + piece : 2 + 3 * piece] if last else ()
    refs = refs[2 + piece + len(before) :]
    flat_target, gram_out, wells_out, basis_ref, hot_ref, flat_out, sem, out_sem = refs[:8]
    held = refs[8 : 8 + piece]
    columns, size_x, size_y, size_z, slots = dims
    lines = size_x * size_y
    wells = well_ref.shape[1]
    side = 16
    groups = [pl.ds(first, side) for first in range(0, LANES, side)]
    copies = [
        pltpu.make_async_copy(source_ref.at[pl.ds(piece * LANES + i * side, side)], basis_ref.at[g], sem.at[i])
        for i, g in enumerate(groups)
    ]
    for copy in copies:
        copy.start()
    fetches = start_copies(zip(others, held), refs[8 + piece]) if piece else []
    stores = []
    row = lax.broadcasted_iota(jnp.int32, (side * side, side * side), 0)
    lane = lax.broadcasted_iota(jnp.int32, (side * side, side * side), 1)
    turn = jnp.where((row % side == lane // side) & (row // side == lane % side), 1.0, 0.0).astype(BF16)
    cell = well_ref[...]
    lane_of = jnp.broadcast_to(lax.rem(cell + size_z, size_z), (size_z, wells))
    lane_of = lane_of == lax.broadcasted_iota(jnp.int32, (size_z, wells), 0)
    line_of = jnp.broadcast_to(jnp.where(cell < 0, -1, cell // size_z), (size_z, wells))
    for line in range(lines):
        hot = jnp.where(lane_of & (line_of == line), 1.0, 0.0)
        hot_ref[line * size_z : (line + 1) * size_z, :] = hot.astype(BF16)
    for index in range(0, len(groups), 2):
        copies[index].wait()
        copies[index + 1].wait()
        first = index * side
        for begin in range(0, lines, side):
            tile = [
                basis_ref[at : at + side, begin : begin + side, :].reshape(side * side, size_z)
                for at in (first, first + side)
            ]
            tile = jnp.dot(turn, jnp.concatenate(tile, axis=1), preferred_element_type=F32).astype(BF16)
            for i in range(side):
                lanes = slice((begin + i) * size_z, (begin + i + 1) * size_z)
                flat_out[first : first + side, lanes] = tile[i * side : (i + 1) * side, :size_z]
                flat_out[first + side : first + 2 * side, lanes] = tile[i * side : (i + 1) * side, size_z:]
        pair = pl.ds(first, 2 * side)
        stores.append(pltpu.make_async_copy(flat_out.at[pair], flat_target.at[pair], out_sem.at[index // 2]))
        stores[-1].start()
    flat = flat_out[...]
    for copy in fetches:
        copy.wait()
    for i, other in enumerate(held + (flat_out,)):
        product = nt_dot(other[...], flat)
        if last:
            place = (piece * (piece + 1) // 2 + i) * LANES
            refs[-1][place : place + LANES, :] = product
        else:
            gram_out[i * LANES : (i + 1) * LANES, :] = product
    at_wells = jnp.dot(flat, hot_ref[...], preferred_element_type=F32)
    if last:
        full_ref, beside, place = refs[-1], LANES // wells, 0
        for i in range(piece):
            full_ref[place : place + (i + 1) * LANES, :] = before[2 * i][...]
            place += (i + 1) * LANES
        place += (piece + 1) * LANES
        full_ref[place:, :] = jnp.zeros((full_ref.shape[0] - place, LANES), F32)
        for i in range(blocks):
            value = at_wells if i == piece else before[2 * i + 1][...]
            at, lanes = place + i // beside * LANES, slice(i % beside * wells, (i % beside + 1) * wells)
            full_ref[at : at + LANES, lanes] = value
        half, even = full_ref.shape[0] // 2, even_places()[1]
        gram_out[...] = jnp.where(even, full_ref[:half, :], full_ref[half:, :])
        wells_out[...] = jnp.where(even, full_ref[half:, :], full_ref[:half, :])
    else:
        wells_out[...] = at_wells
    for store in stores:
        store.wait()


def split_three(value):
    high = value.astype(BF16)
    left = value - high.astype(F32)
    middle = left.astype(BF16)
    return high, middle, (left - middle.astype(F32)).astype(BF16)


def sums_of(dims, solution_ref, basis_refs, well_ref, flat_out, sums_out):
    columns, size_x, size_y, size_z, slots = dims
    lines = size_x * size_y
    wells = well_ref.shape[1]
    for line in range(lines):
        flat_out[:, line * size_z : (line + 1) * size_z] = solution_ref[:, line, :]
    parts = jnp.concatenate(split_three(flat_out[...]), axis=0)
    with_basis = jnp.concatenate([nt_dot(parts, ref[...]) for ref in basis_refs], axis=1)
    with_self = nt_dot(parts, parts)
    sums_out[...] = jnp.zeros(sums_out.shape, F32)
    blocks = len(basis_refs)
    first = with_basis[:columns]
    beyond = with_basis[columns : 2 * columns] + with_basis[2 * columns :]
    for i in range(blocks):
        lanes = slice(i * LANES, (i + 1) * LANES)
        sums_out[i * columns : (i + 1) * columns, :] = first[:, lanes]
        sums_out[(blocks + i) * columns : (blocks + i + 1) * columns, :] = beyond[:, lanes]
    rows = with_self[:columns] + with_self[columns : 2 * columns] + with_self[2 * columns :]
    square = rows[:, :columns] + rows[:, columns : 2 * columns] + rows[:, 2 * columns :]
    at = 2 * blocks * columns
    sums_out[at : at + columns, :columns] = square
    both = jnp.concatenate(split_two(solution_ref[...].reshape(columns * lines, size_z)), axis=1)
    cell = well_ref[...]
    lane_of = jnp.broadcast_to(lax.rem(cell + size_z, size_z), (size_z, wells))
    hot = lane_of == lax.broadcasted_iota(jnp.int32, (size_z, wells), 0)
    hot = jnp.where(hot, 1.0, 0.0).astype(BF16)
    found = jnp.dot(both, jnp.concatenate([hot, hot], axis=0), preferred_element_type=F32)
    line_of = jnp.broadcast_to(jnp.where(cell < 0, -1, cell // size_z), (lines, wells))
    mask = line_of == lax.broadcasted_iota(jnp.int32, (lines, wells), 0)
    found = jnp.where(mask[None], found.reshape(columns, lines, wells), 0.0)
    at += columns
    sums_out[at : at + columns, :wells] = jnp.sum(found, axis=1)


def exact_dot(left, right, transposed=False):
    axes = ((1,), (1,)) if transposed else ((1,), (0,))
    return lax.dot_general(
        left, right, (axes, ((), ())), precision=lax.Precision.HIGHEST, preferred_element_type=F32
    )


def finish_kernel(
    dims, scale, wells, blocks, groups, sums_ref, flat_ref, *refs
):
    mine, other = ([ref[...] for ref in refs[i * groups : (i + 1) * groups]] for i in range(2))
    mine, other, refs = jnp.concatenate(mine, axis=0), jnp.concatenate(other, axis=0), refs[2 * groups :]
    even = even_places()[1]
    table = [jnp.where(even, mine, other), jnp.where(even, other, mine)]
    table = jnp.concatenate(table, axis=0)
    block_out, first_out, coeffs_out, wells_out = refs[blocks : blocks + 4]
    basis_refs = refs[blocks + 4 : -1]
    fetches = start_copies(zip(refs[:blocks], basis_refs), refs[-1])
    columns, size_x, size_y, size_z, slots = dims
    lines = size_x * size_y
    pieces, at = {}, 0
    for i in range(blocks):
        for j in range(i + 1):
            pieces[j, i] = table[at : at + LANES, :]
            pieces[i, j] = pieces[j, i] if i == j else pieces[j, i].T
            at += LANES
    basis_gram = jnp.concatenate(
        [jnp.concatenate([pieces[i, j] for j in range(blocks)], axis=1) for i in range(blocks)], axis=0
    )
    beside = LANES // wells
    wells_basis = []
    for i in range(blocks):
        place = at + i // beside * LANES
        wells_basis.append(table[place : place + LANES, i % beside * wells : (i % beside + 1) * wells])
    wells_basis = jnp.concatenate(wells_basis, axis=0)

    def block(i):
        return sums_ref[i * columns : (i + 1) * columns, :]

    first = jnp.concatenate([block(i) for i in range(blocks)], axis=1)
    beyond = jnp.concatenate([block(blocks + i) for i in range(blocks)], axis=1)
    full = first + beyond
    square = block(2 * blocks)[:, :columns]
    at_wells = block(2 * blocks + 1)[:, :wells]
    gram_parts = split_three(basis_gram)

    def times_gram(value):
        return sum(jnp.dot(value, part, preferred_element_type=F32) for part in gram_parts)

    first_round = first.astype(BF16)
    first_gram = times_gram(first_round)
    second = full - first_gram
    second_round = second.astype(BF16)
    rounds = jnp.concatenate([first_round, second_round], axis=0)
    half = full - 0.5 * (first_gram + times_gram(second_round))
    products = nt_dot(rounds, jnp.concatenate(split_three(half), axis=0))
    products = products[:columns] + products[columns:]
    cross = products[:, :columns] + products[:, columns : 2 * columns] + products[:, 2 * columns :]
    gram = square - cross - cross.T
    spans = jnp.dot(rounds, wells_basis.astype(BF16), preferred_element_type=F32)
    rest_wells = at_wells - spans[:columns] - spans[columns:]
    first_out[...] = first
    coeffs_out[...] = first + second
    row = lax.broadcasted_iota(jnp.int32, (columns, columns), 0)
    lane = lax.broadcasted_iota(jnp.int32, (columns, columns), 1)
    left = gram
    right = jnp.where(row == lane, 1.0, 0.0)
    below = lax.broadcasted_iota(jnp.int32, (columns, 1), 0)
    for k in range(columns - 1):
        factor = jnp.where(below > k, left[:, k : k + 1] / left[k : k + 1, k : k + 1], 0.0)
        right = right - factor * right[k : k + 1, :]
        left = left - factor * left[k : k + 1, :]
    pivots = jnp.sum(jnp.where(row == lane, left, 0.0), axis=1, keepdims=True)
    inverse = right * (scale / jnp.sqrt(pivots))
    wells_out[...] = exact_dot(inverse, rest_wells)
    high, low = split_two(inverse)
    factors = jnp.concatenate([high, high, low], axis=1)
    for copy in fetches:
        copy.wait()
    step = min(8, lines)
    for begin in range(0, lines, step):
        lanes = slice(begin * size_z, (begin + step) * size_z)
        basis_part = jnp.concatenate([ref[:, lanes] for ref in basis_refs], axis=0)
        spans = jnp.dot(rounds, basis_part, preferred_element_type=F32)
        rest = flat_ref[:, lanes] - spans[:columns] - spans[columns:]
        rest_high, rest_low = split_two(rest)
        stacked = jnp.concatenate([rest_high, rest_low, rest_high], axis=0)
        done = jnp.dot(factors, stacked, preferred_element_type=F32)
        for i in range(step):
            block_out[:, begin + i, :] = done[:, i * size_z : (i + 1) * size_z]


def local(
    start_block,
    basis,
    trans_x,
    trans_y,
    trans_z,
    pore_volume,
    shift_table,
    shift_index,
    fault_send,
    fault_recv,
    fault_trans,
    well_cells,
):
    columns, size_x, size_y, size_z = start_block.shape
    devices, slots = fault_send.shape[1:]
    lines = size_x * size_y
    cells = lines * size_z
    total = devices * slots
    sizes = [lax.axis_size(axis) for axis in AXES]
    full_x, full_y, full_z = size_x * sizes[0], size_y * sizes[1], size_z * sizes[2]
    has_b = tuple(size > 2 for size in sizes)
    dims = (columns, size_x, size_y, size_z, slots)
    rows = columns * slots // LANES

    vmem = pl.BlockSpec(memory_space=pltpu.VMEM)
    params = pltpu.CompilerParams(vmem_limit_bytes=8 * 2**20 + 4096 * total)
    wide_params = pltpu.CompilerParams(vmem_limit_bytes=16 * 2**20 + 4096 * total)
    field_type = jax.ShapeDtypeStruct((columns, lines, size_z), F32)
    x_type = jax.ShapeDtypeStruct((columns, size_y, size_z), F32)
    y_type = jax.ShapeDtypeStruct((size_x, columns, size_z), F32)
    z_type = jax.ShapeDtypeStruct((1, columns * lines), F32)
    face_types = [x_type] * (1 + has_b[0]) + [y_type] * (1 + has_b[1]) + [z_type] * (1 + has_b[2])

    def in_hbm(*values):
        return [pltpu.with_memory_space_constraint(value, pltpu.HBM) for value in values]

    shape2 = (lines, size_z)
    start = start_block.reshape(columns, lines, size_z)
    anywhere = pl.BlockSpec(memory_space=pltpu.HBM)
    trans = [value.reshape(shape2) for value in (trans_x, trans_y, trans_z)]
    row_types = [jax.ShapeDtypeStruct((1, total), kind) for kind in (jnp.int32, jnp.int32, F32)]
    edge_types = [
        jax.ShapeDtypeStruct(shape, F32) for shape in ((size_y, size_z), (size_x, size_z), (1, lines))
    ]
    wells = well_cells.shape[0]
    edge_x, edge_y, edge_z, send, recv, weight, well_row = pl.pallas_call(
        functools.partial(edges_kernel, dims),
        out_shape=edge_types + row_types + [jax.ShapeDtypeStruct((1, wells), jnp.int32)],
        in_specs=[anywhere] * 7,
        out_specs=[vmem] * 7,
        scratch_shapes=[pltpu.VMEM(shape2, F32)] * 3
        + [pltpu.VMEM(fault_send.shape, kind) for kind in (jnp.int32, jnp.int32, F32)]
        + [pltpu.VMEM((1, wells), jnp.int32), pltpu.SemaphoreType.DMA((7,))],
        compiler_params=params,
        name="edges",
    )(*in_hbm(*trans, fault_send, fault_recv, fault_trans, well_cells.reshape(1, wells)))
    edges = []
    for axis, edge, more in zip(AXES, (edge_x, edge_y, edge_z), has_b):
        edges += [swap_even(edge, axis)] + ([swap_odd(edge, axis)] if more else [])

    count = basis.shape[0]
    blocks = count // LANES
    early_rows = LANES * (blocks * (blocks + 1) // 2 + -(-blocks // (LANES // wells)))
    groups = 2
    extra = -(-early_rows // (2 * groups * devices))
    half_rows = groups * devices * extra
    parity = [i // sizes[2] % sizes[1] % 2 for i in range(devices)]
    flats, parts = [], []
    for piece in range(blocks):
        last = piece == blocks - 1
        shapes = [(half_rows, LANES)] * 2 if last else [((piece + 1) * LANES, LANES), (LANES, wells)]
        before = parts if last else []
        flat_piece, *part = pl.pallas_call(
            functools.partial(basis_kernel, dims, piece, blocks),
            out_shape=[pltpu.HBM((LANES, cells), BF16)] + [jax.ShapeDtypeStruct(shape, F32) for shape in shapes],
            in_specs=[vmem] + [anywhere] * (1 + piece) + [vmem] * len(before),
            out_specs=[anywhere, vmem, vmem],
            scratch_shapes=[
                pltpu.VMEM((LANES, lines, size_z), BF16),
                pltpu.VMEM((cells, wells), BF16),
                pltpu.VMEM((LANES, cells), BF16),
                pltpu.SemaphoreType.DMA((LANES // 16,)),
                pltpu.SemaphoreType.DMA((LANES // 32,)),
            ]
            + [pltpu.VMEM((LANES, cells), BF16)] * piece
            + [pltpu.SemaphoreType.DMA((max(piece, 1),))]
            + [pltpu.VMEM((2 * half_rows, LANES), F32)] * last,
            compiler_params=wide_params,
            cost_estimate=pl.CostEstimate(
                flops=2 * LANES * cells * ((piece + 1) * LANES + wells),
                bytes_accessed=4 * LANES * cells,
                transcendentals=0,
            ),
            name="basis_gram",
        )(well_row, *in_hbm(basis.reshape(count, lines, size_z), *flats), *before)
        flats.append(flat_piece)
        if not piece:
            part[0], *edges = lax.optimization_barrier((part[0], *edges))
        parts += part

    keep_parts, give_parts = parts[-2:]

    def gather(direction, goes, source, group):
        sent_rows = devices * (rows + (extra if goes else 0))
        return pl.pallas_call(
            functools.partial(gather_kernel, dims, (extra, goes, parity, group * devices * extra)),
            out_shape=jax.ShapeDtypeStruct((sent_rows, LANES), F32),
            in_specs=[vmem] * (2 + len(source)),
            out_specs=vmem,
            compiler_params=params,
            cost_estimate=pl.CostEstimate(
                flops=4 * columns * cells * total, bytes_accessed=4 * columns * cells, transcendentals=0
            ),
            name="fault_gather",
        )(direction, send, *source)

    def transfers(faults, faces):
        faces = list(faces)
        came = {}
        for axis, more in zip(AXES, has_b):
            came[axis] = [swap_even(faces.pop(0), axis)] + ([swap_odd(faces.pop(0), axis)] if more else [])
        faults, came["gy"][0] = lax.optimization_barrier((faults, came["gy"][0]))
        return exchange(faults), came["gx"], came["gy"] + came["gz"]

    def stencil(residual, direction, came, solution):
        more = [] if solution is None else [solution]
        return pl.pallas_call(
            functools.partial(stencil_kernel, dims, has_b, solution is None),
            out_shape=[field_type, field_type],
            in_specs=[vmem] * (3 + len(came) + len(more)),
            out_specs=[vmem] * 2,
            input_output_aliases={1: 0, 3 + len(came): 1} if more else {1: 0},
            compiler_params=params,
            cost_estimate=pl.CostEstimate(
                flops=20 * columns * cells, bytes_accessed=12 * columns * cells, transcendentals=0
            ),
            name="stencil",
        )(ops, residual, direction, *came, *more)

    ops, residual, direction, *faces = pl.pallas_call(
        functools.partial(setup_kernel, dims, has_b),
        out_shape=[jax.ShapeDtypeStruct((10, lines, size_z), F32), field_type, field_type] + face_types,
        in_specs=[vmem] * 4 + [anywhere] * 5 + [vmem] * len(edges),
        out_specs=[vmem] * (3 + len(face_types)),
        scratch_shapes=[pltpu.VMEM(shape2, F32)] * 4
        + [pltpu.SemaphoreType.DMA((5,))],
        compiler_params=params,
        name="setup",
    )(
        shift_table.reshape(1, -1), shift_index.reshape(1, 1), recv, weight,
        *in_hbm(*trans, pore_volume.reshape(shape2), start), *edges,
    )
    needed = columns * (2 * blocks + 2)
    per_device = 1 << (-(-needed // devices) - 1).bit_length()
    sums_type = jax.ShapeDtypeStruct((devices * per_device, LANES), F32)
    flat_type = jax.ShapeDtypeStruct((columns, cells), F32)
    sigma = 1.0 / 0.9
    weight_now = 1.0 / sigma
    solution = None
    tables = {}
    came_parts = swap_even(give_parts, "gy")
    for number in range(TERMS - 1):
        goes = ("", "parts", "sums", "")[number // 2]
        group = number % groups
        source = {"parts": [keep_parts, came_parts], "sums": [tables.get(group)]}.get(goes, [])
        faults = gather(direction, goes, source, group)
        arrived, came, far = transfers(faults, faces)
        residual, solution = stencil(residual, direction, came, solution)
        weight_new = 1.0 / (2.0 * sigma - weight_now)
        last_round = number == TERMS - 2
        body = functools.partial(
            update_kernel, dims, has_b, weight_new * weight_now, 2.0 * weight_new / 0.9,
            last_round, (extra, goes, parity),
        )
        weight_now = weight_new
        scratch = [pltpu.VMEM((columns * lines // 2, 2 * size_z), F32)]
        out_types = [sums_type, flat_type] if last_round else []
        if goes:
            table_rows = 2 * extra if goes == "parts" else devices * extra
            out_types.append(jax.ShapeDtypeStruct((table_rows, LANES), F32))
        operands = [ops, residual, direction, recv, weight, arrived, *far]
        aliases = {}
        if last_round:
            operands.append(solution)
        in_specs = [vmem] * len(operands)
        if not last_round:
            aliases[1], aliases[2] = len(out_types), len(out_types) + 1
            out_types += [field_type, field_type] + face_types
        else:
            operands += [well_row, *in_hbm(*flats)]
            in_specs += [vmem] + [anywhere] * blocks
            scratch.append(pltpu.VMEM((columns, lines, size_z), F32))
            scratch += [pltpu.VMEM((LANES, cells), BF16)] * blocks + [pltpu.SemaphoreType.DMA((blocks,))]
        outs = pl.pallas_call(
            body,
            out_shape=out_types,
            in_specs=in_specs,
            out_specs=[vmem] * len(out_types),
            scratch_shapes=scratch,
            input_output_aliases=aliases,
            compiler_params=wide_params if last_round else params,
            name="update",
        )(*operands)
        if last_round:
            sums, flat = outs
            break
        if goes:
            table, *outs = outs
            tables[group] = table
        residual, direction, *faces = outs

    mine = exchange(sums).reshape(devices, per_device, LANES).sum(axis=0)
    sums = exchange(jnp.tile(mine, (devices, 1)))

    mine = [tables[group] for group in range(groups)]
    scale = math.sqrt(full_x * full_y * full_z)
    new_block, first_coeffs, coeffs, well_resp = pl.pallas_call(
        functools.partial(finish_kernel, dims, scale, wells, blocks, groups),
        out_shape=[
            field_type,
            jax.ShapeDtypeStruct((columns, count), F32),
            jax.ShapeDtypeStruct((columns, count), F32),
            jax.ShapeDtypeStruct((columns, wells), F32),
        ],
        in_specs=[vmem] * (2 + 2 * groups) + [anywhere] * blocks,
        out_specs=[vmem] * 4,
        scratch_shapes=[pltpu.VMEM((LANES, cells), BF16)] * blocks + [pltpu.SemaphoreType.DMA((blocks,))],
        compiler_params=wide_params,
        name="finish",
    )(sums, flat, *mine, *[swap_even(table, "gy") for table in mine], *in_hbm(*flats))
    return new_block.reshape(start_block.shape), first_coeffs.T, coeffs.T, well_resp.T


def solution(mesh):
    in_specs = (
        P(None, "gx", "gy", "gz"),
        P(None, "gx", "gy", "gz"),
        P("gx", "gy", "gz"),
        P("gx", "gy", "gz"),
        P("gx", "gy", "gz"),
        P("gx", "gy", "gz"),
        P(),
        P(),
        P(("gx", "gy", "gz"), None, None),
        P(("gx", "gy", "gz"), None, None),
        P(("gx", "gy", "gz"), None, None),
        P(),
    )
    out_specs = (P(None, "gx", "gy", "gz"), P(), P(), P())
    return jax.shard_map(local, mesh=mesh, in_specs=in_specs, out_specs=out_specs, check_vma=False)
```

```python
import functools
import math

import jax
import jax.numpy as jnp
from jax import lax
from jax.experimental import pallas as pl
from jax.experimental.pallas import tpu as pltpu
from jax.sharding import PartitionSpec as P

TERMS = 8
AXES = ("gx", "gy", "gz")
LANES = 128
BF16 = jnp.bfloat16
F32 = jnp.float32


def swap_even(value, axis):
    size = lax.axis_size(axis)
    pairs = [(i, i ^ 1) for i in range(size) if i ^ 1 < size]
    return lax.ppermute(value, axis, pairs)


def swap_odd(value, axis):
    size = lax.axis_size(axis)
    other = "gy" if axis == "gx" else "gx"
    across = lax.axis_size(other)
    names = (axis, other) if axis == "gx" else (other, axis)

    def number(i, o):
        return i * across + o if axis == "gx" else o * size + i

    pairs = []
    for o in range(across):
        for i in range(size):
            to = (i + 1 if i % 2 else i - 1, o)
            if not 0 <= to[0] < size:
                to = (i, o ^ 1)
            if to[1] < across:
                pairs.append((number(i, o), number(*to)))
    return lax.ppermute(value, names, pairs)


def exchange(value):
    return lax.all_to_all(value, AXES, split_axis=0, concat_axis=0, tiled=True)


def regroup(tile, rows, slots):
    groups = LANES // slots
    columns = tile.shape[0]
    row_group = lax.broadcasted_iota(jnp.int32, tile.shape, 0) // rows
    lane_group = lax.broadcasted_iota(jnp.int32, tile.shape, 1) // slots
    ahead = lax.rem(lane_group - row_group + groups, groups)
    result = tile
    for k in range(1, groups):
        moved = pltpu.roll(tile, k * slots, 1)
        moved = pltpu.roll(moved, columns - k * rows, 0)
        result = jnp.where(ahead == k, moved, result)
    return result


def split_two(value):
    high = value.astype(BF16)
    low = (value - high.astype(F32)).astype(BF16)
    return high, low


def one_hots(cell, lines, size_z):
    half = lines // 2
    total = cell.shape[1]
    line = cell // size_z
    key = line // half * size_z + cell % size_z
    rows = jnp.broadcast_to(line % half, (half, total)) == lax.broadcasted_iota(jnp.int32, (half, total), 0)
    keys = lax.broadcasted_iota(jnp.int32, (2 * size_z, total), 0)
    keys = jnp.where(jnp.broadcast_to(key, (2 * size_z, total)) == keys, 1.0, 0.0).astype(BF16)
    return rows, keys


def nt_dot(left, right):
    return lax.dot_general(left, right, (((1,), (1,)), ((), ())), preferred_element_type=F32)


def even_places():
    return [lax.axis_index(axis) % 2 == 0 for axis in AXES]


def emit_faces(direction_ref, faces_out, dims):
    columns, size_x, size_y, size_z, slots = dims
    lines = size_x * size_y
    x_a, x_b, y_a, y_b, z_a, z_b = faces_out
    even = even_places()
    field = direction_ref[...]
    first_x, last_x = field[:, :size_y, :], field[:, lines - size_y :, :]
    x_a[...] = jnp.where(even[0], last_x, first_x)
    if x_b is not None:
        x_b[...] = jnp.where(even[0], first_x, last_x)
    for i in range(size_x):
        first_y = direction_ref[:, i * size_y, :]
        last_y = direction_ref[:, (i + 1) * size_y - 1, :]
        y_a[i] = jnp.where(even[1], last_y, first_y)
        if y_b is not None:
            y_b[i] = jnp.where(even[1], first_y, last_y)
    both = jnp.concatenate(split_two(field.reshape(columns * lines, size_z)), axis=1)
    row = lax.broadcasted_iota(jnp.int32, (8, size_z), 0)
    lane = lax.broadcasted_iota(jnp.int32, (8, size_z), 1)
    pick = ((row == 0) & (lane == size_z - 1)) | ((row == 1) & (lane == 0))
    pick = jnp.where(pick, 1.0, 0.0).astype(BF16)
    ends = nt_dot(jnp.concatenate([pick, pick], axis=1), both)
    last_z, first_z = ends[0:1, :], ends[1:2, :]
    z_a[...] = jnp.where(even[2], last_z, first_z)
    if z_b is not None:
        z_b[...] = jnp.where(even[2], first_z, last_z)


def gather_kernel(dims, early, *refs):
    extra, goes, parity, begin = early
    direction_ref, send_ref = refs[:2]
    faults_out = refs[-1]
    columns, size_x, size_y, size_z, slots = dims
    lines = size_x * size_y
    rows = columns * slots // LANES
    half = lines // 2
    field = direction_ref[...].astype(BF16)
    field = jnp.concatenate([field[:, :half, :], field[:, half:, :]], axis=2).reshape(columns * half, 2 * size_z)
    for i in range(send_ref.shape[1] // slots if goes else 0):
        at = i * (rows + extra) + rows
        if goes == "sums":
            source = refs[2][parity[i] * extra : (parity[i] + 1) * extra, :]
        else:
            own = slice(begin + i * extra, begin + (i + 1) * extra)
            source = refs[2][own, :] + refs[3][own, :]
        faults_out[at : at + extra, :] = source
    total = send_ref.shape[1]
    width = min(256, total)
    for start in range(0, total, width):
        hot_row, hot_key = one_hots(send_ref[:, start : start + width], lines, size_z)
        found = jnp.dot(field, hot_key, preferred_element_type=F32)
        found = jnp.where(hot_row[None], found.reshape(columns, half, width), 0.0)
        values = jnp.sum(found, axis=1)
        for j in range(0, width, LANES):
            tile = regroup(values[:, j : j + LANES], rows, slots)
            device = (start + j) // slots
            if not goes:
                faults_out[device * rows : device * rows + columns, :] = tile
                continue
            for i in range(LANES // slots):
                at = (device + i) * (rows + extra)
                faults_out[at : at + rows, :] = tile[i * rows : (i + 1) * rows]


def start_copies(pairs, sem):
    copies = [pltpu.make_async_copy(source, target, sem.at[i]) for i, (source, target) in enumerate(pairs)]
    for copy in copies:
        copy.start()
    return copies


def local_wells(cell, dims):
    _, size_x, size_y, size_z, _ = dims
    full_y, full_z = size_y * lax.axis_size("gy"), size_z * lax.axis_size("gz")
    at_x, at_y, at_z = cell // (full_y * full_z), cell // full_z % full_y, cell % full_z
    owned = (
        (at_x // size_x == lax.axis_index("gx"))
        & (at_y // size_y == lax.axis_index("gy"))
        & (at_z // size_z == lax.axis_index("gz"))
    )
    return jnp.where(owned, (at_x % size_x * size_y + at_y % size_y) * size_z + at_z % size_z, -1)


def edges_kernel(dims, *refs):
    columns, size_x, size_y, size_z, slots = dims
    ex_out, ey_out, ez_out = refs[7:10]
    tables_out, wells_out, held, sem = refs[10:13], refs[13], refs[14:21], refs[21]
    copies = start_copies(zip(refs[:7], held), sem)
    for copy in copies:
        copy.wait()
    tx, ty, tz = held[:3]
    lines = size_x * size_y
    ex_out[...] = tx[lines - size_y :, :]
    for i in range(size_x):
        ey_out[i : i + 1, :] = ty[(i + 1) * size_y - 1 : (i + 1) * size_y, :]
    ez_out[...] = tz[...].T[size_z - 1 : size_z, :]
    wells_out[...] = local_wells(held[6][...], dims)
    for table, out in zip(held[3:6], tables_out):
        value = table[0]
        out[...] = jnp.concatenate([value[i : i + 1, :] for i in range(value.shape[0])], axis=1)


def setup_kernel(dims, has_b, *refs):
    shifts_ref, which_ref, recv_ref, weight_ref = refs[:4]
    sources = refs[4:9]
    faces = 3 + sum(has_b)
    edges = unpack_faces(refs[9 : 9 + faces], has_b)
    ops_ref, residual_ref, direction_ref = refs[9 + faces : 12 + faces]
    faces_out = unpack_faces(refs[12 + faces : 12 + 2 * faces], has_b)
    held, sem = refs[12 + 2 * faces : -1], refs[-1]
    tx_ref, ty_ref, tz_ref, pore_ref = held
    copies = start_copies(zip(sources, held + (residual_ref,)), sem)
    columns, size_x, size_y, size_z, slots = dims
    lines = size_x * size_y
    line = lax.broadcasted_iota(jnp.int32, (lines, size_z), 0)
    lane = lax.broadcasted_iota(jnp.int32, (lines, size_z), 1)
    last = [lax.axis_index(axis) == lax.axis_size(axis) - 1 for axis in AXES]
    even = even_places()
    in_y = line % size_y
    for copy in copies[:-1]:
        copy.wait()
    upper_x = jnp.where((line >= lines - size_y) & last[0], 0.0, tx_ref[...])
    upper_y = jnp.where((in_y == size_y - 1) & last[1], 0.0, ty_ref[...])
    upper_z = jnp.where((lane == size_z - 1) & last[2], 0.0, tz_ref[...])
    behind = []
    for i in range(3):
        came = edges[2 * i][...]
        if edges[2 * i + 1] is not None:
            came = jnp.where(even[i], edges[2 * i + 1][...], came)
        behind.append(jnp.where(lax.axis_index(AXES[i]) == 0, 0.0, came))
    lower_x = jnp.concatenate([behind[0], upper_x[: lines - size_y]], axis=0)
    edge_y = jnp.concatenate(
        [jnp.broadcast_to(behind[1][i : i + 1, :], (size_y, size_z)) for i in range(size_x)], axis=0
    )
    lower_y = jnp.where(in_y == 0, edge_y, pltpu.roll(upper_y, 1, 0))
    lower_z = jnp.where(lane == 0, jnp.broadcast_to(behind[2], (8, lines)).T[:, 0:1], pltpu.roll(upper_z, 1, 1))
    total = recv_ref.shape[1]
    cell = recv_ref[...]
    hot_line = jnp.broadcast_to(cell // size_z, (lines, total)) == lax.broadcasted_iota(
        jnp.int32, (lines, total), 0
    )
    hot_lane = jnp.broadcast_to(cell % size_z, (size_z, total)) == lax.broadcasted_iota(
        jnp.int32, (size_z, total), 0
    )
    weight = weight_ref[...]
    high = weight.astype(BF16).astype(F32)
    middle = (weight - high).astype(BF16).astype(F32)
    low = weight - high - middle
    parts = [jnp.where(hot_line, part, 0.0).astype(BF16) for part in (high, middle, low)]
    summed = nt_dot(jnp.concatenate(parts, axis=0), jnp.where(hot_lane, 1.0, 0.0).astype(BF16))
    fault_diag = summed[:lines] + summed[lines : 2 * lines] + summed[2 * lines :]
    number = lax.broadcasted_iota(jnp.int32, shifts_ref.shape, 1)
    shift = jnp.sum(jnp.where(number == which_ref[...], shifts_ref[...], 0.0), axis=1, keepdims=True)
    diagonal = (
        upper_x + lower_x + upper_y + lower_y + upper_z + lower_z + shift * pore_ref[...] + fault_diag
    )
    inverse = 1.0 / diagonal
    inner_y = jnp.where(in_y == size_y - 1, 0.0, upper_y), jnp.where(in_y == 0, 0.0, lower_y)
    inner_z = jnp.where(lane == size_z - 1, 0.0, upper_z), jnp.where(lane == 0, 0.0, lower_z)
    face_y = upper_y - inner_y[0] + (lower_y - inner_y[1])
    face_z = upper_z - inner_z[0] + (lower_z - inner_z[1])
    for i, value in enumerate((upper_x, lower_x, *inner_y, *inner_z, diagonal, inverse, face_y, face_z)):
        ops_ref[i] = value
    copies[-1].wait()
    for c in range(columns):
        direction_ref[c] = residual_ref[c] * inverse
    emit_faces(direction_ref, faces_out, dims)


def unpack_faces(refs, has_b):
    refs = list(refs)
    faces = []
    for more in has_b:
        faces += [refs.pop(0), refs.pop(0) if more else None]
    return faces


def stencil_kernel(dims, has_b, first_round, *refs):
    refs = list(refs)
    columns, size_x, size_y, size_z, slots = dims
    ops_ref, residual_ref, direction_ref = refs[:3]
    refs = refs[3:]
    solution_out, residual_out = refs.pop(), refs.pop()
    solution_ref = None if first_round else refs.pop()
    xa_ref, xb_ref = refs[0], refs[-1]
    lines = size_x * size_y
    even = lax.axis_index(AXES[0]) % 2 == 0
    for c in range(columns):
        value = direction_ref[c]
        x_low = jnp.where(even, xb_ref[c], xa_ref[c])
        x_high = jnp.where(even, xa_ref[c], xb_ref[c])
        beside = ops_ref[0] * jnp.concatenate([value[size_y:], x_high], axis=0)
        beside += ops_ref[1] * jnp.concatenate([x_low, value[: lines - size_y]], axis=0)
        beside += ops_ref[2] * pltpu.roll(value, lines - 1, 0)
        beside += ops_ref[3] * pltpu.roll(value, 1, 0)
        beside += ops_ref[4] * pltpu.roll(value, size_z - 1, 1)
        beside += ops_ref[5] * pltpu.roll(value, 1, 1)
        residual_out[c] = residual_ref[c] - (ops_ref[6] * value - beside)
        solution_out[c] = value if first_round else solution_ref[c] + value


def update_kernel(dims, has_b, keep, gain, last_round, early, *refs):
    refs = list(refs)
    columns, size_x, size_y, size_z, slots = dims
    extra, comes, parity = early
    ops_ref, residual_ref, direction_ref, recv_ref, weight_ref, arrived_ref = refs[:6]
    refs = refs[6:]
    ya_ref, yb_ref, za_ref, zb_ref = unpack_faces(refs[: 2 + has_b[1] + has_b[2]], has_b[1:])
    refs = refs[2 + has_b[1] + has_b[2] :]
    yb_ref = ya_ref if yb_ref is None else yb_ref
    zb_ref = za_ref if zb_ref is None else zb_ref
    if last_round:
        solution_ref, well_ref, *refs = refs
        blocks = (len(refs) - 5) // 2
        sources, (sums_out, flat_out, landed_ref, solution_out) = refs[:blocks], refs[blocks : blocks + 4]
        basis_refs, sem = refs[blocks + 4 : -1], refs[-1]
        fetches = start_copies(zip(sources, basis_refs), sem)
    else:
        landed_ref = refs.pop()
    table_out = refs.pop(0) if comes else None
    if not last_round:
        residual_out, direction_out = refs[:2]
        faces_out = unpack_faces(refs[2:], has_b)
    lines = size_x * size_y
    rows = columns * slots // LANES
    total = recv_ref.shape[1]
    half = lines // 2
    hot_row, hot_key = one_hots(recv_ref[...], lines, size_z)
    hot_row = jnp.where(hot_row, 1.0, 0.0).astype(BF16)
    tiles = []
    devices = total // slots
    if comes:
        per_device = rows + extra
        for i in range(devices):
            landed_ref[i * rows : (i + 1) * rows, :LANES] = arrived_ref[i * per_device : i * per_device + rows, :]
        source_ref = landed_ref
    else:
        source_ref = arrived_ref
    for j in range(total // LANES):
        tiles.append(regroup(source_ref[j * columns : (j + 1) * columns, :LANES], rows, slots))
    if comes == "parts":
        added = [jnp.zeros((extra, LANES), F32)] * 2
        for i in range(devices):
            at = i * per_device + rows
            added[parity[i]] = added[parity[i]] + arrived_ref[at : at + extra, :]
        table_out[:extra, :], table_out[extra:, :] = added
    if comes == "sums":
        for i in range(devices):
            at = i * per_device + rows
            table_out[i * extra : (i + 1) * extra, :] = arrived_ref[at : at + extra, :]
    weighted = (jnp.concatenate(tiles, axis=1) * weight_ref[...]).astype(BF16)
    spread = weighted[:, None, :] * hot_row[None, :, :]
    landed_ref[...] = nt_dot(spread.reshape(columns * half, total), hot_key)
    even = even_places()
    in_slab = lax.broadcasted_iota(jnp.int32, (size_y, size_z), 0)
    lane = lax.broadcasted_iota(jnp.int32, (lines, size_z), 1)
    z_a, z_b = za_ref[...], zb_ref[...]
    z_rows = [jnp.where(even[2], z_b, z_a), jnp.where(even[2], z_a, z_b), jnp.zeros((6, columns * lines), F32)]
    z_cols = jnp.concatenate(z_rows, axis=0).T
    for c in range(columns):
        landed = landed_ref[c * half : (c + 1) * half, :]
        left = residual_ref[c] + jnp.concatenate([landed[:, :size_z], landed[:, size_z:]], axis=0)
        beside_y = []
        for i in range(size_x):
            y_a, y_b = ya_ref[i, c : c + 1, :], yb_ref[i, c : c + 1, :]
            y_low, y_high = jnp.where(even[1], y_b, y_a), jnp.where(even[1], y_a, y_b)
            beside_y.append(jnp.where(in_slab < size_y // 2, y_low, y_high))
        z_low = z_cols[c * lines : (c + 1) * lines, 0:1]
        z_high = z_cols[c * lines : (c + 1) * lines, 1:2]
        left = left + ops_ref[8] * jnp.concatenate(beside_y, axis=0)
        left = left + ops_ref[9] * jnp.where(lane < size_z // 2, z_low, z_high)
        after = keep * direction_ref[c] + gain * (left * ops_ref[7])
        if last_round:
            solution_out[c] = solution_ref[c] + after
        else:
            residual_out[c] = left
            direction_out[c] = after
    if not last_round:
        emit_faces(direction_out, faces_out, dims)
    else:
        for copy in fetches:
            copy.wait()
        sums_of(dims, solution_out, basis_refs, well_ref, flat_out, sums_out)


def basis_kernel(dims, piece, blocks, *refs):
    well_ref, source_ref = refs[:2]
    others = refs[2 : 2 + piece]
    last = piece == blocks - 1
    before = refs[2 + piece : 2 + 3 * piece] if last else ()
    refs = refs[2 + piece + len(before) :]
    flat_target, gram_out, wells_out, basis_ref, hot_ref, flat_out, sem, out_sem = refs[:8]
    held = refs[8 : 8 + piece]
    columns, size_x, size_y, size_z, slots = dims
    lines = size_x * size_y
    wells = well_ref.shape[1]
    side = 16
    groups = [pl.ds(first, side) for first in range(0, LANES, side)]
    copies = [
        pltpu.make_async_copy(source_ref.at[pl.ds(piece * LANES + i * side, side)], basis_ref.at[g], sem.at[i])
        for i, g in enumerate(groups)
    ]
    for copy in copies:
        copy.start()
    fetches = start_copies(zip(others, held), refs[8 + piece]) if piece else []
    stores = []
    row = lax.broadcasted_iota(jnp.int32, (side * side, side * side), 0)
    lane = lax.broadcasted_iota(jnp.int32, (side * side, side * side), 1)
    turn = jnp.where((row % side == lane // side) & (row // side == lane % side), 1.0, 0.0).astype(BF16)
    cell = well_ref[...]
    lane_of = jnp.broadcast_to(lax.rem(cell + size_z, size_z), (size_z, wells))
    lane_of = lane_of == lax.broadcasted_iota(jnp.int32, (size_z, wells), 0)
    line_of = jnp.broadcast_to(jnp.where(cell < 0, -1, cell // size_z), (size_z, wells))
    for line in range(lines):
        hot = jnp.where(lane_of & (line_of == line), 1.0, 0.0)
        hot_ref[line * size_z : (line + 1) * size_z, :] = hot.astype(BF16)
    for index in range(0, len(groups), 2):
        copies[index].wait()
        copies[index + 1].wait()
        first = index * side
        for begin in range(0, lines, side):
            tile = [
                basis_ref[at : at + side, begin : begin + side, :].reshape(side * side, size_z)
                for at in (first, first + side)
            ]
            tile = jnp.dot(turn, jnp.concatenate(tile, axis=1), preferred_element_type=F32).astype(BF16)
            for i in range(side):
                lanes = slice((begin + i) * size_z, (begin + i + 1) * size_z)
                flat_out[first : first + side, lanes] = tile[i * side : (i + 1) * side, :size_z]
                flat_out[first + side : first + 2 * side, lanes] = tile[i * side : (i + 1) * side, size_z:]
        pair = pl.ds(first, 2 * side)
        stores.append(pltpu.make_async_copy(flat_out.at[pair], flat_target.at[pair], out_sem.at[index // 2]))
        stores[-1].start()
    flat = flat_out[...]
    for copy in fetches:
        copy.wait()
    for i, other in enumerate(held + (flat_out,)):
        product = nt_dot(other[...], flat)
        if last:
            place = (piece * (piece + 1) // 2 + i) * LANES
            refs[-1][place : place + LANES, :] = product
        else:
            gram_out[i * LANES : (i + 1) * LANES, :] = product
    at_wells = jnp.dot(flat, hot_ref[...], preferred_element_type=F32)
    if last:
        full_ref, beside, place = refs[-1], LANES // wells, 0
        for i in range(piece):
            full_ref[place : place + (i + 1) * LANES, :] = before[2 * i][...]
            place += (i + 1) * LANES
        place += (piece + 1) * LANES
        full_ref[place:, :] = jnp.zeros((full_ref.shape[0] - place, LANES), F32)
        for i in range(blocks):
            value = at_wells if i == piece else before[2 * i + 1][...]
            at, lanes = place + i // beside * LANES, slice(i % beside * wells, (i % beside + 1) * wells)
            full_ref[at : at + LANES, lanes] = value
        half, even = full_ref.shape[0] // 2, even_places()[1]
        gram_out[...] = jnp.where(even, full_ref[:half, :], full_ref[half:, :])
        wells_out[...] = jnp.where(even, full_ref[half:, :], full_ref[:half, :])
    else:
        wells_out[...] = at_wells
    for store in stores:
        store.wait()


def split_three(value):
    high = value.astype(BF16)
    left = value - high.astype(F32)
    middle = left.astype(BF16)
    return high, middle, (left - middle.astype(F32)).astype(BF16)


def sums_of(dims, solution_ref, basis_refs, well_ref, flat_out, sums_out):
    columns, size_x, size_y, size_z, slots = dims
    lines = size_x * size_y
    wells = well_ref.shape[1]
    for line in range(lines):
        flat_out[:, line * size_z : (line + 1) * size_z] = solution_ref[:, line, :]
    parts = jnp.concatenate(split_three(flat_out[...]), axis=0)
    with_basis = jnp.concatenate([nt_dot(parts, ref[...]) for ref in basis_refs], axis=1)
    with_self = nt_dot(parts, parts)
    sums_out[...] = jnp.zeros(sums_out.shape, F32)
    blocks = len(basis_refs)
    first = with_basis[:columns]
    beyond = with_basis[columns : 2 * columns] + with_basis[2 * columns :]
    for i in range(blocks):
        lanes = slice(i * LANES, (i + 1) * LANES)
        sums_out[i * columns : (i + 1) * columns, :] = first[:, lanes]
        sums_out[(blocks + i) * columns : (blocks + i + 1) * columns, :] = beyond[:, lanes]
    rows = with_self[:columns] + with_self[columns : 2 * columns] + with_self[2 * columns :]
    square = rows[:, :columns] + rows[:, columns : 2 * columns] + rows[:, 2 * columns :]
    at = 2 * blocks * columns
    sums_out[at : at + columns, :columns] = square
    both = jnp.concatenate(split_two(solution_ref[...].reshape(columns * lines, size_z)), axis=1)
    cell = well_ref[...]
    lane_of = jnp.broadcast_to(lax.rem(cell + size_z, size_z), (size_z, wells))
    hot = lane_of == lax.broadcasted_iota(jnp.int32, (size_z, wells), 0)
    hot = jnp.where(hot, 1.0, 0.0).astype(BF16)
    found = jnp.dot(both, jnp.concatenate([hot, hot], axis=0), preferred_element_type=F32)
    line_of = jnp.broadcast_to(jnp.where(cell < 0, -1, cell // size_z), (lines, wells))
    mask = line_of == lax.broadcasted_iota(jnp.int32, (lines, wells), 0)
    found = jnp.where(mask[None], found.reshape(columns, lines, wells), 0.0)
    at += columns
    sums_out[at : at + columns, :wells] = jnp.sum(found, axis=1)


def share_kernel(devices, parts_ref, out_ref):
    rows = parts_ref.shape[0] // devices
    total = parts_ref[:rows, :]
    for i in range(1, devices):
        total = total + parts_ref[i * rows : (i + 1) * rows, :]
    for i in range(devices):
        out_ref[i * rows : (i + 1) * rows, :] = total


def exact_dot(left, right, transposed=False):
    axes = ((1,), (1,)) if transposed else ((1,), (0,))
    return lax.dot_general(
        left, right, (axes, ((), ())), precision=lax.Precision.HIGHEST, preferred_element_type=F32
    )


def finish_kernel(
    dims, scale, wells, blocks, groups, sums_ref, flat_ref, *refs
):
    mine, other = ([ref[...] for ref in refs[i * groups : (i + 1) * groups]] for i in range(2))
    mine, other, refs = jnp.concatenate(mine, axis=0), jnp.concatenate(other, axis=0), refs[2 * groups :]
    even = even_places()[1]
    table = [jnp.where(even, mine, other), jnp.where(even, other, mine)]
    table = jnp.concatenate(table, axis=0)
    block_out, first_out, coeffs_out, wells_out = refs[blocks : blocks + 4]
    basis_refs = refs[blocks + 4 : -1]
    fetches = start_copies(zip(refs[:blocks], basis_refs), refs[-1])
    columns, size_x, size_y, size_z, slots = dims
    lines = size_x * size_y
    pieces, at = {}, 0
    for i in range(blocks):
        for j in range(i + 1):
            pieces[j, i] = table[at : at + LANES, :]
            pieces[i, j] = pieces[j, i] if i == j else pieces[j, i].T
            at += LANES
    basis_gram = jnp.concatenate(
        [jnp.concatenate([pieces[i, j] for j in range(blocks)], axis=1) for i in range(blocks)], axis=0
    )
    beside = LANES // wells
    wells_basis = []
    for i in range(blocks):
        place = at + i // beside * LANES
        wells_basis.append(table[place : place + LANES, i % beside * wells : (i % beside + 1) * wells])
    wells_basis = jnp.concatenate(wells_basis, axis=0)

    def block(i):
        return sums_ref[i * columns : (i + 1) * columns, :]

    first = jnp.concatenate([block(i) for i in range(blocks)], axis=1)
    beyond = jnp.concatenate([block(blocks + i) for i in range(blocks)], axis=1)
    full = first + beyond
    square = block(2 * blocks)[:, :columns]
    at_wells = block(2 * blocks + 1)[:, :wells]
    gram_parts = split_three(basis_gram)

    def times_gram(value):
        return sum(jnp.dot(value, part, preferred_element_type=F32) for part in gram_parts)

    first_round = first.astype(BF16)
    first_gram = times_gram(first_round)
    second = full - first_gram
    second_round = second.astype(BF16)
    rounds = jnp.concatenate([first_round, second_round], axis=0)
    half = full - 0.5 * (first_gram + times_gram(second_round))
    products = nt_dot(rounds, jnp.concatenate(split_three(half), axis=0))
    products = products[:columns] + products[columns:]
    cross = products[:, :columns] + products[:, columns : 2 * columns] + products[:, 2 * columns :]
    gram = square - cross - cross.T
    spans = jnp.dot(rounds, wells_basis.astype(BF16), preferred_element_type=F32)
    rest_wells = at_wells - spans[:columns] - spans[columns:]
    first_out[...] = first
    coeffs_out[...] = first + second
    row = lax.broadcasted_iota(jnp.int32, (columns, columns), 0)
    lane = lax.broadcasted_iota(jnp.int32, (columns, columns), 1)
    left = gram
    right = jnp.where(row == lane, 1.0, 0.0)
    below = lax.broadcasted_iota(jnp.int32, (columns, 1), 0)
    for k in range(columns - 1):
        factor = jnp.where(below > k, left[:, k : k + 1] / left[k : k + 1, k : k + 1], 0.0)
        right = right - factor * right[k : k + 1, :]
        left = left - factor * left[k : k + 1, :]
    pivots = jnp.sum(jnp.where(row == lane, left, 0.0), axis=1, keepdims=True)
    inverse = right * (scale / jnp.sqrt(pivots))
    wells_out[...] = exact_dot(inverse, rest_wells)
    high, low = split_two(inverse)
    factors = jnp.concatenate([high, high, low], axis=1)
    for copy in fetches:
        copy.wait()
    step = min(8, lines)
    for begin in range(0, lines, step):
        lanes = slice(begin * size_z, (begin + step) * size_z)
        basis_part = jnp.concatenate([ref[:, lanes] for ref in basis_refs], axis=0)
        spans = jnp.dot(rounds, basis_part, preferred_element_type=F32)
        rest = flat_ref[:, lanes] - spans[:columns] - spans[columns:]
        rest_high, rest_low = split_two(rest)
        stacked = jnp.concatenate([rest_high, rest_low, rest_high], axis=0)
        done = jnp.dot(factors, stacked, preferred_element_type=F32)
        for i in range(step):
            block_out[:, begin + i, :] = done[:, i * size_z : (i + 1) * size_z]


def local(
    start_block,
    basis,
    trans_x,
    trans_y,
    trans_z,
    pore_volume,
    shift_table,
    shift_index,
    fault_send,
    fault_recv,
    fault_trans,
    well_cells,
):
    columns, size_x, size_y, size_z = start_block.shape
    devices, slots = fault_send.shape[1:]
    lines = size_x * size_y
    cells = lines * size_z
    total = devices * slots
    sizes = [lax.axis_size(axis) for axis in AXES]
    full_x, full_y, full_z = size_x * sizes[0], size_y * sizes[1], size_z * sizes[2]
    has_b = tuple(size > 2 for size in sizes)
    dims = (columns, size_x, size_y, size_z, slots)
    rows = columns * slots // LANES

    vmem = pl.BlockSpec(memory_space=pltpu.VMEM)
    params = pltpu.CompilerParams(vmem_limit_bytes=8 * 2**20 + 4096 * total)
    wide_params = pltpu.CompilerParams(vmem_limit_bytes=16 * 2**20 + 4096 * total)
    field_type = jax.ShapeDtypeStruct((columns, lines, size_z), F32)
    x_type = jax.ShapeDtypeStruct((columns, size_y, size_z), F32)
    y_type = jax.ShapeDtypeStruct((size_x, columns, size_z), F32)
    z_type = jax.ShapeDtypeStruct((1, columns * lines), F32)
    face_types = [x_type] * (1 + has_b[0]) + [y_type] * (1 + has_b[1]) + [z_type] * (1 + has_b[2])

    def in_hbm(*values):
        return [pltpu.with_memory_space_constraint(value, pltpu.HBM) for value in values]

    shape2 = (lines, size_z)
    start = start_block.reshape(columns, lines, size_z)
    anywhere = pl.BlockSpec(memory_space=pltpu.HBM)
    trans = [value.reshape(shape2) for value in (trans_x, trans_y, trans_z)]
    row_types = [jax.ShapeDtypeStruct((1, total), kind) for kind in (jnp.int32, jnp.int32, F32)]
    edge_types = [
        jax.ShapeDtypeStruct(shape, F32) for shape in ((size_y, size_z), (size_x, size_z), (1, lines))
    ]
    wells = well_cells.shape[0]
    edge_x, edge_y, edge_z, send, recv, weight, well_row = pl.pallas_call(
        functools.partial(edges_kernel, dims),
        out_shape=edge_types + row_types + [jax.ShapeDtypeStruct((1, wells), jnp.int32)],
        in_specs=[anywhere] * 7,
        out_specs=[vmem] * 7,
        scratch_shapes=[pltpu.VMEM(shape2, F32)] * 3
        + [pltpu.VMEM(fault_send.shape, kind) for kind in (jnp.int32, jnp.int32, F32)]
        + [pltpu.VMEM((1, wells), jnp.int32), pltpu.SemaphoreType.DMA((7,))],
        compiler_params=params,
        name="edges",
    )(*in_hbm(*trans, fault_send, fault_recv, fault_trans, well_cells.reshape(1, wells)))
    edges = []
    for axis, edge, more in zip(AXES, (edge_x, edge_y, edge_z), has_b):
        edges += [swap_even(edge, axis)] + ([swap_odd(edge, axis)] if more else [])

    count = basis.shape[0]
    blocks = count // LANES
    early_rows = LANES * (blocks * (blocks + 1) // 2 + -(-blocks // (LANES // wells)))
    groups = 2
    extra = -(-early_rows // (2 * groups * devices))
    half_rows = groups * devices * extra
    parity = [i // sizes[2] % sizes[1] % 2 for i in range(devices)]
    flats, parts = [], []
    for piece in range(blocks):
        last = piece == blocks - 1
        shapes = [(half_rows, LANES)] * 2 if last else [((piece + 1) * LANES, LANES), (LANES, wells)]
        before = parts if last else []
        flat_piece, *part = pl.pallas_call(
            functools.partial(basis_kernel, dims, piece, blocks),
            out_shape=[pltpu.HBM((LANES, cells), BF16)] + [jax.ShapeDtypeStruct(shape, F32) for shape in shapes],
            in_specs=[vmem] + [anywhere] * (1 + piece) + [vmem] * len(before),
            out_specs=[anywhere, vmem, vmem],
            scratch_shapes=[
                pltpu.VMEM((LANES, lines, size_z), BF16),
                pltpu.VMEM((cells, wells), BF16),
                pltpu.VMEM((LANES, cells), BF16),
                pltpu.SemaphoreType.DMA((LANES // 16,)),
                pltpu.SemaphoreType.DMA((LANES // 32,)),
            ]
            + [pltpu.VMEM((LANES, cells), BF16)] * piece
            + [pltpu.SemaphoreType.DMA((max(piece, 1),))]
            + [pltpu.VMEM((2 * half_rows, LANES), F32)] * last,
            compiler_params=wide_params,
            cost_estimate=pl.CostEstimate(
                flops=2 * LANES * cells * ((piece + 1) * LANES + wells),
                bytes_accessed=4 * LANES * cells,
                transcendentals=0,
            ),
            name="basis_gram",
        )(well_row, *in_hbm(basis.reshape(count, lines, size_z), *flats), *before)
        flats.append(flat_piece)
        if not piece:
            part[0], *edges = lax.optimization_barrier((part[0], *edges))
        parts += part

    keep_parts, give_parts = parts[-2:]

    def gather(direction, goes, source, group):
        sent_rows = devices * (rows + (extra if goes else 0))
        return pl.pallas_call(
            functools.partial(gather_kernel, dims, (extra, goes, parity, group * devices * extra)),
            out_shape=jax.ShapeDtypeStruct((sent_rows, LANES), F32),
            in_specs=[vmem] * (2 + len(source)),
            out_specs=vmem,
            compiler_params=params,
            cost_estimate=pl.CostEstimate(
                flops=4 * columns * cells * total, bytes_accessed=4 * columns * cells, transcendentals=0
            ),
            name="fault_gather",
        )(direction, send, *source)

    def transfers(faults, faces):
        faces = list(faces)
        came = {}
        for axis, more in zip(AXES, has_b):
            came[axis] = [swap_even(faces.pop(0), axis)] + ([swap_odd(faces.pop(0), axis)] if more else [])
        faults, came["gy"][0] = lax.optimization_barrier((faults, came["gy"][0]))
        return exchange(faults), came["gx"], came["gy"] + came["gz"]

    def stencil(residual, direction, came, solution):
        more = [] if solution is None else [solution]
        return pl.pallas_call(
            functools.partial(stencil_kernel, dims, has_b, solution is None),
            out_shape=[field_type, field_type],
            in_specs=[vmem] * (3 + len(came) + len(more)),
            out_specs=[vmem] * 2,
            input_output_aliases={1: 0, 3 + len(came): 1} if more else {1: 0},
            compiler_params=params,
            cost_estimate=pl.CostEstimate(
                flops=20 * columns * cells, bytes_accessed=12 * columns * cells, transcendentals=0
            ),
            name="stencil",
        )(ops, residual, direction, *came, *more)

    ops, residual, direction, *faces = pl.pallas_call(
        functools.partial(setup_kernel, dims, has_b),
        out_shape=[jax.ShapeDtypeStruct((10, lines, size_z), F32), field_type, field_type] + face_types,
        in_specs=[vmem] * 4 + [anywhere] * 5 + [vmem] * len(edges),
        out_specs=[vmem] * (3 + len(face_types)),
        scratch_shapes=[pltpu.VMEM(shape2, F32)] * 4
        + [pltpu.SemaphoreType.DMA((5,))],
        compiler_params=params,
        name="setup",
    )(
        shift_table.reshape(1, -1), shift_index.reshape(1, 1), recv, weight,
        *in_hbm(*trans, pore_volume.reshape(shape2), start), *edges,
    )
    needed = columns * (2 * blocks + 2)
    per_device = 1 << (-(-needed // devices) - 1).bit_length()
    sums_type = jax.ShapeDtypeStruct((devices * per_device, LANES), F32)
    flat_type = jax.ShapeDtypeStruct((columns, cells), F32)
    sigma = 1.0 / 0.9
    weight_now = 1.0 / sigma
    solution = None
    tables = {}
    came_parts = swap_even(give_parts, "gy")
    for number in range(TERMS - 1):
        goes = ("", "parts", "sums", "")[number // 2]
        group = number % groups
        source = {"parts": [keep_parts, came_parts], "sums": [tables.get(group)]}.get(goes, [])
        faults = gather(direction, goes, source, group)
        arrived, came, far = transfers(faults, faces)
        residual, solution = stencil(residual, direction, came, solution)
        weight_new = 1.0 / (2.0 * sigma - weight_now)
        last_round = number == TERMS - 2
        body = functools.partial(
            update_kernel, dims, has_b, weight_new * weight_now, 2.0 * weight_new / 0.9,
            last_round, (extra, goes, parity),
        )
        weight_now = weight_new
        scratch = [pltpu.VMEM((columns * lines // 2, 2 * size_z), F32)]
        out_types = [sums_type, flat_type] if last_round else []
        if goes:
            table_rows = 2 * extra if goes == "parts" else devices * extra
            out_types.append(jax.ShapeDtypeStruct((table_rows, LANES), F32))
        operands = [ops, residual, direction, recv, weight, arrived, *far]
        aliases = {}
        if last_round:
            operands.append(solution)
        in_specs = [vmem] * len(operands)
        if not last_round:
            aliases[1], aliases[2] = len(out_types), len(out_types) + 1
            out_types += [field_type, field_type] + face_types
        else:
            operands += [well_row, *in_hbm(*flats)]
            in_specs += [vmem] + [anywhere] * blocks
            scratch.append(pltpu.VMEM((columns, lines, size_z), F32))
            scratch += [pltpu.VMEM((LANES, cells), BF16)] * blocks + [pltpu.SemaphoreType.DMA((blocks,))]
        outs = pl.pallas_call(
            body,
            out_shape=out_types,
            in_specs=in_specs,
            out_specs=[vmem] * len(out_types),
            scratch_shapes=scratch,
            input_output_aliases=aliases,
            compiler_params=wide_params if last_round else params,
            name="update",
        )(*operands)
        if last_round:
            sums, flat = outs
            break
        if goes:
            table, *outs = outs
            tables[group] = table
        residual, direction, *faces = outs

    sums = pl.pallas_call(
        functools.partial(share_kernel, devices),
        out_shape=sums_type,
        in_specs=[vmem],
        out_specs=vmem,
        compiler_params=params,
        name="share_sums",
    )(exchange(sums))
    sums = exchange(sums)

    mine = [tables[group] for group in range(groups)]
    scale = math.sqrt(full_x * full_y * full_z)
    new_block, first_coeffs, coeffs, well_resp = pl.pallas_call(
        functools.partial(finish_kernel, dims, scale, wells, blocks, groups),
        out_shape=[
            field_type,
            jax.ShapeDtypeStruct((columns, count), F32),
            jax.ShapeDtypeStruct((columns, count), F32),
            jax.ShapeDtypeStruct((columns, wells), F32),
        ],
        in_specs=[vmem] * (2 + 2 * groups) + [anywhere] * blocks,
        out_specs=[vmem] * 4,
        scratch_shapes=[pltpu.VMEM((LANES, cells), BF16)] * blocks + [pltpu.SemaphoreType.DMA((blocks,))],
        compiler_params=wide_params,
        name="finish",
    )(sums, flat, *mine, *[swap_even(table, "gy") for table in mine], *in_hbm(*flats))
    return new_block.reshape(start_block.shape), first_coeffs.T, coeffs.T, well_resp.T


def solution(mesh):
    in_specs = (
        P(None, "gx", "gy", "gz"),
        P(None, "gx", "gy", "gz"),
        P("gx", "gy", "gz"),
        P("gx", "gy", "gz"),
        P("gx", "gy", "gz"),
        P("gx", "gy", "gz"),
        P(),
        P(),
        P(("gx", "gy", "gz"), None, None),
        P(("gx", "gy", "gz"), None, None),
        P(("gx", "gy", "gz"), None, None),
        P(),
    )
    out_specs = (P(None, "gx", "gy", "gz"), P(), P(), P())
    return jax.shard_map(local, mesh=mesh, in_specs=in_specs, out_specs=out_specs, check_vma=False)
```
